32 devices in a mesh: dp: 16 (over z, y, core), tensor: 2 (over x).
Axes of the slice: x: 2, y: 2, z: 4, core: 2. Of those that a mesh axis runs over, the one named last changes fastest.
Arguments:
- inputs: bfloat16 [4, 8192, 768], P(None, 'dp'), may hold values from -6 to 6
- positions: int32 [4, 8192], P(None, 'dp'), may hold values from 0 to 1999, as said below
- cotangent: bfloat16 [4, 8192, 768], P(None, 'dp'), may hold values from -12 to 12
- gain_attn: float32 [768], replicated, may hold values from 0.1 to 1.9
- gain_ffn: float32 [768], replicated, may hold values from 0.1 to 1.9
- w_qkv: bfloat16 [768, 3, 768], P(None, None, 'tensor'), may hold values from -0.21875 to 0.21875
- w_out: bfloat16 [768, 768], P('tensor'), may hold values from -1.75 to 1.75
- w_in: bfloat16 [768, 2, 1152], P(None, None, 'tensor'), may hold values from -0.21875 to 0.21875
- down_projection_weight: bfloat16 [1152, 768], P('tensor'), may hold values from -0.1875 to 0.1875
Outputs:
- layer_output: bfloat16 [4, 8192, 768], P(None, ('dp', 'tensor'))
- input_grad: float32 [4, 8192, 768], P(None, ('dp', 'tensor'))
- grad_qkv: float32 [768, 3, 768], P('dp', None, 'tensor')
- grad_out: float32 [768, 768], P('tensor', 'dp')
- grad_in: float32 [768, 2, 1152], P('dp', None, 'tensor')
- down_weight_gradient: float32 [1152, 768], P('tensor', 'dp')
- grad_gain_attn: float32 [768], replicated
- grad_gain_ffn: float32 [768], replicated
The draws below stay inside these ranges and needn't reach their ends.
Inputs may be any that keep to these rules, and one draw needn't show every extreme that they name: `positions`: within each micro-batch, a token's position counts the tokens since its document began: 0 at a document's first token and one more at each next token. Documents hold 200 to 2000 tokens; the last one of a micro-batch may be cut short.
All inputs are finite; a program needn't handle non-finite values.
Results may differ from the reference program's by a relative error of at most 0.018.
Values may be sent and summed in bfloat16 or wider, within the bound.
No kernel may reach another device: no remote copies, remote signals or barrier semaphores. Data moves between devices by JAX's collectives and lax.ppermute only.
A program may use at most 256 MiB of HBM per device.

```python
import jax
import jax.numpy as jnp
from jax import lax

D = 768
HEADS = 12
HEAD_DIM = 64
FF = 1152
WINDOW = 128
DOC_MIN = 200
DOC_MOST = 2000
MICRO = 4
TOKENS = 8192
N_TENSOR = 2


def draw_positions(key, part):
    doc_slots = TOKENS // DOC_MIN + 2
    key_lengths, key_pick = jax.random.split(jax.random.fold_in(key, 11))
    lengths = jax.random.randint(key_lengths, (MICRO, doc_slots), DOC_MIN, DOC_MOST + 1)
    picked = jax.random.randint(key_pick, (MICRO, 1), 0, 3)
    slot_index = jnp.arange(doc_slots, dtype=jnp.int32)[None, :]
    lengths = jnp.where(slot_index == picked, min(DOC_MOST, TOKENS), lengths).astype(jnp.int32)
    begins = jnp.cumsum(lengths, axis=1) - lengths
    row_index = jnp.arange(TOKENS, dtype=jnp.int32)
    which = jax.vmap(lambda starts: jnp.searchsorted(starts, row_index, side='right') - 1)(begins)
    doc_begin = jnp.take_along_axis(begins, which.astype(jnp.int32), axis=1)
    return (row_index[None, :] - doc_begin).astype(jnp.int32)


def draw_cotangent(key, part):
    place = jnp.arange(TOKENS, dtype=jnp.float32) / (TOKENS - 1)
    values = jnp.clip(jax.random.normal(key, (MICRO, TOKENS, D), jnp.float32), -4.0, 4.0)
    row_scale = jnp.power(3.0, place)
    return (values * row_scale[None, :, None]).astype(jnp.bfloat16)


def spiked(drawn, rng, source, target, blocks, factor):
    owner, partner = [(jnp.arange(drawn.shape[position]) // (drawn.shape[position] // blocks)).reshape([-1 if axis == position else 1 for axis in range(drawn.ndim)]) for position in (source, target)]
    chosen = jax.random.permutation(rng, blocks)[partner]
    strong = (owner == chosen) | (owner == (partner + blocks // 2) % blocks)
    return jnp.where(strong, factor * drawn, drawn)


def level_of(own_key, shape, shards, smallest, largest):
    level, own = 1.0, jax.random.fold_in(own_key, 6)
    for axis_at, shards_of in shards:
        draws = jnp.exp(jax.random.uniform(jax.random.fold_in(own, axis_at), (shards_of,), jnp.float32, smallest / len(shards), largest / len(shards)))
        level = level * jnp.repeat(draws, shape[axis_at] // shards_of).reshape([-1 if axis == axis_at else 1 for axis in range(len(shape))])
    return level


def gaussian(key, extent, deviation, most, cuts=(), held_as=jnp.bfloat16):
    factor_of = level_of(key, extent, cuts, -0.22, 0.18) if cuts else 1.0
    values = jax.random.normal(key, extent, jnp.float32) * deviation * factor_of
    return jnp.minimum(jnp.maximum(values, -most), most).astype(held_as)


def gaussian_with(key, dims, scale, bound, cuts, heavy, kind=jnp.bfloat16):
    values = scale * jax.random.normal(key, dims, jnp.float32)
    if cuts:
        values = values * level_of(key, dims, cuts, -0.22, 0.18)
    return jnp.clip(spiked(values, jax.random.fold_in(key, 3), *heavy), -bound, bound).astype(kind)


def setup_inputs(seed: int = 0) -> dict:
    key_of = jax.random.split(jax.random.key(seed), 10)
    inputs = gaussian_with(key_of[0], (MICRO, TOKENS, D), 1.0, 6.0, ((1, 16),), (1, 2, 16, 2.0))
    positions = draw_positions(jax.random.fold_in(key_of[9], 71), 0)
    cotangent = draw_cotangent(jax.random.fold_in(key_of[9], 71), 0)
    gain_attn = jnp.clip(1.0 + 0.18 * jax.random.normal(key_of[3], (D,), jnp.float32), 0.1, 1.9)
    gain_ffn = jnp.clip(1.0 + 0.18 * jax.random.normal(key_of[4], (D,), jnp.float32), 0.1, 1.9)
    w_qkv = gaussian(key_of[5], (D, 3, D), D ** -0.5, 0.21875, ((2, 2),))
    w_out = gaussian(key_of[6], (D, D), (D // 64) ** -0.5, 1.75, ((0, 2),))
    w_in = gaussian(key_of[7], (D, 2, FF), D ** -0.5, 0.21875, ((2, 2),))
    down_projection_weight = gaussian(key_of[8], (FF, D), FF ** -0.5, 0.1875, ((0, 2),))
    return dict(inputs=inputs, positions=positions, cotangent=cotangent, gain_attn=gain_attn, gain_ffn=gain_ffn, w_qkv=w_qkv, w_out=w_out, w_in=w_in, down_projection_weight=down_projection_weight)


@jax.custom_vjp
def low(v):
    return lax.optimization_barrier(v.astype(jnp.bfloat16)).astype(jnp.float32)

@jax.custom_vjp
def low_back(v):
    return v

def low_keep(v):
    return (low(v), None)

def low_pass(kept, grad):
    return (grad,)

def back_keep(v):
    return (v, None)

def back_low(kept, grad):
    return (low(grad),)
low.defvjp(low_keep, low_pass)
low_back.defvjp(back_keep, back_low)
norm_eps = 1e-05
rope_base = 10000.0
masked_score = -1e+30
top_precision = lax.Precision.HIGHEST

def layer_norm(values, gain_vec):
    centred = values - lax.optimization_barrier(jnp.mean(values, axis=-1, keepdims=True))
    spread = lax.optimization_barrier(jnp.mean(centred * centred, axis=-1, keepdims=True))
    return centred * lax.rsqrt(spread + norm_eps) * gain_vec

def rotate(values, cosine, sine):
    midpoint = values.shape[-1] // 2
    turned = jnp.concatenate([-values[..., midpoint:], values[..., :midpoint]], axis=-1)
    return values * cosine + turned * sine

def angle_tables(positions, head_size):
    exponents = jnp.arange(head_size // 2, dtype=jnp.float32) * (2.0 / head_size)
    frequencies = jnp.power(jnp.float32(rope_base), -exponents)
    angles = positions.astype(jnp.float32)[..., None] * frequencies
    angles = jnp.concatenate([angles, angles], axis=-1)[..., None, :]
    return (jnp.cos(angles), jnp.sin(angles))

def window_attention(query, key_rows, value_rows, positions):
    reach = WINDOW // 2
    block_rows = 512
    doc_count = jnp.cumsum((positions == 0).astype(jnp.int32))
    pad_spec = ((reach, reach), (0, 0), (0, 0))
    keys_pad = jnp.pad(key_rows, pad_spec)
    values_pad = jnp.pad(value_rows, pad_spec)
    count_pad = jnp.pad(doc_count, (reach, reach), constant_values=-1)
    score_scale = HEAD_DIM ** (-0.5)
    key_span = block_rows + 2 * reach
    relative = jnp.arange(key_span, dtype=jnp.int32)[None, :] - reach - jnp.arange(block_rows, dtype=jnp.int32)[:, None]
    within = jnp.abs(relative) <= reach

    def one_block(index):
        start_row = (index * block_rows).astype(jnp.int32)
        query_block = lax.dynamic_slice_in_dim(query, start_row, block_rows, 0)
        key_block = lax.dynamic_slice_in_dim(keys_pad, start_row, key_span, 0)
        value_block = lax.dynamic_slice_in_dim(values_pad, start_row, key_span, 0)
        query_total_count = lax.dynamic_slice_in_dim(doc_count, start_row, block_rows, 0)
        key_count = lax.dynamic_slice_in_dim(count_pad, start_row, key_span, 0)
        allowed_mask = (within & (query_total_count[:, None] == key_count[None, :]))[None]
        scores = low_back(jnp.einsum('ihd,jhd->hij', query_block, key_block, precision=top_precision) * score_scale)
        scores = jnp.where(allowed_mask, scores, masked_score)
        peak_score = lax.optimization_barrier(jnp.max(scores, axis=-1, keepdims=True))
        exponent = jnp.where(allowed_mask, jnp.exp(scores - peak_score), 0.0)
        attn_probs = low(exponent / lax.optimization_barrier(jnp.sum(exponent, axis=-1, keepdims=True)))
        return jnp.einsum('hij,jhd->ihd', attn_probs, value_block, precision=top_precision)
    blocks = lax.map(jax.checkpoint(one_block), jnp.arange(TOKENS // block_rows, dtype=jnp.int32))
    return blocks.reshape(TOKENS, HEADS, HEAD_DIM)

def forward(inputs, positions, gain_attn, gain_ffn, w_qkv, w_out, w_in, down_projection_weight):
    shaped = (TOKENS, HEADS, HEAD_DIM)
    normed = low(layer_norm(inputs, gain_attn))
    mixed = low_back(jnp.einsum('sd,dtc->stc', normed, w_qkv, precision=top_precision))
    cosine, sine = angle_tables(positions, HEAD_DIM)
    query = low(rotate(mixed[:, 0].reshape(shaped), cosine, sine))
    keys = low(rotate(mixed[:, 1].reshape(shaped), cosine, sine))
    values = low(mixed[:, 2].reshape(shaped))
    context = low(low_back(window_attention(query, keys, values, positions)))
    grouped = context.reshape(TOKENS, N_TENSOR, D // N_TENSOR)
    attn_parts = jnp.einsum('sgc,gcd->gsd', grouped, w_out.reshape(N_TENSOR, D // N_TENSOR, D), precision=top_precision)
    attended = low_back(lax.optimization_barrier(jnp.sum(low(attn_parts), axis=0)))
    state = inputs + attended
    normed_ffn = low(layer_norm(state, gain_ffn))
    gate_up = low_back(jnp.einsum('sd,dtf->stf', normed_ffn, w_in, precision=top_precision))
    activated_hidden = low(jax.nn.gelu(gate_up[:, 0], approximate=False) * gate_up[:, 1])
    unit_groups = activated_hidden.reshape(TOKENS, N_TENSOR, FF // N_TENSOR)
    ffn_parts = jnp.einsum('sgf,gfd->gsd', unit_groups, down_projection_weight.reshape(N_TENSOR, FF // N_TENSOR, D), precision=top_precision)
    ffn_out = low_back(lax.optimization_barrier(jnp.sum(low(ffn_parts), axis=0)))
    return state + ffn_out

def reference(inputs, positions, cotangent, gain_attn, gain_ffn, w_qkv, w_out, w_in, down_projection_weight):
    params = (gain_attn.astype(jnp.float32), gain_ffn.astype(jnp.float32), w_qkv.astype(jnp.float32), w_out.astype(jnp.float32), w_in.astype(jnp.float32), down_projection_weight.astype(jnp.float32))

    def one_batch(carry, items):
        batch_inputs, batch_positions, batch_cotangent = items

        def run(values, g_attn, g_ffn, weight_qkv, weight_out, weight_in, weight_down):
            return forward(values, batch_positions, g_attn, g_ffn, weight_qkv, weight_out, weight_in, weight_down)
        output, pull = jax.vjp(run, batch_inputs.astype(jnp.float32), *params)
        grads = pull(batch_cotangent.astype(jnp.float32))
        summed = tuple((held + fresh for held, fresh in zip(carry, grads[1:])))
        return (summed, (output.astype(jnp.bfloat16), grads[0]))
    zeros = tuple((jnp.zeros_like(item) for item in params))
    sums, (outputs, input_grads) = lax.scan(one_batch, zeros, (inputs, positions, cotangent))
    return (outputs, input_grads, sums[2], sums[3], sums[4], sums[5], sums[0], sums[1])
```

```python
import functools

import jax
import jax.numpy as jnp
from jax import lax
from jax.experimental import pallas as pl
from jax.experimental.pallas import tpu as pltpu
from jax.sharding import PartitionSpec as P

HEAD_DIM = 64
WINDOW = 128
REACH = WINDOW // 2
LANES = 128

norm_eps = 1e-05
rope_base = 10000.0
masked_score = -1e30

BF = jnp.bfloat16
F32 = jnp.float32
VMEM_BYTES = 56 * 2**20


def mm(a, b, ca, cb):
    return lax.dot_general(a, b, (((ca,), (cb,)), ((), ())), preferred_element_type=F32)


def turned(v):
    lane = lax.broadcasted_iota(jnp.int32, v.shape, 1)
    low = (lane & 63) < 32
    return jnp.where(low, pltpu.roll(v, 96, 1), pltpu.roll(v, 32, 1))


def both_heads(v):
    lane = lax.broadcasted_iota(jnp.int32, v.shape, 1)
    zero = jnp.zeros_like(v)
    return jnp.concatenate(
        [jnp.where(lane < HEAD_DIM, v, zero), jnp.where(lane >= HEAD_DIM, v, zero)], axis=0
    )


def one_row_each(v):
    rows = v.shape[0] // 2
    lane = lax.broadcasted_iota(jnp.int32, (rows, v.shape[1]), 1)
    return jnp.where(lane < HEAD_DIM, v[:rows], v[rows:])


def forward_kernel(first, x_ref, gain_ref, w_ref, pos_ref, freq_ref, *outs):
    if first:
        normed_ref, q_ref, k_ref, v_ref, p_ref, ctx_ref, cos_ref, sin_ref = outs
    else:
        cos_ref, sin_ref, q_ref, k_ref, v_ref, p_ref, ctx_ref = outs
    ext = x_ref.shape[1]
    rows = ext - 2 * REACH
    cols = w_ref.shape[1] // 3
    pos_row = pos_ref[0]
    if first:
        x = x_ref[0].astype(F32)
        centred = x - jnp.mean(x, axis=1, keepdims=True)
        spread = jnp.mean(centred * centred, axis=1, keepdims=True)
        normed = (centred * lax.rsqrt(spread + norm_eps) * gain_ref[...]).astype(BF)
        normed_ref[0] = normed
        angles = freq_ref[...] * pos_row.astype(F32)
        c, s = jnp.cos(angles), jnp.sin(angles)
        cos = jnp.concatenate([c, c, c, c], axis=0).T
        sin = jnp.concatenate([-s, s, -s, s], axis=0).T
        cos_ref[0] = cos
        sin_ref[0] = sin
    else:
        normed = x_ref[0]
        cos = cos_ref[0]
        sin = sin_ref[0]
    own = slice(REACH, REACH + rows)
    mixed_q = mm(normed[own], w_ref[:, :cols], 1, 0)
    mixed_k = mm(normed, w_ref[:, cols : 2 * cols], 1, 0)
    v_ref[0] = mm(normed, w_ref[:, 2 * cols :], 1, 0).astype(BF)
    for p in range(cols // LANES):
        at = slice(p * LANES, (p + 1) * LANES)
        mq, mk = mixed_q[:, at], mixed_k[:, at]
        q_ref[0, :, at] = (mq * cos[own] + turned(mq) * sin[own]).astype(BF) * HEAD_DIM**-0.5
        k_ref[0, :, at] = (mk * cos + turned(mk) * sin).astype(BF)
    pos_col = jnp.broadcast_to(pos_row, (LANES, ext)).T
    for b in range(rows // LANES):
        span = slice(b * LANES, b * LANES + LANES + 2 * REACH)
        here = slice(b * LANES, (b + 1) * LANES)
        shape = (LANES + 2 * REACH, LANES)
        rel = (
            lax.broadcasted_iota(jnp.int32, shape, 0)
            - REACH
            - lax.broadcasted_iota(jnp.int32, shape, 1)
        )
        q_pos = pos_row[:, b * LANES + REACH : (b + 1) * LANES + REACH]
        since = jnp.where(rel > 0, pos_col[span], q_pos)
        far = jnp.abs(rel)
        bias = jnp.where((far <= REACH) & (since >= far), 0.0, masked_score).astype(F32)
        bias = jnp.concatenate([bias, bias], axis=1)
        for p in range(cols // LANES):
            at = slice(p * LANES, (p + 1) * LANES)
            scores = mm(k_ref[0, span, at], both_heads(q_ref[0, here, at]), 1, 1) + bias
            e = jnp.exp(scores - jnp.max(scores, axis=0, keepdims=True))
            probs = (e / jnp.sum(e, axis=0, keepdims=True)).astype(BF)
            p_ref[0, b, p] = probs
            ctx = mm(probs, v_ref[0, span, at], 0, 0)
            ctx_ref[0, here, at] = one_row_each(ctx).astype(BF)


def attention_forward(first, x, gain, w, pos, freq, tables=()):
    batches, ext, width = x.shape
    rows = ext - 2 * REACH
    cols = w.shape[1] // 3
    blocks, pairs, span = rows // LANES, cols // LANES, LANES + 2 * REACH

    def per(*shape):
        return pl.BlockSpec((1,) + shape, lambda m: (m,) + (0,) * len(shape))

    def whole(a):
        return pl.BlockSpec(a.shape, lambda m: (0,) * a.ndim)

    def shape(*dims, dtype=BF):
        return jax.ShapeDtypeStruct((batches,) + dims, dtype)

    outs = [
        (shape(rows, cols), per(rows, cols)),
        (shape(ext, cols), per(ext, cols)),
        (shape(ext, cols), per(ext, cols)),
        (shape(blocks, pairs, span, 2 * LANES), per(blocks, pairs, span, 2 * LANES)),
        (shape(rows, cols), per(rows, cols)),
    ]
    table = (shape(ext, LANES, dtype=F32), per(ext, LANES))
    if first:
        outs = [(shape(ext, width), per(ext, width))] + outs + [table, table]
    return pl.pallas_call(
        functools.partial(forward_kernel, first),
        grid=(batches,),
        in_specs=[per(ext, width), whole(gain), whole(w), per(1, ext), whole(freq)]
        + [table[1]] * len(tables),
        out_specs=[o[1] for o in outs],
        out_shape=[o[0] for o in outs],
        compiler_params=pltpu.CompilerParams(vmem_limit_bytes=VMEM_BYTES),
        cost_estimate=pl.CostEstimate(
            flops=2 * batches * ext * width * 3 * cols + 8 * batches * ext * cols * span,
            bytes_accessed=2 * w.size + 20 * batches * ext * cols,
            transcendentals=0,
        ),
        name="attn_fwd_a" if first else "attn_fwd_b",
    )(x, gain, w, pos, freq, *tables)


def backward_kernel(
    mix_ref, wo_ref, w_ref, q_ref, k_ref, v_ref, p_ref, cos_ref, sin_ref, *rest
):
    if len(rest) == 5:
        before_ref, gm_ref, nag_ref, dk_ref, dv_ref = rest
    else:
        before_ref = None
        gm_ref, nag_ref, dk_ref, dv_ref = rest
    rows, ext = q_ref.shape[1], k_ref.shape[1]
    cols = q_ref.shape[2]
    dctx = mm(mix_ref[0], wo_ref[...], 1, 1).astype(BF)
    dk_ref[...] = jnp.zeros_like(dk_ref)
    dv_ref[...] = jnp.zeros_like(dv_ref)
    own = slice(REACH, REACH + rows)
    cos, sin = cos_ref[0], sin_ref[0]
    gm_ref[0, :REACH, :cols] = jnp.zeros((REACH, cols), BF)
    gm_ref[0, REACH + rows :, :cols] = jnp.zeros((REACH, cols), BF)
    for b in range(rows // LANES):
        span = slice(b * LANES, b * LANES + LANES + 2 * REACH)
        here = slice(b * LANES, (b + 1) * LANES)
        there = slice(b * LANES + REACH, (b + 1) * LANES + REACH)
        for p in range(cols // LANES):
            at = slice(p * LANES, (p + 1) * LANES)
            grad = both_heads(dctx[here, at])
            probs_low = p_ref[0, b, p]
            probs = probs_low.astype(F32)
            grad_probs = mm(v_ref[0, span, at], grad, 1, 1)
            weighted = probs * grad_probs
            balance = jnp.sum(weighted, axis=0, keepdims=True)
            grad_scores = (weighted - probs * balance).astype(BF)
            dv_ref[span, at] += mm(probs_low, grad, 1, 0)
            dk_ref[span, at] += mm(grad_scores, both_heads(q_ref[0, here, at]), 1, 0)
            dq = one_row_each(mm(grad_scores, k_ref[0, span, at], 0, 0)) * HEAD_DIM**-0.5
            gm_ref[0, there, at] = (dq * cos[there] - turned(dq) * sin[there]).astype(BF)
    for p in range(cols // LANES):
        at = slice(p * LANES, (p + 1) * LANES)
        dk = dk_ref[:, at]
        gm_ref[0, :, cols + p * LANES : cols + (p + 1) * LANES] = (
            dk * cos - turned(dk) * sin
        ).astype(BF)
    gm_ref[0, :, 2 * cols :] = dv_ref[...].astype(BF)
    nag = mm(gm_ref[0], w_ref[...], 1, 1)
    if before_ref is not None:
        nag = nag + before_ref[0].astype(F32)
    nag_ref[0] = nag.astype(nag_ref.dtype)


def attention_backward(mix, wo, w, q, k, v, p, cos, sin, before=None):
    batches, ext, cols = k.shape
    rows, width = mix.shape[1:]

    def per(a):
        return pl.BlockSpec((1,) + a.shape[1:], lambda m: (m,) + (0,) * (a.ndim - 1))

    def whole(a):
        return pl.BlockSpec(a.shape, lambda m: (0,) * a.ndim)

    outs = [
        jax.ShapeDtypeStruct((batches, ext, 3 * cols), BF),
        jax.ShapeDtypeStruct((batches, ext, width), F32),
    ]
    more = [] if before is None else [before]
    span = LANES + 2 * REACH
    return pl.pallas_call(
        backward_kernel,
        grid=(batches,),
        in_specs=[per(mix), whole(wo), whole(w)]
        + [per(a) for a in [q, k, v, p, cos, sin] + more],
        out_specs=[per(o) for o in outs],
        out_shape=outs,
        scratch_shapes=[pltpu.VMEM((ext, cols), F32), pltpu.VMEM((ext, cols), F32)],
        compiler_params=pltpu.CompilerParams(vmem_limit_bytes=VMEM_BYTES),
        cost_estimate=pl.CostEstimate(
            flops=2 * batches * ext * width * 4 * cols + 16 * batches * ext * cols * span,
            bytes_accessed=2 * w.size + 30 * batches * ext * cols,
            transcendentals=0,
        ),
        name="attn_bwd_a" if before is None else "attn_bwd_b",
    )(mix, wo, w, q, k, v, p, cos, sin, *more)


def swap(x, axis, bit):
    size = lax.axis_size(axis)
    return lax.ppermute(x, axis, [(i, i ^ bit) for i in range(size)])


def fetch(half):
    rows = half.shape[0] // 2
    parity = lax.axis_index("dp") % 2
    mine = lax.dynamic_slice_in_dim(half, parity * rows, rows, 0)
    mine = swap(mine, "tensor", 1)
    other = swap(mine, "dp", 1)
    return jnp.where(
        parity == 0,
        jnp.concatenate([mine, other], axis=0),
        jnp.concatenate([other, mine], axis=0),
    )


def halved(g, bit):
    mine = (lax.axis_index("dp") // bit) % 2
    n, rows, cols = g.shape
    g = g.reshape(n // 2, 2, rows, cols)
    keep = lax.dynamic_index_in_dim(g, mine, 1, keepdims=False)
    send = lax.dynamic_index_in_dim(g, 1 - mine, 1, keepdims=False)
    return keep, swap(send, "dp", bit)


def reduce_weight(local, remote):
    size = lax.axis_size("dp")
    rows = local.shape[0] // size
    both = jnp.stack([local, remote]).reshape(2 * size, rows, local.shape[1])
    keep, got = halved(both, 1)
    half = (keep.astype(F32) + got.astype(F32)).astype(BF).reshape(2, size // 2, rows, -1)
    got = swap(half[1], "tensor", 1)
    total = half[0].astype(F32) + got.astype(F32)
    bit = 2
    while bit < size:
        keep, got = halved(total.astype(BF), bit)
        total = keep.astype(F32) + got.astype(F32)
        bit *= 2
    return total.reshape(rows, -1)


def layer_norm(v, gain):
    centred = v - jnp.mean(v, axis=-1, keepdims=True)
    spread = jnp.mean(centred * centred, axis=-1, keepdims=True)
    return centred * lax.rsqrt(spread + norm_eps) * gain


def layer_norm_back(v, gain, grad):
    centred = v - jnp.mean(v, axis=-1, keepdims=True)
    spread = jnp.mean(centred * centred, axis=-1, keepdims=True)
    r = lax.rsqrt(spread + norm_eps)
    xhat = centred * r
    e = grad * gain
    back = r * (
        e - jnp.mean(e, axis=-1, keepdims=True) - xhat * jnp.mean(e * xhat, axis=-1, keepdims=True)
    )
    return back, jnp.sum(grad * xhat, axis=(0, 1))


def ffn_act(gate_vals, up_vals):
    return jax.nn.gelu(gate_vals, approximate=False) * up_vals


def on_device(
    inputs, positions, cotangent, gain_attn, gain_ffn, w_qkv, w_out, w_in, down_projection_weight
):
    batches, row_count, width = inputs.shape
    parts, t = lax.axis_size("tensor"), lax.axis_index("tensor")
    dp = lax.axis_size("dp")
    share = row_count // parts
    ext = share + 2 * REACH

    def edge(a):
        last = lax.slice_in_dim(a, row_count - REACH, row_count, axis=1)
        initial = lax.slice_in_dim(a, 0, REACH, axis=1)
        outer = jnp.where(t == 0, last, initial)
        perm = [(2 * i, 2 * i + 2) for i in range(dp - 1)]
        perm += [(2 * i + 3, 2 * i + 1) for i in range(dp - 1)]
        outer = lax.ppermute(outer, ("dp", "tensor"), perm)
        inner = lax.dynamic_slice_in_dim(a, t * (share - REACH), share + REACH, 1)
        return jnp.where(
            t == 0,
            jnp.concatenate([outer, inner], axis=1),
            jnp.concatenate([inner, outer], axis=1),
        )

    cols = w_qkv.shape[2]
    units = w_in.shape[2]
    qkv_mine = w_qkv.reshape(width, 3 * cols)
    qkv_peer = fetch(qkv_mine)
    out_peer = fetch(w_out)
    in_mine = w_in.reshape(width, 2 * units)
    in_peer = fetch(in_mine)
    down_peer = fetch(down_projection_weight)
    x_ext = edge(inputs)
    pos_ext = edge(positions)[:, None, :]
    x_own = lax.dynamic_slice_in_dim(inputs, t * share, share, 1).astype(F32)
    cot = lax.dynamic_slice_in_dim(cotangent, t * share, share, 1)
    freq = jnp.power(
        F32(rope_base), -jnp.arange(HEAD_DIM // 2, dtype=F32) * (2.0 / HEAD_DIM)
    )[:, None]
    gain_row = gain_attn[None, :]
    normed, q0, k0, v0, p0, ctx0, cos, sin = attention_forward(
        True, x_ext, gain_row, qkv_mine, pos_ext, freq
    )
    q1, k1, v1, p1, ctx1 = attention_forward(
        False, normed, gain_row, qkv_peer, pos_ext, freq, (cos, sin)
    )
    context = jnp.concatenate([ctx0, ctx1], axis=2)
    out_full = jnp.concatenate([w_out, out_peer], axis=0)
    attended = jnp.einsum("mrc,cd->mrd", context, out_full, preferred_element_type=F32)
    state = x_own + attended
    normed_ffn = layer_norm(state, gain_ffn).astype(BF)
    gate_w = jnp.concatenate([in_mine[:, :units], in_peer[:, :units]], axis=1)
    up_w = jnp.concatenate([in_mine[:, units:], in_peer[:, units:]], axis=1)
    down_w = jnp.concatenate([down_projection_weight, down_peer], axis=0)
    gate = jnp.einsum("mrd,df->mrf", normed_ffn, gate_w, preferred_element_type=F32)
    up = jnp.einsum("mrd,df->mrf", normed_ffn, up_w, preferred_element_type=F32)
    grad_act = jnp.einsum("mrd,fd->mrf", cot, down_w, preferred_element_type=F32)
    acted, pull = jax.vjp(ffn_act, gate, up)
    grad_gate, grad_up = (g.astype(BF) for g in pull(grad_act))
    acted = acted.astype(BF)
    ffn_out = jnp.einsum("mrf,fd->mrd", acted, down_w, preferred_element_type=F32)
    layer_output = (state + ffn_out).astype(BF)
    normed_grad = jnp.einsum(
        "mrf,df->mrd", grad_gate, gate_w, preferred_element_type=F32
    ) + jnp.einsum("mrf,df->mrd", grad_up, up_w, preferred_element_type=F32)
    back, grad_gain_ffn = layer_norm_back(state, gain_ffn, normed_grad)
    state_grad = cot.astype(F32) + back
    mix_grad = state_grad.astype(BF)

    def over_rows(a, b):
        return jnp.einsum("mrd,mrc->dc", a, b, preferred_element_type=F32).astype(BF)

    grad_down = over_rows(cot, acted)
    grad_g, grad_u = over_rows(normed_ffn, grad_gate), over_rows(normed_ffn, grad_up)
    ffn_sum = reduce_weight(
        jnp.concatenate([grad_g[:, :units], grad_u[:, :units], grad_down[:, :units]], axis=1),
        jnp.concatenate([grad_g[:, units:], grad_u[:, units:], grad_down[:, units:]], axis=1),
    )
    grad_out = over_rows(mix_grad, context)
    out_sum = reduce_weight(grad_out[:, :cols], grad_out[:, cols:])
    gm1, nag1 = attention_backward(mix_grad, out_peer, qkv_peer, q1, k1, v1, p1, cos, sin)
    gm0, nag_ext = attention_backward(
        mix_grad, w_out, qkv_mine, q0, k0, v0, p0, cos, sin, nag1
    )
    qkv_sum = reduce_weight(over_rows(normed, gm0), over_rows(normed, gm1))

    devices = dp * parts
    up_perm = [(i, i + 1) for i in range(devices - 1)]
    down_perm = [(i + 1, i) for i in range(devices - 1)]
    from_before = lax.ppermute(nag_ext[:, ext - REACH :].astype(BF), ("dp", "tensor"), up_perm)
    from_after = lax.ppermute(nag_ext[:, :REACH].astype(BF), ("dp", "tensor"), down_perm)
    nag = (
        nag_ext[:, REACH : REACH + share]
        + jnp.pad(from_before.astype(F32), ((0, 0), (0, share - REACH), (0, 0)))
        + jnp.pad(from_after.astype(F32), ((0, 0), (share - REACH, 0), (0, 0)))
    )
    back, grad_gain_attn = layer_norm_back(x_own, gain_attn, nag)
    input_grad = state_grad + back
    gains = jnp.stack([grad_gain_attn, grad_gain_ffn])
    gains = gains + swap(gains, "tensor", 1)
    bit = 1
    while bit < dp:
        gains = gains + swap(gains, "dp", bit)
        bit *= 2
    mine = width // dp
    return (
        layer_output,
        input_grad,
        qkv_sum.reshape(mine, 3, cols),
        out_sum.T,
        ffn_sum[:, : 2 * units].reshape(mine, 2, units),
        ffn_sum[:, 2 * units :].T,
        gains[0],
        gains[1],
    )


def solution(mesh):
    placed = (
        P(None, "dp", None),
        P(None, "dp"),
        P(None, "dp", None),
        P(),
        P(),
        P(None, None, "tensor"),
        P("tensor", None),
        P(None, None, "tensor"),
        P("tensor", None),
    )
    return jax.shard_map(
        on_device,
        mesh=mesh,
        in_specs=placed,
        out_specs=(
            P(None, ("dp", "tensor"), None),
            P(None, ("dp", "tensor"), None),
            P("dp", None, "tensor"),
            P("tensor", "dp"),
            P("dp", None, "tensor"),
            P("tensor", "dp"),
            P(),
            P(),
        ),
        check_vma=False,
    )
```

```python
import functools

import jax
import jax.numpy as jnp
import numpy as np
from jax import lax
from jax.experimental import pallas as pl
from jax.experimental.pallas import tpu as pltpu
from jax.sharding import PartitionSpec as P

HEAD_DIM = 64
WINDOW = 128
REACH = WINDOW // 2
LANES = 128
SPAN = LANES + 2 * REACH
SCALE = HEAD_DIM**-0.5
DIGIT = 64

norm_eps = 1e-05
rope_base = 10000.0
masked_score = -1e30

BF = jnp.bfloat16
F32 = jnp.float32
VMEM_BYTES = 60 * 2**20


def mm(a, b, ca, cb):
    return lax.dot_general(a, b, (((ca,), (cb,)), ((), ())), preferred_element_type=F32)


def turned(v):
    lane = lax.broadcasted_iota(jnp.int32, v.shape, 1)
    low = (lane & 63) < 32
    return jnp.where(low, pltpu.roll(v, 96, 1), pltpu.roll(v, 32, 1))


def both_heads(v):
    lane = lax.broadcasted_iota(jnp.int32, v.shape, 1)
    zero = jnp.zeros_like(v)
    return jnp.concatenate(
        [jnp.where(lane < HEAD_DIM, v, zero), jnp.where(lane >= HEAD_DIM, v, zero)], axis=0
    )


def one_row_each(v):
    rows = v.shape[0] // 2
    lane = lax.broadcasted_iota(jnp.int32, (rows, v.shape[1]), 1)
    return jnp.where(lane < HEAD_DIM, v[:rows], v[rows:])


def norm_parts(v):
    centred = v - jnp.mean(v, axis=1, keepdims=True)
    spread = jnp.mean(centred * centred, axis=1, keepdims=True)
    r = lax.rsqrt(spread + norm_eps)
    return centred * r, r


def norm_back(xhat, r, e):
    return r * (
        e - jnp.mean(e, axis=1, keepdims=True) - xhat * jnp.mean(e * xhat, axis=1, keepdims=True)
    )


def transpose_into(at_ref, at, v, block, parity):
    vt = v.T
    width = vt.shape[0]
    if block is None:
        at_ref[:, at] = vt
        return
    for i in range(width // block):
        odd = parity if i % 2 == 0 else 1 - parity
        to = pl.multiple_of((i // 2) * block + odd * (width // 2), 16)
        at_ref[pl.ds(to, block), at] = vt[i * block : (i + 1) * block]


def join(own_ref, mine_ref, other_ref, parity, rows):
    own_ref[..., pl.ds(pl.multiple_of(parity * rows, 16), rows), :] = mine_ref[...]
    own_ref[..., pl.ds(pl.multiple_of((1 - parity) * rows, 16), rows), :] = other_ref[...]


class Specs:
    def __init__(self, batches, group=1):
        self.batches = batches // group
        self.group = group
        self.ins, self.args, self.outs, self.shapes = [], [], [], []

    def per(self, a, block=None, at=None, start=0):
        block = (self.group,) + (a.shape[1:] if block is None else block)
        last = self.batches - 1

        def index(m, place):
            m = jnp.minimum(m, last)
            rest = (0,) * (len(block) - 1) if at is None else at(place)
            return (m + start,) + rest

        self.ins.append(pl.BlockSpec(block, index))
        self.args.append(a)

    def whole(self, *arrays):
        for a in arrays:
            self.ins.append(
                pl.BlockSpec(
                    a.shape, lambda m, place, n=a.ndim: (0,) * n, pipeline_mode=pl.Buffered(1)
                )
            )
            self.args.append(a)

    def first_rows(self, a, rows):
        self.ins.append(
            pl.BlockSpec(
                (rows, a.shape[1]), lambda m, place: (0, 0), pipeline_mode=pl.Buffered(1)
            )
        )
        self.args.append(a)

    def after(self, *arrays):
        for a in arrays:
            self.ins.append(pl.BlockSpec(memory_space=pl.ANY))
            self.args.append(a)

    def out_part(self, batches, start, *dims, dtype=BF):
        last = self.batches - 1
        n = len(dims)
        self.outs.append(
            pl.BlockSpec(
                (1,) + dims, lambda m, place: (jnp.minimum(m, last) + start,) + (0,) * n
            )
        )
        self.shapes.append(jax.ShapeDtypeStruct((batches,) + dims, dtype))

    def out(self, *dims, dtype=BF):
        last = self.batches - 1
        n = len(dims)
        self.outs.append(
            pl.BlockSpec(
                (self.group,) + dims, lambda m, place: (jnp.minimum(m, last),) + (0,) * n
            )
        )
        self.shapes.append(jax.ShapeDtypeStruct((self.batches * self.group,) + dims, dtype))

    def out_columns(self, rows, cols, dtype=BF):
        last = self.batches - 1
        self.outs.append(pl.BlockSpec((rows, cols), lambda m, place: (0, jnp.minimum(m, last))))
        self.shapes.append(jax.ShapeDtypeStruct((rows, self.batches * cols), dtype))

    def out_whole(self, *dims, dtype=BF):
        self.outs.append(
            pl.BlockSpec(
                dims, lambda m, place: (0,) * len(dims), pipeline_mode=pl.Buffered(1)
            )
        )
        self.shapes.append(jax.ShapeDtypeStruct(dims, dtype))

    def call(self, kernel, place, name, steps=None, scratch=(), flops=0, moved=0, alias=None):
        return pl.pallas_call(
            kernel,
            grid_spec=pltpu.PrefetchScalarGridSpec(
                num_scalar_prefetch=1,
                grid=(self.batches if steps is None else steps,),
                in_specs=self.ins,
                out_specs=self.outs,
                scratch_shapes=list(scratch),
            ),
            out_shape=self.shapes,
            input_output_aliases={} if alias is None else alias,
            compiler_params=pltpu.CompilerParams(vmem_limit_bytes=VMEM_BYTES),
            cost_estimate=pl.CostEstimate(flops=flops, bytes_accessed=moved, transcendentals=0),
            name=name,
        )(place, *self.args)


def attend(q_ref, k_ref, v_ref, p_ref, ctx_ref, pos_row):
    rows, cols = q_ref.shape[1:]
    pos_col = jnp.broadcast_to(pos_row, (LANES, pos_row.shape[1])).T
    for b in range(rows // LANES):
        span = slice(b * LANES, b * LANES + SPAN)
        here = slice(b * LANES, (b + 1) * LANES)
        rel = (
            lax.broadcasted_iota(jnp.int32, (SPAN, LANES), 0)
            - REACH
            - lax.broadcasted_iota(jnp.int32, (SPAN, LANES), 1)
        )
        q_pos = pos_row[:, b * LANES + REACH : (b + 1) * LANES + REACH]
        since = jnp.where(rel > 0, pos_col[span], q_pos)
        far = jnp.abs(rel)
        bias = jnp.where((far <= REACH) & (since >= far), 0.0, masked_score).astype(F32)
        bias = jnp.concatenate([bias, bias], axis=1)
        for p in range(cols // LANES):
            at = slice(p * LANES, (p + 1) * LANES)
            scores = mm(k_ref[0, span, at], both_heads(q_ref[0, here, at]), 1, 1) + bias
            e = jnp.exp(scores - jnp.max(scores, axis=0, keepdims=True))
            probs = (e / jnp.sum(e, axis=0, keepdims=True)).astype(BF)
            p_ref[0, b, p] = probs
            ctx = mm(probs, v_ref[0, span, at], 0, 0)
            ctx_ref[0, here, at] = one_row_each(ctx).astype(BF)


def project(normed, w_ref, cos, sin, q_ref, k_ref, v_ref):
    rows, cols = q_ref.shape[1:]
    own = slice(REACH, REACH + rows)
    mixed_q = mm(normed[own], w_ref[0], 1, 0)
    mixed_k = mm(normed, w_ref[1], 1, 0)
    v_ref[0] = mm(normed, w_ref[2], 1, 0).astype(BF)
    for p in range(cols // LANES):
        at = slice(p * LANES, (p + 1) * LANES)
        mq, mk = mixed_q[:, at], mixed_k[:, at]
        q_ref[0, :, at] = (mq * cos[own] + turned(mq) * sin[own]).astype(BF) * SCALE
        k_ref[0, :, at] = (mk * cos + turned(mk) * sin).astype(BF)


def forward_own(
    block, place, x_ref, outer_ref, pos_ref, gain_ref, w_ref, freq_ref,
    normed_ref, at_ref, pos_out_ref, cos_ref, sin_ref, q_ref, k_ref, v_ref, p_ref, ctx_ref,
    x_scr,
):
    t, parity = place[0], place[1]
    rows, ext = q_ref.shape[1], k_ref.shape[1]
    inner = rows + REACH
    x_scr[pl.ds(pl.multiple_of((1 - t) * REACH, 16), inner), :] = x_ref[
        0, pl.ds(pl.multiple_of(t * (rows - REACH), 16), inner), :
    ]
    x_scr[pl.ds(pl.multiple_of(t * inner, 16), REACH), :] = outer_ref[0, :REACH]
    pos = pos_ref[0]
    digits = outer_ref[0, REACH:].astype(F32)[:1, : 2 * REACH]
    pos_outer = (digits[:, :REACH] * DIGIT + digits[:, REACH:]).astype(jnp.int32)
    pos_row = jnp.where(
        t == 0,
        jnp.concatenate([pos_outer, pos[:, :inner]], axis=1),
        jnp.concatenate([pos[:, rows - REACH :], pos_outer], axis=1),
    )
    pos_out_ref[0] = pos_row
    xhat, _ = norm_parts(x_scr[...].astype(F32))
    normed = (xhat * gain_ref[...]).astype(BF)
    normed_ref[0] = normed
    transpose_into(at_ref, slice(None), normed, block, parity)
    angles = freq_ref[...] * pos_row.astype(F32)
    c, s = jnp.cos(angles), jnp.sin(angles)
    cos = jnp.concatenate([c, c, c, c], axis=0).T
    sin = jnp.concatenate([-s, s, -s, s], axis=0).T
    cos_ref[0] = cos
    sin_ref[0] = sin
    project(normed, w_ref, cos, sin, q_ref, k_ref, v_ref)
    attend(q_ref, k_ref, v_ref, p_ref, ctx_ref, pos_row)


def forward_peer(
    place, normed_ref, pos_ref, cos_ref, sin_ref, mine_ref, other_ref,
    q_ref, k_ref, v_ref, p_ref, ctx_ref, w_scr,
):
    @pl.when(pl.program_id(0) == 0)
    def _():
        join(w_scr, mine_ref, other_ref, place[1], mine_ref.shape[1])

    project(normed_ref[0], w_scr, cos_ref[0], sin_ref[0], q_ref, k_ref, v_ref)
    attend(q_ref, k_ref, v_ref, p_ref, ctx_ref, pos_ref[0])


def attention_outs(s, rows, ext, cols):
    s.out(rows, cols)
    s.out(ext, cols)
    s.out(ext, cols)
    s.out(rows // LANES, cols // LANES, SPAN, 2 * LANES)
    s.out(rows, cols)


def split_units(units):
    return units // LANES * LANES, units % LANES


def ffn_kernel(
    block, place, x_ref, cot_ref, ctx0_ref, ctx1_ref, gain_ref,
    wo_ref, wi_ref, wd_ref, mine_ref, other_ref, y_ref, mix_ref, gain_out, keep_ref, send_ref,
    wo, half, gate_w, up_w, down_w, nft, cott, mixt, gg_s, gu_s, act_s, ctx_s,
):
    m = pl.program_id(0)
    parity = place[1]
    steps = pl.num_programs(0) - 1
    units = wi_ref.shape[1]
    main, rest_units = split_units(units)
    group, rows, width = x_ref.shape
    rows = group * rows

    @pl.when(m == 0)
    def _():
        cols = wo_ref.shape[0]
        wo[:cols] = wo_ref[...]

        def fetched(at, n):
            part = slice(at, at + n)
            join(half.at[: 2 * n], mine_ref.at[part], other_ref.at[part], parity, n)

        fetched(0, cols // 2)
        wo[cols:] = half[:cols]
        for j, (full, own) in enumerate(((gate_w, wi_ref.at[0]), (up_w, wi_ref.at[1]), (down_w, wd_ref))):
            fetched(cols // 2 + j * (units // 2), units // 2)
            full[:main] = own[:main]
            full[main : 2 * main] = half[:main]
            full[2 * main : 2 * main + rest_units] = own[main:]
            full[2 * main + rest_units :] = half[main:units]
        gain_out[...] = jnp.zeros_like(gain_out)

    @pl.when(m < steps)
    def _():
        here = pl.ds(pl.multiple_of(m * rows, 16), rows)
        along = pl.ds(pl.multiple_of(m * rows, LANES), rows)

        def flat(ref):
            return ref[...].reshape(rows, ref.shape[2])

        ctx = jnp.concatenate([flat(ctx0_ref), flat(ctx1_ref)], axis=1)
        ctx_s[here, :] = ctx
        state = flat(x_ref).astype(F32) + mm(ctx, wo[...], 1, 0)
        xhat, r = norm_parts(state)
        gain = gain_ref[...]
        nf = (xhat * gain).astype(BF)
        transpose_into(nft, along, nf, block, parity)
        cot = flat(cot_ref)
        transpose_into(cott, along, cot, block, parity)
        step = 2 * LANES
        for c in range(0, 2 * units, step):
            at = slice(c, min(c + step, 2 * units))
            g = mm(nf, gate_w[at], 1, 1)
            u = mm(nf, up_w[at], 1, 1)
            ga = mm(cot, down_w[at], 1, 1)
            cdf = 0.5 * (1.0 + lax.erf(g * 0.5**0.5))
            gelu = g * cdf
            slope = cdf + g * jnp.exp(-0.5 * g * g) * 0.3989422804014327
            act_s[here, at] = (gelu * u).astype(BF)
            gg_s[here, at] = (ga * u * slope).astype(BF)
            gu_s[here, at] = (ga * gelu).astype(BF)
        out = state + mm(act_s[here, :], down_w[...], 1, 0)
        y_ref[...] = out.astype(BF).reshape(y_ref.shape)
        grad = mm(gg_s[here, :], gate_w[...], 1, 0) + mm(gu_s[here, :], up_w[...], 1, 0)
        gain_out[...] += jnp.sum(grad * xhat, axis=0, keepdims=True)
        sg = cot.astype(F32) + norm_back(xhat, r, grad * gain)
        mix = sg.astype(BF)
        mix_ref[...] = mix.reshape(mix_ref.shape)
        transpose_into(mixt, along, mix, block, parity)

    @pl.when(m == steps)
    def _():
        cols = wo_ref.shape[0]
        for j, to_ref in ((0, keep_ref), (1, send_ref)):
            at = slice(j * width // 2, (j + 1) * width // 2)
            ends = []
            for i, (at_ref, b_ref) in enumerate(((nft, gg_s), (nft, gu_s), (cott, act_s))):
                to = slice(i * main, (i + 1) * main)
                for peer in range(2):
                    part = b_ref[:, peer * main : (peer + 1) * main]
                    to_ref[peer, :, to] = mm(at_ref[at], part, 1, 0).astype(BF)
                ends.append(mm(at_ref[at], b_ref[:, 2 * main :], 1, 0).astype(BF))
            zero = jnp.zeros((width // 2, rest_units), BF)
            for peer in range(2):
                to = slice(3 * main, 3 * main + cols)
                part = ctx_s[:, peer * cols : (peer + 1) * cols]
                to_ref[peer, :, to] = mm(mixt[at], part, 1, 0).astype(BF)
                part = slice(peer * rest_units, (peer + 1) * rest_units)
                to_ref[peer, :, 3 * main + cols :] = jnp.concatenate(
                    [end[:, part] for end in ends] + [zero], axis=1
                )


def backward_kernel(peer, last, after, place, mix_ref, wo_ref, w_ref, *rest):
    rest = list(rest)
    if peer:
        wo_other, w_other = rest.pop(0), rest.pop(0)
    q_ref, k_ref, v_ref, p_ref, cos_ref, sin_ref = rest[:6]
    rest = rest[6:]
    if not peer:
        before_ref, normed_ref = rest.pop(0), rest.pop(0)
    if last:
        at_ref, gm_before = rest.pop(0), rest.pop(0)
    rest = rest[after:]
    nag_ref = rest.pop(0)
    if not peer:
        left_ref, right_ref, gain_out = rest.pop(0), rest.pop(0), rest.pop(0)
    if last:
        keep_ref, send_ref = rest.pop(0), rest.pop(0)
    else:
        gm_out = rest.pop(0)
    dk_ref, dv_ref, gm_ref = rest.pop(0), rest.pop(0), rest.pop(0)
    m = pl.program_id(0)
    if peer:
        wo_scr, w_scr = rest

        @pl.when(m == 0)
        def _():
            join(wo_scr, wo_ref, wo_other, place[1], wo_ref.shape[0])
            join(w_scr, w_ref, w_other, place[1], w_ref.shape[1])

        wo_ref, w_ref = wo_scr, w_scr
    rows, cols = q_ref.shape[1:]
    ext = k_ref.shape[1]
    own = slice(REACH, REACH + rows)

    def one_batch():
        dctx = mm(mix_ref[0], wo_ref[...], 1, 1).astype(BF)
        dk_ref[...] = jnp.zeros_like(dk_ref)
        dv_ref[...] = jnp.zeros_like(dv_ref)
        cos, sin = cos_ref[0], sin_ref[0]
        gm_ref[m, :REACH, :cols] = jnp.zeros((REACH, cols), BF)
        gm_ref[m, REACH + rows :, :cols] = jnp.zeros((REACH, cols), BF)
        for b in range(rows // LANES):
            span = slice(b * LANES, b * LANES + SPAN)
            here = slice(b * LANES, (b + 1) * LANES)
            there = slice(b * LANES + REACH, (b + 1) * LANES + REACH)
            for p in range(cols // LANES):
                at = slice(p * LANES, (p + 1) * LANES)
                grad = both_heads(dctx[here, at])
                probs_low = p_ref[0, b, p]
                probs = probs_low.astype(F32)
                weighted = probs * mm(v_ref[0, span, at], grad, 1, 1)
                balance = jnp.sum(weighted, axis=0, keepdims=True)
                grad_scores = (weighted - probs * balance).astype(BF)
                dv_ref[span, at] += mm(probs_low, grad, 1, 0)
                dk_ref[span, at] += mm(grad_scores, both_heads(q_ref[0, here, at]), 1, 0)
                dq = one_row_each(mm(grad_scores, k_ref[0, span, at], 0, 0)) * SCALE
                gm_ref[m, there, at] = (dq * cos[there] - turned(dq) * sin[there]).astype(BF)
        for p in range(cols // LANES):
            at = slice(p * LANES, (p + 1) * LANES)
            dk = dk_ref[:, at]
            gm_ref[m, :, cols + p * LANES : cols + (p + 1) * LANES] = (
                dk * cos - turned(dk) * sin
            ).astype(BF)
        gm_ref[m, :, 2 * cols :] = dv_ref[...].astype(BF)
        nag = mm(gm_ref[m, :, cols : 2 * cols], w_ref[1], 1, 1)
        nag = nag + mm(gm_ref[m, :, 2 * cols :], w_ref[2], 1, 1)
        nag_q = mm(gm_ref[m, own, :cols], w_ref[0], 1, 1)
        if peer:
            nag_ref[0, :REACH] = nag[:REACH].astype(BF)
            nag_ref[0, own] = (nag[own] + nag_q).astype(BF)
            nag_ref[0, REACH + rows :] = nag[REACH + rows :].astype(BF)
        else:
            nag = nag + before_ref[0].astype(F32)
            left_ref[0] = nag[:REACH].astype(BF)
            right_ref[0] = nag[REACH + rows :].astype(BF)
            nag_own = nag[own] + nag_q
            nag_ref[0] = nag_own.astype(BF)
            normed = normed_ref[0].astype(F32)
            total = (
                jnp.sum(nag[:REACH] * normed[:REACH], axis=0, keepdims=True)
                + jnp.sum(nag_own * normed[own], axis=0, keepdims=True)
                + jnp.sum(nag[REACH + rows :] * normed[REACH + rows :], axis=0, keepdims=True)
            )

            @pl.when(m == 0)
            def _():
                gain_out[...] = total

            @pl.when(m > 0)
            def _():
                gain_out[...] += total

        if not last:
            gm_out[0] = gm_ref[m]

    if not last:
        one_batch()
        return
    steps = pl.num_programs(0) - 1
    pl.when(m < steps)(one_batch)

    @pl.when(m == steps)
    def _():
        half, earlier = at_ref.shape[0] // 2, gm_before.shape[0] * ext
        one = gm_before[...].reshape(earlier, 3 * cols)
        two = gm_ref[...].reshape(-1, 3 * cols)
        for j, to in ((0, keep_ref), (1, send_ref)):
            at = slice(j * half, (j + 1) * half)
            total = mm(at_ref[at, :earlier], one, 1, 0) + mm(at_ref[at, earlier:], two, 1, 0)
            to[...] = total.astype(BF)


def last_kernel(place, x_ref, nag_ref, before_ref, after_ref, mix_ref, gain_ref, *rest):
    out_ref = rest[-1]
    rows = nag_ref.shape[1]
    gain = gain_ref[...]
    step = 32
    for c in range(0, rows, step):
        at = slice(c, c + step)
        xhat, r = norm_parts(x_ref[0, at].astype(F32))
        nag = nag_ref[0, at].astype(F32)
        if c < REACH:
            nag = nag + before_ref[0, at].astype(F32)
        if c >= rows - REACH:
            nag = nag + after_ref[0, c - rows + REACH : c - rows + REACH + step].astype(F32)
        out_ref[0, at] = mix_ref[0, at].astype(F32) + norm_back(xhat, r, nag * gain)


def swap(x, axis, bit):
    size = lax.axis_size(axis)
    return lax.ppermute(x, axis, [(i, i ^ bit) for i in range(size)])


def then(value, *earlier):
    return lax.optimization_barrier((value, *earlier))[0]


def quarter(half, axis):
    rows = half.shape[axis] // 2
    return lax.dynamic_slice_in_dim(half, (lax.axis_index("dp") % 2) * rows, rows, axis)


class Halving:
    def __init__(self, total, rows, bit):
        self.mine = (lax.axis_index("dp") // bit) % 2
        self.g = total.astype(BF).reshape(-1, 2, rows, total.shape[-1])
        self.sent = lax.dynamic_index_in_dim(self.g, 1 - self.mine, 1, keepdims=False)
        self.got = swap(self.sent, "dp", bit)

    def total(self, *earlier):
        keep = lax.dynamic_index_in_dim(self.g, self.mine, 1, keepdims=False)
        total = keep.astype(F32) + then(self.got, *earlier).astype(F32)
        return total.reshape(-1, total.shape[-1])


def sum_from(total, rows, bit, size):
    while bit < size:
        total = Halving(total, rows, bit).total()
        bit *= 2
    return total


def sorted_halves(keep, send, block, size):
    if block is not None:
        return keep, send
    n, half, cols = keep.shape
    g = jnp.concatenate([keep, send], axis=1).reshape(n, size // 2, 2, 2 * half // size, cols)
    parity = lax.axis_index("dp") % 2
    keep = lax.dynamic_index_in_dim(g, parity, 2, keepdims=False)
    send = lax.dynamic_index_in_dim(g, 1 - parity, 2, keepdims=False)
    return keep.reshape(n, half, cols), send.reshape(n, half, cols)


def on_device(
    inputs, positions, cotangent, gain_attn, gain_ffn, w_qkv, w_out, w_in, down_projection_weight
):
    batches, row_count, width = inputs.shape
    parts, t = lax.axis_size("tensor"), lax.axis_index("tensor")
    dp = lax.axis_size("dp")
    rows = row_count // parts
    ext = rows + 2 * REACH
    cols = w_qkv.shape[2]
    units = w_in.shape[2]
    place = jnp.stack([t, lax.axis_index("dp") % 2]).astype(jnp.int32)
    mine = width // dp
    block = mine if mine % 16 == 0 else None

    digits = jnp.concatenate([positions // DIGIT, positions % DIGIT], axis=1).astype(BF)
    digits = digits.reshape(batches, 2, row_count)
    edges = [
        jnp.concatenate(
            [
                lax.slice_in_dim(inputs, at, at + REACH, axis=1),
                jnp.broadcast_to(
                    jnp.pad(
                        lax.slice_in_dim(digits, at, at + REACH, axis=2).reshape(batches, 1, -1),
                        ((0, 0), (0, 0), (0, width - 2 * REACH)),
                    ),
                    (batches, 16, width),
                ),
            ],
            axis=1,
        )
        for at in (row_count - REACH, 0)
    ]
    perm = [(2 * i, 2 * i + 2) for i in range(dp - 1)]
    perm += [(2 * i + 3, 2 * i + 1) for i in range(dp - 1)]
    x_outer = lax.ppermute(jnp.where(t == 0, *edges), ("dp", "tensor"), perm)

    qkv = w_qkv.transpose(1, 0, 2)
    w_in = w_in.transpose(1, 2, 0)
    w_down = down_projection_weight
    qkv_mine = swap(quarter(qkv, 1), "tensor", 1)
    freq = jnp.asarray(
        np.power(
            np.float32(rope_base),
            -np.arange(HEAD_DIM // 2, dtype=np.float32) * np.float32(2.0 / HEAD_DIM),
        )[:, None]
    )

    work = 2 * batches * ext * width * 3 * cols + 8 * batches * rows * cols * SPAN
    s = Specs(batches)
    s.per(inputs)
    s.per(x_outer)
    s.per(positions[:, None, :])
    s.whole(gain_attn[None, :], qkv, freq)
    s.out(ext, width)
    s.out_columns(width, ext)
    s.out(1, ext, dtype=jnp.int32)
    s.out(ext, LANES, dtype=F32)
    s.out(ext, LANES, dtype=F32)
    attention_outs(s, rows, ext, cols)
    normed, normed_t, pos_ext, cos, sin, q0, k0, v0, p0, ctx0 = s.call(
        functools.partial(forward_own, block), place, "attn_fwd_own",
        scratch=[pltpu.VMEM((ext, width), BF)], flops=work, moved=20 * batches * ext * width,
    )

    rest_mine = jnp.concatenate(
        [quarter(w_out, 0), quarter(w_in, 1).reshape(units, width), quarter(w_down, 0)]
    )
    rest_mine = swap(then(rest_mine, ctx0), "tensor", 1)
    qkv_other = swap(then(qkv_mine, ctx0), "dp", 1)
    s = Specs(batches)
    for a in (normed, pos_ext, cos, sin):
        s.per(a)
    s.whole(qkv_mine, qkv_other)
    attention_outs(s, rows, ext, cols)
    q1, k1, v1, p1, ctx1 = s.call(
        forward_peer, place, "attn_fwd_peer",
        scratch=[pltpu.VMEM((3, width, cols), BF)], flops=work, moved=20 * batches * ext * cols,
    )
    rest_other = swap(then(rest_mine, ctx1), "dp", 1)

    own_block = (rows, width)
    group = 2 if batches % 2 == 0 else 1
    s = Specs(batches, group)
    s.per(inputs, own_block, lambda place: (place[0], 0))
    s.per(cotangent, own_block, lambda place: (place[0], 0))
    s.per(ctx0)
    s.per(ctx1)
    s.whole(gain_ffn[None, :], w_out, w_in, w_down, rest_mine, rest_other)
    s.out(rows, width)
    s.out(rows, width)
    s.out_whole(1, width, dtype=F32)
    main, rest = split_units(units)
    in_cols, out_cols = 2 * main, 3 * main + cols + 4 * rest
    for _ in range(2):
        s.out_whole(2, width // 2, out_cols)
    y, mix, gain_ffn_part, keep, send = s.call(
        functools.partial(ffn_kernel, block), place, "ffn", steps=s.batches + 1,
        scratch=[
            pltpu.VMEM((2 * cols, width), BF),
            pltpu.VMEM((max(units, cols), width), BF),
            pltpu.VMEM((2 * units, width), BF),
            pltpu.VMEM((2 * units, width), BF),
            pltpu.VMEM((2 * units, width), BF),
        ] + [pltpu.VMEM((width, batches * rows), BF)] * 3
        + [pltpu.VMEM((batches * rows, 2 * units), BF)] * 3
        + [pltpu.VMEM((batches * rows, 2 * cols), BF)],
        flops=6 * batches * rows * width * 2 * (3 * units + cols), moved=4 * 10**7,
    )
    keep, send = sorted_halves(keep, send, block, dp)
    got = swap(send, "dp", 1)

    half_rows = cols // 2

    def backward(peer, saved, start, stop, nag1, gm_before, after, name):
        last, part = gm_before is not None, stop - start
        s = Specs(part)
        s.per(mix, start=start)
        if peer:
            s.first_rows(rest_mine, half_rows)
            s.whole(qkv_mine)
            s.first_rows(rest_other, half_rows)
            s.whole(qkv_other)
        else:
            s.whole(w_out, qkv)
        for a in (*saved, cos, sin):
            s.per(a, start=start)
        if not peer:
            s.per(nag1, start=start)
            s.per(normed, start=start)
        if last:
            s.whole(normed_t, gm_before)
        s.after(*after)
        scratch = [pltpu.VMEM((ext, cols), F32)] * 2 + [pltpu.VMEM((part, ext, 3 * cols), BF)]
        alias = None
        if peer:
            if nag1 is not None:
                s.after(nag1)
                after += (nag1,)
                alias = {len(s.args): 0}
            s.out_part(batches, start, ext, width)
            scratch += [pltpu.VMEM((cols, width), BF), pltpu.VMEM((3, width, cols), BF)]
        else:
            s.out(rows, width)
            s.out(REACH, width)
            s.out(REACH, width)
            s.out_whole(1, width, dtype=F32)
        if last:
            s.out_whole(width // 2, 3 * cols)
            s.out_whole(width // 2, 3 * cols)
        else:
            s.out(ext, 3 * cols)
        return s.call(
            functools.partial(backward_kernel, peer, last, len(after)),
            place, name, steps=part + 1 if last else None, scratch=scratch, alias=alias,
            flops=(2 * ext * width * 4 * cols + 20 * rows * cols * SPAN) * part,
            moved=30 * part * ext * cols,
        )

    def halos(to_before, to_after):
        devices = dp * parts
        up = [(i, i + 1) for i in range(devices - 1)]
        down = [(i + 1, i) for i in range(devices - 1)]
        return (
            lax.ppermute(to_after, ("dp", "tensor"), up),
            lax.ppermute(to_before, ("dp", "tensor"), down),
        )

    saved0, saved1 = (q0, k0, v0, p0), (q1, k1, v1, p1)
    nag1, gm1a = backward(True, saved1, 0, 1, None, None, (), "attn_bwd_peer_a")
    got = then(got, gm1a)

    def cores(at, peer):
        return (keep[peer, :, at].astype(F32) + got[peer, :, at].astype(F32)).astype(BF)

    a_at, b_at = slice(0, in_cols), slice(in_cols, None)
    a_peer = cores(a_at, 1)
    a_from_peer = swap(a_peer, "tensor", 1)
    b_sum = Halving(cores(b_at, slice(None)).reshape(width, -1), mine, 2)
    nag1, keep1, send1 = backward(
        True, saved1, 1, batches, nag1, gm1a, (a_peer, b_sum.sent), "attn_bwd_peer_b"
    )
    keep1, send1 = sorted_halves(keep1[None], send1[None], block, dp)
    got1 = swap(send1[0], "dp", 1)
    a_own = cores(a_at, 0).astype(F32)
    a_sum = Halving(a_own + then(a_from_peer, send1).astype(F32), mine, 2)
    b_sum = b_sum.total(send1).reshape(2, width // 4, -1)
    b_peer = b_sum[1].astype(BF)
    b_from_peer = swap(b_peer, "tensor", 1)
    part = batches // 2
    nag_a, to_before, to_after, gain_a, gm0a = backward(
        False, saved0, 0, part, nag1, None, (send1, a_sum.sent, b_peer), "attn_bwd_own_a"
    )
    halos_a = halos(to_before, to_after)
    qkv_peer = (keep1[0].astype(F32) + then(got1, gm0a).astype(F32)).astype(BF)
    qkv_from_peer = swap(qkv_peer, "tensor", 1)
    b_sum = b_sum[0] + then(b_from_peer, gm0a).astype(F32)
    f_sum = Halving(jnp.concatenate([a_sum.total(gm0a), b_sum], axis=1), mine, 4)
    nag_b, to_before, to_after, gain_b, keep0, send0 = backward(
        False, saved0, part, batches, nag1, gm0a, (qkv_peer, f_sum.sent), "attn_bwd_own_b"
    )
    keep0, send0 = sorted_halves(keep0[None], send0[None], block, dp)
    got0 = swap(send0[0], "dp", 1)
    halos_b = halos(to_before, to_after)
    f_sum = Halving(f_sum.total(send0), mine, 8)
    gains = jnp.concatenate([(gain_a + gain_b) / gain_attn[None, :], gain_ffn_part])
    index = [2 * i + j for i in range(dp) for j in range(2)]
    both = lax.ppermute(gains, ("dp", "tensor"), [(i, i ^ 3) for i in index])
    gains_got = swap(gains, "dp", 1), swap(gains, "tensor", 1), both

    def finish(nag, halos, start, after, into, name):
        s = Specs(part)
        s.per(inputs, own_block, lambda place: (place[0], 0), start=start)
        for a in (nag, *halos):
            s.per(a)
        s.per(mix, start=start)
        s.whole(gain_attn[None, :])
        s.after(*after)
        if into is not None:
            s.after(into)
        s.outs.append(pl.BlockSpec((1, rows, width), lambda m, place: (m + start, 0, 0)))
        s.shapes.append(jax.ShapeDtypeStruct((batches, rows, width), F32))
        return s.call(
            last_kernel, place, name, flops=10**7, moved=8 * part * rows * width,
            alias=None if into is None else {len(s.args): 0},
        )[0]

    input_grad = finish(nag_a, halos_a, 0, (send0, f_sum.sent, gains), None, "input_grad_a")
    got0, qkv_from_peer, *gains_got = lax.optimization_barrier(
        (got0, qkv_from_peer, *gains_got, input_grad)
    )[:5]
    qkv_sum = keep0[0].astype(F32) + got0.astype(F32) + qkv_from_peer.astype(F32)
    qkv_sum = Halving(qkv_sum, mine, 2)
    gains = gains + sum(gains_got)
    gains_got = swap(gains, "dp", 2)
    input_grad = finish(
        nag_b, halos_b, part, (qkv_sum.sent, gains), input_grad, "input_grad_b"
    )
    f_sum = sum_from(f_sum.total(input_grad), mine, 16, dp)
    bit = 4
    while bit <= dp:
        gains = gains + then(gains_got, input_grad)
        qkv_sum = qkv_sum.total(input_grad)
        if bit < dp:
            qkv_sum = Halving(qkv_sum, mine, bit)
            gains_got = swap(gains, "dp", bit)
        bit *= 2
    qkv_sum = qkv_sum.reshape(mine, 3, cols)

    def unit_columns(j):
        tail = 3 * main + cols + j * rest
        return jnp.concatenate(
            [f_sum[:, j * main : (j + 1) * main], f_sum[:, tail : tail + rest]], axis=1
        )

    return (
        y,
        input_grad,
        qkv_sum,
        f_sum[:, 3 * main : 3 * main + cols].T,
        jnp.stack([unit_columns(0), unit_columns(1)], axis=1),
        unit_columns(2).T,
        gains[0],
        gains[1],
    )


def solution(mesh):
    placed = (
        P(None, "dp", None),
        P(None, "dp"),
        P(None, "dp", None),
        P(),
        P(),
        P(None, None, "tensor"),
        P("tensor", None),
        P(None, None, "tensor"),
        P("tensor", None),
    )
    return jax.shard_map(
        on_device,
        mesh=mesh,
        in_specs=placed,
        out_specs=(
            P(None, ("dp", "tensor"), None),
            P(None, ("dp", "tensor"), None),
            P("dp", None, "tensor"),
            P("tensor", "dp"),
            P("dp", None, "tensor"),
            P("tensor", "dp"),
            P(),
            P(),
        ),
        check_vma=False,
    )
```

```python
import functools

import jax
import jax.numpy as jnp
import numpy as np
from jax import lax
from jax.experimental import pallas as pl
from jax.experimental.pallas import tpu as pltpu
from jax.sharding import PartitionSpec as P

HEAD_DIM = 64
WINDOW = 128
REACH = WINDOW // 2
LANES = 128
SPAN = LANES + 2 * REACH
SCALE = HEAD_DIM**-0.5
DIGIT = 64
MORE = 16

norm_eps = 1e-05
rope_base = 10000.0
masked_score = -1e30

BF = jnp.bfloat16
F32 = jnp.float32
VMEM_BYTES = 60 * 2**20


def mm(a, b, ca, cb):
    return lax.dot_general(a, b, (((ca,), (cb,)), ((), ())), preferred_element_type=F32)


def turned(v):
    lane = lax.broadcasted_iota(jnp.int32, v.shape, 1)
    low = (lane & 63) < 32
    return jnp.where(low, pltpu.roll(v, 96, 1), pltpu.roll(v, 32, 1))


def both_heads(v):
    lane = lax.broadcasted_iota(jnp.int32, v.shape, 1)
    zero = jnp.zeros_like(v)
    return jnp.concatenate(
        [jnp.where(lane < HEAD_DIM, v, zero), jnp.where(lane >= HEAD_DIM, v, zero)], axis=0
    )


def one_row_each(v):
    rows = v.shape[0] // 2
    lane = lax.broadcasted_iota(jnp.int32, (rows, v.shape[1]), 1)
    return jnp.where(lane < HEAD_DIM, v[:rows], v[rows:])


def norm_parts(v):
    centred = v - jnp.mean(v, axis=1, keepdims=True)
    spread = jnp.mean(centred * centred, axis=1, keepdims=True)
    r = lax.rsqrt(spread + norm_eps)
    return centred * r, r


def norm_back(xhat, r, e):
    return r * (
        e - jnp.mean(e, axis=1, keepdims=True) - xhat * jnp.mean(e * xhat, axis=1, keepdims=True)
    )


def transpose_into(at_ref, at, v, block, parity):
    vt = v.T
    width = vt.shape[0]
    if block is None:
        at_ref[:, at] = vt
        return
    for i in range(width // block):
        odd = parity if i % 2 == 0 else 1 - parity
        to = pl.multiple_of((i // 2) * block + odd * (width // 2), 16)
        at_ref[pl.ds(to, block), at] = vt[i * block : (i + 1) * block]


def join(own_ref, mine_ref, other_ref, parity, rows):
    own_ref[..., pl.ds(pl.multiple_of(parity * rows, 16), rows), :] = mine_ref[...]
    own_ref[..., pl.ds(pl.multiple_of((1 - parity) * rows, 16), rows), :] = other_ref[...]


class Specs:
    def __init__(self, batches, group=1):
        self.batches = batches // group
        self.group = group
        self.ins, self.args, self.outs, self.shapes = [], [], [], []

    def per(self, a, block=None, at=None, start=0):
        block = (self.group,) + (a.shape[1:] if block is None else block)
        last = self.batches - 1

        def index(m, place):
            m = jnp.minimum(m, last)
            rest = (0,) * (len(block) - 1) if at is None else at(place)
            return (m + start,) + rest

        self.ins.append(pl.BlockSpec(block, index))
        self.args.append(a)

    def whole(self, *arrays):
        for a in arrays:
            self.ins.append(
                pl.BlockSpec(
                    a.shape, lambda m, place, n=a.ndim: (0,) * n, pipeline_mode=pl.Buffered(1)
                )
            )
            self.args.append(a)

    def after(self, *arrays):
        for a in arrays:
            self.ins.append(pl.BlockSpec(memory_space=pl.ANY))
            self.args.append(a)

    def out_part(self, batches, start, *dims, dtype=BF):
        last = self.batches - 1
        n = len(dims)
        self.outs.append(
            pl.BlockSpec(
                (1,) + dims, lambda m, place: (jnp.minimum(m, last) + start,) + (0,) * n
            )
        )
        self.shapes.append(jax.ShapeDtypeStruct((batches,) + dims, dtype))

    def out(self, *dims, dtype=BF):
        last = self.batches - 1
        n = len(dims)
        self.outs.append(
            pl.BlockSpec(
                (self.group,) + dims, lambda m, place: (jnp.minimum(m, last),) + (0,) * n
            )
        )
        self.shapes.append(jax.ShapeDtypeStruct((self.batches * self.group,) + dims, dtype))

    def out_columns(self, rows, cols, dtype=BF):
        last = self.batches - 1
        self.outs.append(pl.BlockSpec((rows, cols), lambda m, place: (0, jnp.minimum(m, last))))
        self.shapes.append(jax.ShapeDtypeStruct((rows, self.batches * cols), dtype))

    def out_whole(self, *dims, dtype=BF):
        self.outs.append(
            pl.BlockSpec(
                dims, lambda m, place: (0,) * len(dims), pipeline_mode=pl.Buffered(1)
            )
        )
        self.shapes.append(jax.ShapeDtypeStruct(dims, dtype))

    def call(self, kernel, place, name, steps=None, scratch=(), flops=0, moved=0, alias=None):
        return pl.pallas_call(
            kernel,
            grid_spec=pltpu.PrefetchScalarGridSpec(
                num_scalar_prefetch=1,
                grid=(self.batches if steps is None else steps,),
                in_specs=self.ins,
                out_specs=self.outs,
                scratch_shapes=list(scratch),
            ),
            out_shape=self.shapes,
            input_output_aliases={} if alias is None else alias,
            compiler_params=pltpu.CompilerParams(vmem_limit_bytes=VMEM_BYTES),
            cost_estimate=pl.CostEstimate(flops=flops, bytes_accessed=moved, transcendentals=0),
            name=name,
        )(place, *self.args)


def in_turn(units, first, mid, last):
    begun, middle, n = {}, {}, len(units)
    for i in range(-1, n + 1):
        if i + 1 < n:
            begun[i + 1] = first(*units[i + 1])
        if i >= 1:
            last(*units[i - 1], begun.pop(i - 1), middle.pop(i - 1))
        if 0 <= i < n:
            middle[i] = mid(*units[i], begun[i])


def places(b, p):
    here = slice(b * LANES, (b + 1) * LANES)
    return here, slice(b * LANES, b * LANES + SPAN), slice(p * LANES, (p + 1) * LANES)


def attend(q_ref, k_ref, v_ref, p_ref, ctx_ref, pos_row):
    rows, cols = q_ref.shape[1:]
    pos_col = jnp.broadcast_to(pos_row, (LANES, pos_row.shape[1])).T
    biases = []
    for b in range(rows // LANES):
        rel = (
            lax.broadcasted_iota(jnp.int32, (SPAN, LANES), 0)
            - REACH
            - lax.broadcasted_iota(jnp.int32, (SPAN, LANES), 1)
        )
        q_pos = pos_row[:, b * LANES + REACH : (b + 1) * LANES + REACH]
        since = jnp.where(rel > 0, pos_col[b * LANES : b * LANES + SPAN], q_pos)
        far = jnp.abs(rel)
        bias = jnp.where((far <= REACH) & (since >= far), 0.0, masked_score).astype(F32)
        biases.append(jnp.concatenate([bias, bias], axis=1))

    def first(b, p):
        here, span, at = places(b, p)
        return mm(k_ref[0, span, at], both_heads(q_ref[0, here, at]), 1, 1)

    def mid(b, p, scores):
        scores = scores + biases[b]
        e = jnp.exp(scores - jnp.max(scores, axis=0, keepdims=True))
        probs = (e * (1.0 / jnp.sum(e, axis=0, keepdims=True))).astype(BF)
        p_ref[0, b, p] = probs
        return probs

    def last(b, p, _, probs):
        here, span, at = places(b, p)
        ctx_ref[0, here, at] = one_row_each(mm(probs, v_ref[0, span, at], 0, 0)).astype(BF)

    units = [(b, p) for b in range(rows // LANES) for p in range(cols // LANES)]
    in_turn(units, first, mid, last)


def project(normed, w_ref, cos, sin, q_ref, k_ref, v_ref):
    rows, cols = q_ref.shape[1:]
    own = slice(REACH, REACH + rows)
    mixed_q = mm(normed[own], w_ref[0], 1, 0)
    mixed_k = mm(normed, w_ref[1], 1, 0)
    v_ref[0] = mm(normed, w_ref[2], 1, 0).astype(BF)
    for p in range(cols // LANES):
        at = slice(p * LANES, (p + 1) * LANES)
        mq, mk = mixed_q[:, at], mixed_k[:, at]
        q_ref[0, :, at] = (mq * cos[own] + turned(mq) * sin[own]).astype(BF) * SCALE
        k_ref[0, :, at] = (mk * cos + turned(mk) * sin).astype(BF)


def forward_own(
    block, place, x_ref, outer_ref, pos_ref, gain_ref, w_ref, freq_ref, _out, _rest,
    normed_ref, at_ref, pos_out_ref, cos_ref, sin_ref, q_ref, k_ref, v_ref, p_ref, ctx_ref,
    x_scr,
):
    t, parity = place[0], place[1]
    rows, ext = q_ref.shape[1], k_ref.shape[1]
    inner = rows + REACH
    x_scr[pl.ds(pl.multiple_of((1 - t) * REACH, 16), inner), :] = x_ref[
        0, pl.ds(pl.multiple_of(t * (rows - REACH), 16), inner), :
    ]
    x_scr[pl.ds(pl.multiple_of(t * inner, 16), REACH), :] = outer_ref[0, :REACH]
    pos = pos_ref[0]
    digits = outer_ref[0, REACH:].astype(F32)[:1, : 2 * REACH]
    pos_outer = (digits[:, :REACH] * DIGIT + digits[:, REACH:]).astype(jnp.int32)
    pos_row = jnp.where(
        t == 0,
        jnp.concatenate([pos_outer, pos[:, :inner]], axis=1),
        jnp.concatenate([pos[:, rows - REACH :], pos_outer], axis=1),
    )
    pos_out_ref[0] = pos_row
    xhat, _ = norm_parts(x_scr[...].astype(F32))
    normed = (xhat * gain_ref[...]).astype(BF)
    normed_ref[0] = normed
    transpose_into(at_ref, slice(None), normed, block, parity)
    angles = freq_ref[...] * pos_row.astype(F32)
    c, s = jnp.cos(angles), jnp.sin(angles)
    cos = jnp.concatenate([c, c, c, c], axis=0).T
    sin = jnp.concatenate([-s, s, -s, s], axis=0).T
    cos_ref[0] = cos
    sin_ref[0] = sin
    project(normed, w_ref, cos, sin, q_ref, k_ref, v_ref)
    attend(q_ref, k_ref, v_ref, p_ref, ctx_ref, pos_row)


def forward_peer(
    place, normed_ref, pos_ref, cos_ref, sin_ref, mine_ref, other_ref,
    q_ref, k_ref, v_ref, p_ref, ctx_ref, w_scr,
):
    @pl.when(pl.program_id(0) == 0)
    def _():
        join(w_scr, mine_ref, other_ref, place[1], mine_ref.shape[1])

    project(normed_ref[0], w_scr, cos_ref[0], sin_ref[0], q_ref, k_ref, v_ref)
    attend(q_ref, k_ref, v_ref, p_ref, ctx_ref, pos_ref[0])


def attention_outs(s, rows, ext, cols):
    s.out(rows, cols)
    s.out(ext, cols)
    s.out(ext, cols)
    s.out(rows // LANES, cols // LANES, SPAN, 2 * LANES)
    s.out(rows, cols)


def split_units(units):
    return units // LANES * LANES, units % LANES


def flat(ref):
    return ref[...].reshape(-1, ref.shape[2])


def hidden_units(nf, cot, gate_w, up_w, down_w, count, here, act_s, gg_s, gu_s):
    def first(at):
        return mm(nf, gate_w[at], 1, 1), mm(nf, up_w[at], 1, 1), mm(cot, down_w[at], 1, 1)

    def mid(at, begun):
        g, u, ga = begun
        cdf = 0.5 * (1.0 + lax.erf(g * 0.5**0.5))
        gelu = g * cdf
        slope = cdf + g * jnp.exp(-0.5 * g * g) * 0.3989422804014327
        act_s[here, at] = (gelu * u).astype(BF)
        gg_s[here, at] = (ga * u * slope).astype(BF)
        gu_s[here, at] = (ga * gelu).astype(BF)

    step = 2 * LANES
    chunks = [(slice(c, min(c + step, count)),) for c in range(0, count, step)]
    in_turn(chunks, first, mid, lambda *_: None)


def ffn_own_kernel(
    block, place, x_ref, cot_ref, ctx0_ref, ctx1_ref, gain_ref, wo_ref, wi_ref, wd_ref,
    wo_mine, wo_other, state_ref, out_ref, grad_ref, keep_ref, send_ref,
    wo, nft, cott, gg_s, gu_s, act_s,
):
    m = pl.program_id(0)
    parity = place[1]
    steps = pl.num_programs(0) - 1
    main = gg_s.shape[1]
    group, rows, width = x_ref.shape
    rows = group * rows

    @pl.when(m == 0)
    def _():
        cols = wo_ref.shape[0]
        wo[:cols] = wo_ref[...]
        join(wo.at[cols:], wo_mine, wo_other, parity, cols // 2)

    @pl.when(m < steps)
    def _():
        here = pl.ds(pl.multiple_of(m * rows, 16), rows)
        along = pl.ds(pl.multiple_of(m * rows, LANES), rows)
        ctx = jnp.concatenate([flat(ctx0_ref), flat(ctx1_ref)], axis=1)
        state = flat(x_ref).astype(F32) + mm(ctx, wo[...], 1, 0)
        state_ref[...] = state.reshape(state_ref.shape)
        nf = (norm_parts(state)[0] * gain_ref[...]).astype(BF)
        transpose_into(nft, along, nf, block, parity)
        cot = flat(cot_ref)
        transpose_into(cott, along, cot, block, parity)
        hidden_units(nf, cot, wi_ref.at[0], wi_ref.at[1], wd_ref, main, here, act_s, gg_s, gu_s)
        out = mm(act_s[here, :], wd_ref[:main], 1, 0)
        out_ref[...] = out.astype(BF).reshape(out_ref.shape)
        grad = mm(gg_s[here, :], wi_ref[0, :main], 1, 0) + mm(gu_s[here, :], wi_ref[1, :main], 1, 0)
        grad_ref[...] = grad.astype(BF).reshape(grad_ref.shape)

    @pl.when(m == steps)
    def _():
        for j, to_ref in ((0, keep_ref), (1, send_ref)):
            at = slice(j * width // 2, (j + 1) * width // 2)
            for i, (at_ref, b_ref) in enumerate(((nft, gg_s), (nft, gu_s), (cott, act_s))):
                to_ref[:, i * main : (i + 1) * main] = mm(at_ref[at], b_ref[...], 1, 0).astype(BF)


def ffn_peer_kernel(
    block, place, state_ref, out_ref, grad_ref, cot_ref, ctx0_ref, ctx1_ref, gain_ref,
    wi_tail, wd_tail, mine_ref, other_ref, y_ref, mix_ref, gain_out, keep_ref, send_ref,
    half, gate_w, up_w, down_w, nft, cott, mixt, gg_s, gu_s, act_s, ctx_s,
):
    m = pl.program_id(0)
    parity = place[1]
    steps = pl.num_programs(0) - 1
    units = half.shape[0]
    main, rest = split_units(units)
    group, rows, width = state_ref.shape
    rows = group * rows

    @pl.when(m == 0)
    def _():
        for j, (full, own) in enumerate(
            ((gate_w, wi_tail.at[0]), (up_w, wi_tail.at[1]), (down_w, wd_tail))
        ):
            part = slice(j * (units // 2), (j + 1) * (units // 2))
            join(half, mine_ref.at[part], other_ref.at[part], parity, units // 2)
            full[:main] = half[:main]
            full[main : main + rest] = own[...]
            full[main + rest :] = half[main:]
        gain_out[...] = jnp.zeros_like(gain_out)

    @pl.when(m < steps)
    def _():
        here = pl.ds(pl.multiple_of(m * rows, 16), rows)
        along = pl.ds(pl.multiple_of(m * rows, LANES), rows)
        ctx_s[here, :] = jnp.concatenate([flat(ctx0_ref), flat(ctx1_ref)], axis=1)
        state = flat(state_ref)
        xhat, r = norm_parts(state)
        gain = gain_ref[...]
        nf = (xhat * gain).astype(BF)
        transpose_into(nft, along, nf, block, parity)
        cot = flat(cot_ref)
        transpose_into(cott, along, cot, block, parity)
        hidden_units(nf, cot, gate_w, up_w, down_w, main + 2 * rest, here, act_s, gg_s, gu_s)
        out = state + flat(out_ref).astype(F32) + mm(act_s[here, :], down_w[...], 1, 0)
        y_ref[...] = out.astype(BF).reshape(y_ref.shape)
        grad = flat(grad_ref).astype(F32) + mm(gg_s[here, :], gate_w[...], 1, 0)
        grad = grad + mm(gu_s[here, :], up_w[...], 1, 0)
        gain_out[...] += jnp.sum(grad * xhat, axis=0, keepdims=True)
        mix = (cot.astype(F32) + norm_back(xhat, r, grad * gain)).astype(BF)
        mix_ref[...] = mix.reshape(mix_ref.shape)
        transpose_into(mixt, along, mix, block, parity)

    @pl.when(m == steps)
    def _():
        cols = ctx0_ref.shape[2]
        own_at = 3 * main + cols + 4 * rest
        zero = jnp.zeros((width // 2, rest), BF)
        for j, to_ref in ((0, keep_ref), (1, send_ref)):
            at = slice(j * width // 2, (j + 1) * width // 2)
            ends = []
            for i, (at_ref, b_ref) in enumerate(((nft, gg_s), (nft, gu_s), (cott, act_s))):
                to = slice(i * main, (i + 1) * main)
                to_ref[:, to] = mm(at_ref[at], b_ref[:, :main], 1, 0).astype(BF)
                ends.append(mm(at_ref[at], b_ref[:, main:], 1, 0).astype(BF))
            out = mm(mixt[at], ctx_s[...], 1, 0).astype(BF)
            for out_at, out_cols, part in (
                (own_at, slice(0, cols), slice(0, rest)),
                (3 * main, slice(cols, 2 * cols), slice(rest, 2 * rest)),
            ):
                to_ref[:, out_at : out_at + cols] = out[:, out_cols]
                to_ref[:, out_at + cols : out_at + cols + 4 * rest] = jnp.concatenate(
                    [end[:, part] for end in ends] + [zero], axis=1
                )


def backward_kernel(peer, last, after, place, mix_ref, wo_ref, w_ref, *rest):
    rest = list(rest)
    if peer:
        wo_other, w_other = rest.pop(0), rest.pop(0)
    q_ref, k_ref, v_ref, p_ref, cos_ref, sin_ref = rest[:6]
    rest = rest[6:]
    if not peer:
        before_ref, normed_ref = rest.pop(0), rest.pop(0)
    gain_sums = None
    if last:
        at_ref, gm_before = rest.pop(0), rest.pop(0)
        if not peer:
            gain_sums = rest.pop(0), rest.pop(0), rest.pop(0)
    rest = rest[after:]
    nag_ref = rest.pop(0)
    if not peer:
        left_ref, right_ref, gain_out = rest.pop(0), rest.pop(0), rest.pop(0)
    if last:
        keep_ref, send_ref = rest.pop(0), rest.pop(0)
    else:
        gm_out = rest.pop(0)
    gm_ref = rest.pop(0)
    m = pl.program_id(0)
    if peer:
        wo_scr, w_scr = rest

        @pl.when(m == 0)
        def _():
            join(wo_scr, wo_ref, wo_other, place[1], wo_ref.shape[0])
            join(w_scr, w_ref, w_other, place[1], w_ref.shape[1])

        wo_ref, w_ref = wo_scr, w_scr
    rows, cols = q_ref.shape[1:]
    ext = k_ref.shape[1]
    own = slice(REACH, REACH + rows)

    def one_batch():
        dctx = mm(mix_ref[0], wo_ref[...], 1, 1).astype(BF)
        cos, sin = cos_ref[0], sin_ref[0]
        gm_ref[m, :REACH, :cols] = jnp.zeros((REACH, cols), BF)
        gm_ref[m, REACH + rows :, :cols] = jnp.zeros((REACH, cols), BF)
        blocks = rows // LANES
        key_parts, value_parts = {}, {}

        def first(b, p):
            here, span, at = places(b, p)
            grad = both_heads(dctx[here, at])
            return grad, mm(v_ref[0, span, at], grad, 1, 1)

        def mid(b, p, begun):
            probs = p_ref[0, b, p].astype(F32)
            weighted = probs * begun[1]
            balance = jnp.sum(weighted, axis=0, keepdims=True)
            return (weighted - probs * balance).astype(BF)

        def over_blocks(parts, p):
            out = []
            for b in range(blocks + 1):
                piece = None
                if b < blocks:
                    piece = parts[b, p][:LANES]
                if b > 0:
                    more = parts[b - 1, p][LANES:]
                    piece = more if piece is None else piece + more
                out.append(piece)
            return jnp.concatenate(out, axis=0)

        def end(b, p, begun, grad_scores):
            here, span, at = places(b, p)
            there = slice(b * LANES + REACH, (b + 1) * LANES + REACH)
            value_parts[b, p] = mm(p_ref[0, b, p], begun[0], 1, 0)
            key_parts[b, p] = mm(grad_scores, both_heads(q_ref[0, here, at]), 1, 0)
            dq = one_row_each(mm(grad_scores, k_ref[0, span, at], 0, 0)) * SCALE
            gm_ref[m, there, at] = (dq * cos[there] - turned(dq) * sin[there]).astype(BF)
            if b == blocks - 1:
                dk = over_blocks(key_parts, p)
                gm_ref[m, :, cols + p * LANES : cols + (p + 1) * LANES] = (
                    dk * cos - turned(dk) * sin
                ).astype(BF)
                dv = over_blocks(value_parts, p).astype(BF)
                gm_ref[m, :, 2 * cols + p * LANES : 2 * cols + (p + 1) * LANES] = dv

        units = [(b, p) for p in range(cols // LANES) for b in range(blocks)]
        in_turn(units, first, mid, end)
        nag = mm(gm_ref[m, :, cols : 2 * cols], w_ref[1], 1, 1)
        nag = nag + mm(gm_ref[m, :, 2 * cols :], w_ref[2], 1, 1)
        nag_q = mm(gm_ref[m, own, :cols], w_ref[0], 1, 1)
        if peer:
            nag_ref[0, :REACH] = nag[:REACH].astype(BF)
            nag_ref[0, own] = (nag[own] + nag_q).astype(BF)
            nag_ref[0, REACH + rows :] = nag[REACH + rows :].astype(BF)
        else:
            nag = nag + before_ref[0].astype(F32)
            left_ref[0] = nag[:REACH].astype(BF)
            right_ref[0] = nag[REACH + rows :].astype(BF)
            nag_own = nag[own] + nag_q
            nag_ref[0] = nag_own.astype(BF)
            normed = normed_ref[0].astype(F32)
            total = (
                jnp.sum(nag[:REACH] * normed[:REACH], axis=0, keepdims=True)
                + jnp.sum(nag_own * normed[own], axis=0, keepdims=True)
                + jnp.sum(nag[REACH + rows :] * normed[REACH + rows :], axis=0, keepdims=True)
            )

            @pl.when(m == 0)
            def _():
                gain_out[...] = total

            @pl.when(m > 0)
            def _():
                gain_out[...] += total

        if not last:
            gm_out[0] = gm_ref[m]

    if not last:
        one_batch()
        return
    steps = pl.num_programs(0) - 1
    pl.when(m < steps)(one_batch)

    @pl.when(m == steps)
    def _():
        half, earlier = at_ref.shape[0] // 2, gm_before.shape[0] * ext
        one = gm_before[...].reshape(earlier, 3 * cols)
        two = gm_ref[...].reshape(-1, 3 * cols)
        for j, to in ((0, keep_ref), (1, send_ref)):
            at = slice(j * half, (j + 1) * half)
            total = mm(at_ref[at, :earlier], one, 1, 0) + mm(at_ref[at, earlier:], two, 1, 0)
            to[:half] = total.astype(BF)
            if gain_sums is not None:
                gain_ref, attn_ref, ffn_ref = gain_sums
                width = gain_ref.shape[1]
                attn = (attn_ref[...] + gain_out[...]) / gain_ref[...]
                zero = jnp.zeros((MORE - 2, width), F32)
                gains = jnp.concatenate([attn, ffn_ref[...], zero], axis=0)
                to[half:, :width] = gains.astype(BF)
                to[half:, width:] = jnp.zeros((MORE, to.shape[1] - width), BF)


def last_kernel(place, x_ref, nag_ref, before_ref, after_ref, mix_ref, gain_ref, *rest):
    out_ref = rest[-1]
    rows = nag_ref.shape[1]
    gain = gain_ref[...]
    step = 32
    for c in range(0, rows, step):
        at = slice(c, c + step)
        xhat, r = norm_parts(x_ref[0, at].astype(F32))
        nag = nag_ref[0, at].astype(F32)
        if c < REACH:
            nag = nag + before_ref[0, at].astype(F32)
        if c >= rows - REACH:
            nag = nag + after_ref[0, c - rows + REACH : c - rows + REACH + step].astype(F32)
        out_ref[0, at] = mix_ref[0, at].astype(F32) + norm_back(xhat, r, nag * gain)


def swap(x, axis, bit):
    size = lax.axis_size(axis)
    return lax.ppermute(x, axis, [(i, i ^ bit) for i in range(size)])


def then(value, *earlier):
    return lax.optimization_barrier((value, *earlier))[0]


def quarter(half, axis):
    rows = half.shape[axis] // 2
    return lax.dynamic_slice_in_dim(half, (lax.axis_index("dp") % 2) * rows, rows, axis)


class Halving:
    def __init__(self, total, rows, bit, beside=None):
        self.mine = (lax.axis_index("dp") // bit) % 2
        self.g = total.astype(BF).reshape(-1, 2, rows, total.shape[-1])
        self.sent = lax.dynamic_index_in_dim(self.g, 1 - self.mine, 1, keepdims=False)
        self.beside = beside
        if beside is not None:
            self.sent = jnp.concatenate([self.sent.reshape(-1, total.shape[-1]), beside])
        self.got = swap(self.sent, "dp", bit)

    def total(self, *earlier):
        keep = lax.dynamic_index_in_dim(self.g, self.mine, 1, keepdims=False)
        got = then(self.got, *earlier).astype(F32)
        if self.beside is None:
            total = keep.astype(F32) + got
            return total.reshape(-1, total.shape[-1])
        keep = keep.astype(F32).reshape(-1, got.shape[-1])
        return keep + got[:-MORE], self.beside.astype(F32) + got[-MORE:]


def sum_from(total, rows, bit, size):
    while bit < size:
        total = Halving(total, rows, bit).total()
        bit *= 2
    return total


def sorted_halves(keep, send, block, size):
    if block is not None:
        return keep, send
    n, half, cols = keep.shape
    g = jnp.concatenate([keep, send], axis=1).reshape(n, size // 2, 2, 2 * half // size, cols)
    parity = lax.axis_index("dp") % 2
    keep = lax.dynamic_index_in_dim(g, parity, 2, keepdims=False)
    send = lax.dynamic_index_in_dim(g, 1 - parity, 2, keepdims=False)
    return keep.reshape(n, half, cols), send.reshape(n, half, cols)


def on_device(
    inputs, positions, cotangent, gain_attn, gain_ffn, w_qkv, w_out, w_in, down_projection_weight
):
    batches, row_count, width = inputs.shape
    parts, t = lax.axis_size("tensor"), lax.axis_index("tensor")
    dp = lax.axis_size("dp")
    rows = row_count // parts
    ext = rows + 2 * REACH
    cols = w_qkv.shape[2]
    units = w_in.shape[2]
    place = jnp.stack([t, lax.axis_index("dp") % 2]).astype(jnp.int32)
    mine = width // dp
    block = mine if mine % 16 == 0 else None

    digits = jnp.concatenate([positions // DIGIT, positions % DIGIT], axis=1).astype(BF)
    digits = digits.reshape(batches, 2, row_count)
    edges = [
        jnp.concatenate(
            [
                lax.slice_in_dim(inputs, at, at + REACH, axis=1),
                jnp.broadcast_to(
                    jnp.pad(
                        lax.slice_in_dim(digits, at, at + REACH, axis=2).reshape(batches, 1, -1),
                        ((0, 0), (0, 0), (0, width - 2 * REACH)),
                    ),
                    (batches, 16, width),
                ),
            ],
            axis=1,
        )
        for at in (row_count - REACH, 0)
    ]
    perm = [(2 * i, 2 * i + 2) for i in range(dp - 1)]
    perm += [(2 * i + 3, 2 * i + 1) for i in range(dp - 1)]
    x_outer = lax.ppermute(jnp.where(t == 0, *edges), ("dp", "tensor"), perm)

    qkv = w_qkv.transpose(1, 0, 2)
    w_in = w_in.transpose(1, 2, 0)
    w_down = down_projection_weight
    qkv_mine = swap(quarter(qkv, 1), "tensor", 1)
    freq = jnp.asarray(
        np.power(
            np.float32(rope_base),
            -np.arange(HEAD_DIM // 2, dtype=np.float32) * np.float32(2.0 / HEAD_DIM),
        )[:, None]
    )

    work = 2 * batches * ext * width * 3 * cols + 8 * batches * rows * cols * SPAN
    s = Specs(batches)
    s.per(inputs)
    s.per(x_outer)
    s.per(positions[:, None, :])
    s.whole(gain_attn[None, :], qkv, freq)
    out_mine = quarter(w_out, 0)
    rest_mine = jnp.concatenate([quarter(w_in, 1).reshape(units, width), quarter(w_down, 0)])
    s.after(out_mine, rest_mine)
    s.out(ext, width)
    s.out_columns(width, ext)
    s.out(1, ext, dtype=jnp.int32)
    s.out(ext, LANES, dtype=F32)
    s.out(ext, LANES, dtype=F32)
    attention_outs(s, rows, ext, cols)
    normed, normed_t, pos_ext, cos, sin, q0, k0, v0, p0, ctx0 = s.call(
        functools.partial(forward_own, block), place, "attn_fwd_own",
        scratch=[pltpu.VMEM((ext, width), BF)], flops=work, moved=20 * batches * ext * width,
    )

    out_mine = swap(then(out_mine, ctx0), "tensor", 1)
    rest_mine = swap(then(rest_mine, ctx0), "tensor", 1)
    qkv_other = swap(then(qkv_mine, ctx0), "dp", 1)
    s = Specs(batches)
    for a in (normed, pos_ext, cos, sin):
        s.per(a)
    s.whole(qkv_mine, qkv_other)
    attention_outs(s, rows, ext, cols)
    q1, k1, v1, p1, ctx1 = s.call(
        forward_peer, place, "attn_fwd_peer",
        scratch=[pltpu.VMEM((3, width, cols), BF)], flops=work, moved=20 * batches * ext * cols,
    )
    out_other = swap(then(out_mine, ctx1), "dp", 1)

    own_block = (rows, width)
    group = 2 if batches % 2 == 0 else 1
    main, rest = split_units(units)
    in_cols = 2 * main
    own_place = lambda place: (place[0], 0)
    s = Specs(batches, group)
    s.per(inputs, own_block, own_place)
    s.per(cotangent, own_block, own_place)
    s.per(ctx0)
    s.per(ctx1)
    s.whole(gain_ffn[None, :], w_out)
    s.ins.append(pl.BlockSpec((2, main, width), lambda m, place: (0, 0, 0)))
    s.ins.append(pl.BlockSpec((main, width), lambda m, place: (0, 0)))
    s.args += [w_in, w_down]
    s.whole(out_mine, out_other)
    s.out(rows, width, dtype=F32)
    s.out(rows, width)
    s.out(rows, width)
    for _ in range(2):
        s.out_whole(width // 2, 3 * main)
    state, part_out, part_grad, keep, send = s.call(
        functools.partial(ffn_own_kernel, block), place, "ffn_own", steps=s.batches + 1,
        scratch=[pltpu.VMEM((2 * cols, width), BF)]
        + [pltpu.VMEM((width, batches * rows), BF)] * 2
        + [pltpu.VMEM((batches * rows, main), BF)] * 3,
        flops=2 * batches * rows * width * (9 * main + 2 * cols), moved=3 * 10**7,
    )
    own_keep, send = sorted_halves(keep[None], send[None], block, dp)
    own_got = swap(send[0], "dp", 1)
    rest_other = swap(then(rest_mine, state), "dp", 1)

    s = Specs(batches, group)
    for a in (state, part_out, part_grad):
        s.per(a)
    s.per(cotangent, own_block, own_place)
    s.per(ctx0)
    s.per(ctx1)
    s.whole(gain_ffn[None, :])
    s.ins.append(pl.BlockSpec((2, rest, width), lambda m, place: (0, main // rest, 0)))
    s.ins.append(pl.BlockSpec((rest, width), lambda m, place: (main // rest, 0)))
    s.args += [w_in, w_down]
    s.whole(rest_mine, rest_other)
    s.out(rows, width)
    s.out(rows, width)
    s.out_whole(1, width, dtype=F32)
    for _ in range(2):
        s.out_whole(width // 2, 3 * main + 2 * (cols + 4 * rest))
    y, mix, gain_ffn_part, keep, send = s.call(
        functools.partial(ffn_peer_kernel, block), place, "ffn_peer", steps=s.batches + 1,
        scratch=[pltpu.VMEM((units, width), BF)]
        + [pltpu.VMEM((main + 2 * rest, width), BF)] * 3
        + [pltpu.VMEM((width, batches * rows), BF)] * 3
        + [pltpu.VMEM((batches * rows, main + 2 * rest), BF)] * 3
        + [pltpu.VMEM((batches * rows, 2 * cols), BF)],
        flops=2 * batches * rows * width * (9 * (main + 2 * rest) + 2 * cols), moved=4 * 10**7,
    )
    keep, send = sorted_halves(keep[None], send[None], block, dp)
    got = swap(send[0], "dp", 1)

    def backward(peer, saved, start, stop, nag1, gm_before, after, name, gain_sums=()):
        last, part = gm_before is not None, stop - start
        s = Specs(part)
        s.per(mix, start=start)
        if peer:
            s.whole(out_mine, qkv_mine, out_other, qkv_other)
        else:
            s.whole(w_out, qkv)
        for a in (*saved, cos, sin):
            s.per(a, start=start)
        if not peer:
            s.per(nag1, start=start)
            s.per(normed, start=start)
        more = 0
        if last:
            s.whole(normed_t, gm_before)
            if gain_sums:
                s.whole(*gain_sums)
                more = MORE
        s.after(*after)
        scratch = [pltpu.VMEM((part, ext, 3 * cols), BF)]
        alias = None
        if peer:
            if nag1 is not None:
                s.after(nag1)
                after += (nag1,)
                alias = {len(s.args): 0}
            s.out_part(batches, start, ext, width)
            scratch += [pltpu.VMEM((cols, width), BF), pltpu.VMEM((3, width, cols), BF)]
        else:
            s.out(rows, width)
            s.out(REACH, width)
            s.out(REACH, width)
            s.out_whole(1, width, dtype=F32)
        if last:
            s.out_whole(width // 2 + more, 3 * cols)
            s.out_whole(width // 2 + more, 3 * cols)
        else:
            s.out(ext, 3 * cols)
        return s.call(
            functools.partial(backward_kernel, peer, last, len(after)),
            place, name, steps=part + 1 if last else None, scratch=scratch, alias=alias,
            flops=(2 * ext * width * 4 * cols + 20 * rows * cols * SPAN) * part,
            moved=30 * part * ext * cols,
        )

    def halos(to_before, to_after):
        devices = dp * parts
        up = [(i, i + 1) for i in range(devices - 1)]
        down = [(i + 1, i) for i in range(devices - 1)]
        return (
            lax.ppermute(to_after, ("dp", "tensor"), up),
            lax.ppermute(to_before, ("dp", "tensor"), down),
        )

    saved0, saved1 = (q0, k0, v0, p0), (q1, k1, v1, p1)
    nag1, gm1a = backward(True, saved1, 0, 1, None, None, (), "attn_bwd_peer_a")
    got, own_got = then(got, gm1a), then(own_got, gm1a)

    def cores(keep, got, *at):
        at = slice(*at)
        return (keep[0, :, at].astype(F32) + got[:, at].astype(F32)).astype(BF)

    own_at = 3 * main + cols + 4 * rest
    a_peer = cores(keep, got, 0, in_cols)
    a_from_peer = swap(a_peer, "tensor", 1)
    b_own = [cores(own_keep, own_got, in_cols, None), cores(keep, got, own_at, None)]
    b_peer = cores(keep, got, in_cols, own_at)
    b_sum = Halving(jnp.concatenate([jnp.concatenate(b_own, axis=1), b_peer]), mine, 2)
    nag1, keep1, send1 = backward(
        True, saved1, 1, batches, nag1, gm1a, (a_peer, b_sum.sent), "attn_bwd_peer_b"
    )
    keep1, send1 = sorted_halves(keep1[None], send1[None], block, dp)
    got1 = swap(send1[0], "dp", 1)
    a_own = cores(own_keep, own_got, 0, in_cols).astype(F32)
    a_sum = Halving(a_own + then(a_from_peer, send1).astype(F32), mine, 2)
    b_sum = b_sum.total(send1).reshape(2, width // 4, -1)
    b_peer = b_sum[1].astype(BF)
    b_from_peer = swap(b_peer, "tensor", 1)
    part = batches // 2
    nag_a, to_before, to_after, gain_a, gm0a = backward(
        False, saved0, 0, part, nag1, None, (send1, a_sum.sent, b_peer), "attn_bwd_own_a"
    )
    halos_a = halos(to_before, to_after)
    qkv_peer = (keep1[0].astype(F32) + then(got1, gm0a).astype(F32)).astype(BF)
    qkv_from_peer = swap(qkv_peer, "tensor", 1)
    b_sum = b_sum[0] + then(b_from_peer, gm0a).astype(F32)
    f_sum = Halving(jnp.concatenate([a_sum.total(gm0a), b_sum], axis=1), mine, 4)
    nag_b, to_before, to_after, _, keep0, send0 = backward(
        False, saved0, part, batches, nag1, gm0a, (qkv_peer, f_sum.sent), "attn_bwd_own_b",
        (gain_attn[None, :], gain_a, gain_ffn_part),
    )
    beside = keep0[width // 2 :]
    keep0, sorted0 = sorted_halves(
        keep0[None, : width // 2], send0[None, : width // 2], block, dp
    )
    if block is None:
        send0 = jnp.concatenate([sorted0[0], beside])
    got0 = swap(send0, "dp", 1)
    halos_b = halos(to_before, to_after)
    f_sum = Halving(f_sum.total(send0), mine, 8)

    def finish(nag, halos, start, after, into, name):
        s = Specs(part)
        s.per(inputs, own_block, own_place, start=start)
        for a in (nag, *halos):
            s.per(a)
        s.per(mix, start=start)
        s.whole(gain_attn[None, :])
        s.after(*after)
        if into is not None:
            s.after(into)
        s.outs.append(pl.BlockSpec((1, rows, width), lambda m, place: (m + start, 0, 0)))
        s.shapes.append(jax.ShapeDtypeStruct((batches, rows, width), F32))
        return s.call(
            last_kernel, place, name, flops=10**7, moved=8 * part * rows * width,
            alias=None if into is None else {len(s.args): 0},
        )[0]

    input_grad = finish(nag_a, halos_a, 0, (send0, f_sum.sent), None, "input_grad_a")
    got0, qkv_from_peer = then(got0, input_grad), then(qkv_from_peer, input_grad)
    got0, gains = got0[: width // 2].astype(F32), got0[width // 2 :].astype(F32)
    gains = (beside.astype(F32) + gains).astype(BF)
    qkv_sum = keep0[0].astype(F32) + got0 + qkv_from_peer.astype(F32)
    qkv_sum = Halving(qkv_sum, mine, 2, gains)
    input_grad = finish(nag_b, halos_b, part, (qkv_sum.sent,), input_grad, "input_grad_b")
    f_sum = sum_from(f_sum.total(input_grad), mine, 16, dp)
    bit = 4
    while bit < dp:
        total, gains = qkv_sum.total(input_grad)
        gains = gains.astype(BF)
        qkv_sum = Halving(total, mine, bit, gains)
        bit *= 2
    gains = gains[:, :width]
    peer = swap(gains, "tensor", 1).astype(F32)
    index = [2 * i + j for i in range(dp) for j in range(2)]
    both = lax.ppermute(gains, ("dp", "tensor"), [(i, (i ^ 1) ^ dp) for i in index])
    qkv_sum, gains = qkv_sum.total(input_grad)
    gains = gains[:, :width] + (peer + both.astype(F32))
    qkv_sum = qkv_sum.reshape(mine, 3, cols)

    def unit_columns(j):
        tail = 3 * main + cols + j * rest
        return jnp.concatenate(
            [f_sum[:, j * main : (j + 1) * main], f_sum[:, tail : tail + rest]], axis=1
        )

    return (
        y,
        input_grad,
        qkv_sum,
        f_sum[:, 3 * main : 3 * main + cols].T,
        jnp.stack([unit_columns(0), unit_columns(1)], axis=1),
        unit_columns(2).T,
        gains[0],
        gains[1],
    )


def solution(mesh):
    placed = (
        P(None, "dp", None),
        P(None, "dp"),
        P(None, "dp", None),
        P(),
        P(),
        P(None, None, "tensor"),
        P("tensor", None),
        P(None, None, "tensor"),
        P("tensor", None),
    )
    return jax.shard_map(
        on_device,
        mesh=mesh,
        in_specs=placed,
        out_specs=(
            P(None, ("dp", "tensor"), None),
            P(None, ("dp", "tensor"), None),
            P("dp", None, "tensor"),
            P("tensor", "dp"),
            P("dp", None, "tensor"),
            P("tensor", "dp"),
            P(),
            P(),
        ),
        check_vma=False,
    )
```

```python
import functools

import jax
import jax.numpy as jnp
import numpy as np
from jax import lax
from jax.experimental import pallas as pl
from jax.experimental.pallas import tpu as pltpu
from jax.sharding import PartitionSpec as P

HEAD_DIM = 64
WINDOW = 128
REACH = WINDOW // 2
LANES = 128
SPAN = LANES + 2 * REACH
SCALE = HEAD_DIM**-0.5
DIGIT = 64
MORE = 16

norm_eps = 1e-05
rope_base = 10000.0
masked_score = -1e30

BF = jnp.bfloat16
F32 = jnp.float32
VMEM_BYTES = 60 * 2**20


def mm(a, b, ca, cb):
    return lax.dot_general(a, b, (((ca,), (cb,)), ((), ())), preferred_element_type=F32)


def turned(v):
    lane = lax.broadcasted_iota(jnp.int32, v.shape, 1)
    low = (lane & 63) < 32
    return jnp.where(low, pltpu.roll(v, 96, 1), pltpu.roll(v, 32, 1))


def both_heads(v):
    lane = lax.broadcasted_iota(jnp.int32, v.shape, 1)
    zero = jnp.zeros_like(v)
    return jnp.concatenate(
        [jnp.where(lane < HEAD_DIM, v, zero), jnp.where(lane >= HEAD_DIM, v, zero)], axis=0
    )


def one_row_each(v):
    rows = v.shape[0] // 2
    lane = lax.broadcasted_iota(jnp.int32, (rows, v.shape[1]), 1)
    return jnp.where(lane < HEAD_DIM, v[:rows], v[rows:])


def norm_parts(v):
    centred = v - jnp.mean(v, axis=1, keepdims=True)
    spread = jnp.mean(centred * centred, axis=1, keepdims=True)
    r = lax.rsqrt(spread + norm_eps)
    return centred * r, r


def norm_back(xhat, r, e):
    return r * (
        e - jnp.mean(e, axis=1, keepdims=True) - xhat * jnp.mean(e * xhat, axis=1, keepdims=True)
    )


def transpose_into(at_ref, at, v, block, parity):
    vt = v.T
    width = vt.shape[0]
    if block is None:
        at_ref[:, at] = vt
        return
    for i in range(width // block):
        odd = parity if i % 2 == 0 else 1 - parity
        to = pl.multiple_of((i // 2) * block + odd * (width // 2), 16)
        at_ref[pl.ds(to, block), at] = vt[i * block : (i + 1) * block]


def join(own_ref, mine_ref, other_ref, parity, rows):
    own_ref[..., pl.ds(pl.multiple_of(parity * rows, 16), rows), :] = mine_ref[...]
    own_ref[..., pl.ds(pl.multiple_of((1 - parity) * rows, 16), rows), :] = other_ref[...]


def join_out(own_ref, mine_ref, other_ref, parity):
    rows = mine_ref.shape[0] // 2
    for ref, place in ((mine_ref, parity), (other_ref, 1 - parity)):
        at = pl.ds(pl.multiple_of(place * rows, 16), rows)
        own_ref[at, : 2 * rows] = ref[:rows]
        own_ref[at, 2 * rows :] = ref[rows:]


class Specs:
    def __init__(self, batches, group=1):
        self.batches = batches // group
        self.group = group
        self.ins, self.args, self.outs, self.shapes = [], [], [], []

    def per(self, a, block=None, at=None, start=0):
        block = (self.group,) + (a.shape[1:] if block is None else block)
        last = self.batches - 1

        def index(m, place):
            m = jnp.minimum(m, last)
            rest = (0,) * (len(block) - 1) if at is None else at(place)
            return (m + start,) + rest

        self.ins.append(pl.BlockSpec(block, index))
        self.args.append(a)

    def whole(self, *arrays):
        for a in arrays:
            self.ins.append(
                pl.BlockSpec(
                    a.shape, lambda m, place, n=a.ndim: (0,) * n, pipeline_mode=pl.Buffered(1)
                )
            )
            self.args.append(a)

    def after(self, *arrays):
        for a in arrays:
            self.ins.append(pl.BlockSpec(memory_space=pl.ANY))
            self.args.append(a)

    def out_part(self, batches, start, *dims, dtype=BF):
        last = self.batches - 1
        n = len(dims)
        self.outs.append(
            pl.BlockSpec(
                (1,) + dims, lambda m, place: (jnp.minimum(m, last) + start,) + (0,) * n
            )
        )
        self.shapes.append(jax.ShapeDtypeStruct((batches,) + dims, dtype))

    def out(self, *dims, dtype=BF):
        last = self.batches - 1
        n = len(dims)
        self.outs.append(
            pl.BlockSpec(
                (self.group,) + dims, lambda m, place: (jnp.minimum(m, last),) + (0,) * n
            )
        )
        self.shapes.append(jax.ShapeDtypeStruct((self.batches * self.group,) + dims, dtype))

    def out_columns(self, rows, cols, dtype=BF):
        last = self.batches - 1
        self.outs.append(pl.BlockSpec((rows, cols), lambda m, place: (0, jnp.minimum(m, last))))
        self.shapes.append(jax.ShapeDtypeStruct((rows, self.batches * cols), dtype))

    def out_any(self, *dims, dtype=BF):
        self.outs.append(pl.BlockSpec(memory_space=pl.ANY))
        self.shapes.append(jax.ShapeDtypeStruct(dims, dtype))

    def out_whole(self, *dims, dtype=BF):
        self.outs.append(
            pl.BlockSpec(
                dims, lambda m, place: (0,) * len(dims), pipeline_mode=pl.Buffered(1)
            )
        )
        self.shapes.append(jax.ShapeDtypeStruct(dims, dtype))

    def call(self, kernel, place, name, steps=None, scratch=(), flops=0, moved=0, alias=None):
        return pl.pallas_call(
            kernel,
            grid_spec=pltpu.PrefetchScalarGridSpec(
                num_scalar_prefetch=1,
                grid=(self.batches if steps is None else steps,),
                in_specs=self.ins,
                out_specs=self.outs,
                scratch_shapes=list(scratch),
            ),
            out_shape=self.shapes,
            input_output_aliases={} if alias is None else alias,
            compiler_params=pltpu.CompilerParams(vmem_limit_bytes=VMEM_BYTES),
            cost_estimate=pl.CostEstimate(
                flops=flops // 10, bytes_accessed=moved // 10, transcendentals=0
            ),
            name=name,
        )(place, *self.args)


def in_turn(units, first, mid, last):
    begun, middle, n = {}, {}, len(units)
    for i in range(-1, n + 1):
        if i + 1 < n:
            begun[i + 1] = first(*units[i + 1])
        if i >= 1:
            last(*units[i - 1], begun.pop(i - 1), middle.pop(i - 1))
        if 0 <= i < n:
            middle[i] = mid(*units[i], begun[i])


def places(b, p):
    here = slice(b * LANES, (b + 1) * LANES)
    return here, slice(b * LANES, b * LANES + SPAN), slice(p * LANES, (p + 1) * LANES)


def attend(q_ref, k_ref, v_ref, p_ref, ctx_ref, pos_row):
    rows, cols = q_ref.shape[1:]
    pos_col = jnp.broadcast_to(pos_row, (LANES, pos_row.shape[1])).T
    biases = []
    for b in range(rows // LANES):
        rel = (
            lax.broadcasted_iota(jnp.int32, (SPAN, LANES), 0)
            - REACH
            - lax.broadcasted_iota(jnp.int32, (SPAN, LANES), 1)
        )
        q_pos = pos_row[:, b * LANES + REACH : (b + 1) * LANES + REACH]
        since = jnp.where(rel > 0, pos_col[b * LANES : b * LANES + SPAN], q_pos)
        far = jnp.abs(rel)
        bias = jnp.where((far <= REACH) & (since >= far), 0.0, masked_score).astype(F32)
        biases.append(jnp.concatenate([bias, bias], axis=1))

    def first(b, p):
        here, span, at = places(b, p)
        return mm(k_ref[0, span, at], both_heads(q_ref[0, here, at]), 1, 1)

    def mid(b, p, scores):
        scores = scores + biases[b]
        e = jnp.exp(scores - jnp.max(scores, axis=0, keepdims=True))
        probs = (e * (1.0 / jnp.sum(e, axis=0, keepdims=True))).astype(BF)
        p_ref[0, b, p] = probs
        return probs

    def last(b, p, _, probs):
        here, span, at = places(b, p)
        ctx_ref[0, here, at] = one_row_each(mm(probs, v_ref[0, span, at], 0, 0)).astype(BF)

    units = [(b, p) for b in range(rows // LANES) for p in range(cols // LANES)]
    in_turn(units, first, mid, last)


def project(normed, w_ref, cos, sin, q_ref, k_ref, v_ref):
    rows, cols = q_ref.shape[1:]
    own = slice(REACH, REACH + rows)
    mixed_q = mm(normed[own], w_ref[0], 1, 0)
    mixed_k = mm(normed, w_ref[1], 1, 0)
    v_ref[0] = mm(normed, w_ref[2], 1, 0).astype(BF)
    for p in range(cols // LANES):
        at = slice(p * LANES, (p + 1) * LANES)
        mq, mk = mixed_q[:, at], mixed_k[:, at]
        q_ref[0, :, at] = (mq * cos[own] + turned(mq) * sin[own]).astype(BF) * SCALE
        k_ref[0, :, at] = (mk * cos + turned(mk) * sin).astype(BF)


def forward_own(
    block, place, x_ref, outer_ref, pos_ref, gain_ref, w_ref, freq_ref, wi_ref, wd_ref,
    normed_ref, at_ref, pos_out_ref, cos_ref, sin_ref, rest_ref,
    q_ref, k_ref, v_ref, p_ref, ctx_ref, x_scr, half_scr, sems,
):
    t, parity = place[0], place[1]
    more = wi_ref.shape[1] // 2
    part = pl.ds(pl.multiple_of(parity * more, 16), more)
    sources = [wi_ref.at[0, part], wi_ref.at[1, part], wd_ref.at[part]]
    held = [half_scr.at[i * more : (i + 1) * more] for i in range(3)]
    targets = [rest_ref.at[i * more : (i + 1) * more] for i in range(3)]
    reads = [pltpu.make_async_copy(a, b, sems.at[i]) for i, (a, b) in enumerate(zip(sources, held))]
    writes = [
        pltpu.make_async_copy(a, b, sems.at[3 + i]) for i, (a, b) in enumerate(zip(held, targets))
    ]
    m = pl.program_id(0)

    @pl.when(m == 0)
    def _():
        for copy in reads:
            copy.start()

    @pl.when(m == 1)
    def _():
        for copy in reads:
            copy.wait()
        for copy in writes:
            copy.start()

    @pl.when(m == pl.num_programs(0) - 1)
    def _():
        for copy in writes:
            copy.wait()

    rows, ext = q_ref.shape[1], k_ref.shape[1]
    inner = rows + REACH
    x_scr[pl.ds(pl.multiple_of((1 - t) * REACH, 16), inner), :] = x_ref[
        0, pl.ds(pl.multiple_of(t * (rows - REACH), 16), inner), :
    ]
    x_scr[pl.ds(pl.multiple_of(t * inner, 16), REACH), :] = outer_ref[0, :REACH]
    pos = pos_ref[0]
    digits = outer_ref[0, REACH:].astype(F32)[:1, : 2 * REACH]
    pos_outer = (digits[:, :REACH] * DIGIT + digits[:, REACH:]).astype(jnp.int32)
    pos_row = jnp.where(
        t == 0,
        jnp.concatenate([pos_outer, pos[:, :inner]], axis=1),
        jnp.concatenate([pos[:, rows - REACH :], pos_outer], axis=1),
    )
    pos_out_ref[0] = pos_row
    xhat, _ = norm_parts(x_scr[...].astype(F32))
    normed = (xhat * gain_ref[...]).astype(BF)
    normed_ref[0] = normed
    transpose_into(at_ref, slice(None), normed, block, parity)
    angles = freq_ref[...] * pos_row.astype(F32)
    c, s = jnp.cos(angles), jnp.sin(angles)
    cos = jnp.concatenate([c, c, c, c], axis=0).T
    sin = jnp.concatenate([-s, s, -s, s], axis=0).T
    cos_ref[0] = cos
    sin_ref[0] = sin
    project(normed, w_ref, cos, sin, q_ref, k_ref, v_ref)
    attend(q_ref, k_ref, v_ref, p_ref, ctx_ref, pos_row)


def forward_peer(
    place, normed_ref, pos_ref, cos_ref, sin_ref, mine_ref, other_ref,
    q_ref, k_ref, v_ref, p_ref, ctx_ref, w_scr,
):
    @pl.when(pl.program_id(0) == 0)
    def _():
        join(w_scr, mine_ref.at[:3], other_ref.at[:3], place[1], mine_ref.shape[1])

    project(normed_ref[0], w_scr, cos_ref[0], sin_ref[0], q_ref, k_ref, v_ref)
    attend(q_ref, k_ref, v_ref, p_ref, ctx_ref, pos_ref[0])


def attention_outs(s, rows, ext, cols):
    s.out(rows, cols)
    s.out(ext, cols)
    s.out(ext, cols)
    s.out(rows // LANES, cols // LANES, SPAN, 2 * LANES)
    s.out(rows, cols)


def split_units(units):
    return units // LANES * LANES, units % LANES


def flat(ref):
    return ref[...].reshape(-1, ref.shape[2])


def hidden_units(nf, cot, gate_w, up_w, down_w, count, here, act_s, gg_s, gu_s):
    def first(at):
        return mm(nf, gate_w[at], 1, 1), mm(nf, up_w[at], 1, 1), mm(cot, down_w[at], 1, 1)

    def mid(at, begun):
        g, u, ga = begun
        cdf = 0.5 * (1.0 + lax.erf(g * 0.5**0.5))
        gelu = g * cdf
        slope = cdf + g * jnp.exp(-0.5 * g * g) * 0.3989422804014327
        act_s[here, at] = (gelu * u).astype(BF)
        gg_s[here, at] = (ga * u * slope).astype(BF)
        gu_s[here, at] = (ga * gelu).astype(BF)

    step = 2 * LANES
    chunks = [(slice(c, min(c + step, count)),) for c in range(0, count, step)]
    in_turn(chunks, first, mid, lambda *_: None)


def ffn_own_kernel(
    block, place, x_ref, cot_ref, ctx0_ref, ctx1_ref, gain_ref, wo_ref, wi_ref, wd_ref,
    wo_mine, wo_other, state_ref, out_ref, grad_ref, keep_ref, send_ref,
    wo, nft, cott, gg_s, gu_s, act_s,
):
    m = pl.program_id(0)
    parity = place[1]
    steps = pl.num_programs(0) - 1
    main = gg_s.shape[1]
    group, rows, width = x_ref.shape
    rows = group * rows

    @pl.when(m == 0)
    def _():
        cols = wo_ref.shape[0]
        wo[:cols] = wo_ref[...]
        join_out(wo.at[cols:], wo_mine.at[0], wo_other.at[0], parity)

    @pl.when(m < steps)
    def _():
        here = pl.ds(pl.multiple_of(m * rows, 16), rows)
        along = pl.ds(pl.multiple_of(m * rows, LANES), rows)
        ctx = jnp.concatenate([flat(ctx0_ref), flat(ctx1_ref)], axis=1)
        state = flat(x_ref).astype(F32) + mm(ctx, wo[...], 1, 0)
        state_ref[...] = state.reshape(state_ref.shape)
        nf = (norm_parts(state)[0] * gain_ref[...]).astype(BF)
        transpose_into(nft, along, nf, block, parity)
        cot = flat(cot_ref)
        transpose_into(cott, along, cot, block, parity)
        hidden_units(nf, cot, wi_ref.at[0], wi_ref.at[1], wd_ref, main, here, act_s, gg_s, gu_s)
        out = mm(act_s[here, :], wd_ref[:main], 1, 0)
        out_ref[...] = out.astype(BF).reshape(out_ref.shape)
        grad = mm(gg_s[here, :], wi_ref[0, :main], 1, 0) + mm(gu_s[here, :], wi_ref[1, :main], 1, 0)
        grad_ref[...] = grad.astype(BF).reshape(grad_ref.shape)

    @pl.when(m == steps)
    def _():
        for j, to_ref in ((0, keep_ref), (1, send_ref)):
            at = slice(j * width // 2, (j + 1) * width // 2)
            for i, (at_ref, b_ref) in enumerate(((nft, gg_s), (nft, gu_s), (cott, act_s))):
                to_ref[:, i * main : (i + 1) * main] = mm(at_ref[at], b_ref[...], 1, 0).astype(BF)


def ffn_peer_kernel(
    block, place, state_ref, out_ref, grad_ref, cot_ref, ctx0_ref, ctx1_ref, gain_ref,
    wi_tail, wd_tail, mine_ref, other_ref, _, y_ref, mix_ref, gain_out, keep_ref, send_ref,
    half, gate_w, up_w, down_w, nft, cott, mixt, gg_s, gu_s, act_s, ctx_s,
):
    m = pl.program_id(0)
    parity = place[1]
    steps = pl.num_programs(0) - 1
    units = half.shape[0]
    main, rest = split_units(units)
    group, rows, width = state_ref.shape
    rows = group * rows

    @pl.when(m == 0)
    def _():
        for j, (full, own) in enumerate(
            ((gate_w, wi_tail.at[0]), (up_w, wi_tail.at[1]), (down_w, wd_tail))
        ):
            part = slice(j * (units // 2), (j + 1) * (units // 2))
            join(half, mine_ref.at[part], other_ref.at[part], parity, units // 2)
            full[:main] = half[:main]
            full[main : main + rest] = own[...]
            full[main + rest :] = half[main:]
        gain_out[...] = jnp.zeros_like(gain_out)

    @pl.when(m < steps)
    def _():
        here = pl.ds(pl.multiple_of(m * rows, 16), rows)
        along = pl.ds(pl.multiple_of(m * rows, LANES), rows)
        ctx_s[here, :] = jnp.concatenate([flat(ctx0_ref), flat(ctx1_ref)], axis=1)
        state = flat(state_ref)
        xhat, r = norm_parts(state)
        gain = gain_ref[...]
        nf = (xhat * gain).astype(BF)
        transpose_into(nft, along, nf, block, parity)
        cot = flat(cot_ref)
        transpose_into(cott, along, cot, block, parity)
        hidden_units(nf, cot, gate_w, up_w, down_w, main + 2 * rest, here, act_s, gg_s, gu_s)
        out = state + flat(out_ref).astype(F32) + mm(act_s[here, :], down_w[...], 1, 0)
        y_ref[...] = out.astype(BF).reshape(y_ref.shape)
        grad = flat(grad_ref).astype(F32) + mm(gg_s[here, :], gate_w[...], 1, 0)
        grad = grad + mm(gu_s[here, :], up_w[...], 1, 0)
        gain_out[...] += jnp.sum(grad * xhat, axis=0, keepdims=True)
        mix = (cot.astype(F32) + norm_back(xhat, r, grad * gain)).astype(BF)
        mix_ref[...] = mix.reshape(mix_ref.shape)
        transpose_into(mixt, along, mix, block, parity)

    @pl.when(m == steps)
    def _():
        cols = ctx0_ref.shape[2]
        own_at = 3 * main + cols + 4 * rest
        zero = jnp.zeros((width // 2, rest), BF)
        for j, to_ref in ((0, keep_ref), (1, send_ref)):
            at = slice(j * width // 2, (j + 1) * width // 2)
            ends = []
            for i, (at_ref, b_ref) in enumerate(((nft, gg_s), (nft, gu_s), (cott, act_s))):
                to = slice(i * main, (i + 1) * main)
                to_ref[:, to] = mm(at_ref[at], b_ref[:, :main], 1, 0).astype(BF)
                ends.append(mm(at_ref[at], b_ref[:, main:], 1, 0).astype(BF))
            out = mm(mixt[at], ctx_s[...], 1, 0).astype(BF)
            for out_at, out_cols, part in (
                (own_at, slice(0, cols), slice(0, rest)),
                (3 * main, slice(cols, 2 * cols), slice(rest, 2 * rest)),
            ):
                to_ref[:, out_at : out_at + cols] = out[:, out_cols]
                to_ref[:, out_at + cols : out_at + cols + 4 * rest] = jnp.concatenate(
                    [end[:, part] for end in ends] + [zero], axis=1
                )


def backward_kernel(plan, place, mix_ref, *rest):
    peer, sums, ends = plan["peer"], plan["sums"], plan["ends"]
    rest = list(rest)
    first_ref, second_ref = rest.pop(0), rest.pop(0)
    q_ref, k_ref, v_ref, p_ref, cos_ref, sin_ref = rest[:6]
    rest = rest[6:]
    before_ref = rest.pop(0) if plan["adds"] else None
    if ends:
        normed_ref = rest.pop(0)
    if sums:
        at_ref = rest.pop(0)
    gm_before = rest.pop(0) if plan["earlier"] else None
    gain_sums = None
    if plan["gains"]:
        gain_sums = rest.pop(0), rest.pop(0), rest.pop(0)
    rest = rest[plan["after"] :]
    nag_ref = rest.pop(0)
    if ends:
        inner_ref, outer_ref, gain_out = rest.pop(0), rest.pop(0), rest.pop(0)
    if sums:
        keep_ref, send_ref = rest.pop(0), rest.pop(0)
    else:
        gm_out = rest.pop(0)
    gm_ref = rest.pop(0)
    m = pl.program_id(0)
    if peer:
        wo_scr, w_scr = rest

        @pl.when(m == 0)
        def _():
            join_out(wo_scr, first_ref.at[3], second_ref.at[3], place[1])
            rows = first_ref.shape[1]
            join(w_scr, first_ref.at[:3], second_ref.at[:3], place[1], rows)

        wo_ref, w_ref = wo_scr, w_scr
    else:
        wo_ref, w_ref = first_ref, second_ref
    rows, cols = q_ref.shape[1:]
    ext = k_ref.shape[1]
    own = slice(REACH, REACH + rows)

    def one_batch():
        dctx = mm(mix_ref[0], wo_ref[...], 1, 1).astype(BF)
        cos, sin = cos_ref[0], sin_ref[0]
        gm_ref[m, :REACH, :cols] = jnp.zeros((REACH, cols), BF)
        gm_ref[m, REACH + rows :, :cols] = jnp.zeros((REACH, cols), BF)
        blocks = rows // LANES
        key_parts, value_parts = {}, {}

        def first(b, p):
            here, span, at = places(b, p)
            grad = both_heads(dctx[here, at])
            return grad, mm(v_ref[0, span, at], grad, 1, 1)

        def mid(b, p, begun):
            probs = p_ref[0, b, p].astype(F32)
            weighted = probs * begun[1]
            balance = jnp.sum(weighted, axis=0, keepdims=True)
            return (weighted - probs * balance).astype(BF)

        def over_blocks(parts, p):
            out = []
            for b in range(blocks + 1):
                piece = None
                if b < blocks:
                    piece = parts[b, p][:LANES]
                if b > 0:
                    more = parts[b - 1, p][LANES:]
                    piece = more if piece is None else piece + more
                out.append(piece)
            return jnp.concatenate(out, axis=0)

        def end(b, p, begun, grad_scores):
            here, span, at = places(b, p)
            there = slice(b * LANES + REACH, (b + 1) * LANES + REACH)
            value_parts[b, p] = mm(p_ref[0, b, p], begun[0], 1, 0)
            key_parts[b, p] = mm(grad_scores, both_heads(q_ref[0, here, at]), 1, 0)
            dq = one_row_each(mm(grad_scores, k_ref[0, span, at], 0, 0)) * SCALE
            gm_ref[m, there, at] = (dq * cos[there] - turned(dq) * sin[there]).astype(BF)
            if b == blocks - 1:
                dk = over_blocks(key_parts, p)
                gm_ref[m, :, cols + p * LANES : cols + (p + 1) * LANES] = (
                    dk * cos - turned(dk) * sin
                ).astype(BF)
                dv = over_blocks(value_parts, p).astype(BF)
                gm_ref[m, :, 2 * cols + p * LANES : 2 * cols + (p + 1) * LANES] = dv

        units = [(b, p) for p in range(cols // LANES) for b in range(blocks)]
        in_turn(units, first, mid, end)
        nag = mm(gm_ref[m, :, cols : 2 * cols], w_ref[1], 1, 1)
        nag = nag + mm(gm_ref[m, :, 2 * cols :], w_ref[2], 1, 1)
        nag_q = mm(gm_ref[m, own, :cols], w_ref[0], 1, 1)
        if before_ref is not None:
            nag = nag + before_ref[0].astype(F32)
        if not ends:
            nag_ref[0, :REACH] = nag[:REACH].astype(BF)
            nag_ref[0, own] = (nag[own] + nag_q).astype(BF)
            nag_ref[0, REACH + rows :] = nag[REACH + rows :].astype(BF)
        else:
            left = nag[:REACH].astype(BF)
            right = nag[REACH + rows :].astype(BF)
            inner_ref[0] = jnp.where(place[0] == 0, right, left)
            outer_ref[0] = jnp.where(place[0] == 0, left, right)
            nag_own = nag[own] + nag_q
            nag_ref[0] = nag_own.astype(BF)
            normed = normed_ref[0].astype(F32)
            total = (
                jnp.sum(nag[:REACH] * normed[:REACH], axis=0, keepdims=True)
                + jnp.sum(nag_own * normed[own], axis=0, keepdims=True)
                + jnp.sum(nag[REACH + rows :] * normed[REACH + rows :], axis=0, keepdims=True)
            )

            @pl.when(m == 0)
            def _():
                gain_out[...] = total

            @pl.when(m > 0)
            def _():
                gain_out[...] += total

        if not sums:
            gm_out[0] = gm_ref[m]

    if not sums:
        one_batch()
        return
    steps = pl.num_programs(0) - 1
    pl.when(m < steps)(one_batch)

    @pl.when(m == steps)
    def _():
        half = at_ref.shape[0] // 2
        two = gm_ref[...].reshape(-1, 3 * cols)
        earlier = at_ref.shape[1] - two.shape[0]
        moves = []
        for lo, hi in plan["order"]:
            for j in range(3):
                moves.append((j * cols + lo * LANES, j * cols + hi * LANES))
        for j, to in ((0, keep_ref), (1, send_ref)):
            at = slice(j * half, (j + 1) * half)
            total = mm(at_ref[at, earlier:], two, 1, 0)
            if gm_before is not None:
                one = gm_before[...].reshape(earlier, 3 * cols)
                total = total + mm(at_ref[at, :earlier], one, 1, 0)
            total = total.astype(BF)
            into = 0
            for lo, hi in moves:
                to[:half, into : into + hi - lo] = total[:, lo:hi]
                into += hi - lo
            if gain_sums is not None:
                gain_ref, attn_ref, ffn_ref = gain_sums
                width, wide = gain_ref.shape[1], to.shape[1]
                attn = (attn_ref[...] + gain_out[...]) / gain_ref[...]
                zero = jnp.zeros((MORE - 2, width), F32)
                gains = jnp.concatenate([attn, ffn_ref[...], zero], axis=0).astype(BF)
                for i in range(width // wide):
                    to[half + i * MORE : half + (i + 1) * MORE] = gains[:, i * wide : (i + 1) * wide]


def last_kernel(place, x_ref, nag_ref, inner_ref, outer_ref, mix_ref, gain_ref, *rest):
    out_ref = rest[-1]
    rows = nag_ref.shape[1]
    gain = gain_ref[...]
    step = 32
    for c in range(0, rows, step):
        at = slice(c, c + step)
        xhat, r = norm_parts(x_ref[0, at].astype(F32))
        nag = nag_ref[0, at].astype(F32)
        if c < REACH:
            more = jnp.where(place[0] == 0, outer_ref[0, at], inner_ref[0, at])
            nag = nag + more.astype(F32)
        if c >= rows - REACH:
            end = slice(c - rows + REACH, c - rows + REACH + step)
            more = jnp.where(place[0] == 0, inner_ref[0, end], outer_ref[0, end])
            nag = nag + more.astype(F32)
        out_ref[0, at] = mix_ref[0, at].astype(F32) + norm_back(xhat, r, nag * gain)


def swap(x, axis, bit):
    size = lax.axis_size(axis)
    return lax.ppermute(x, axis, [(i, i ^ bit) for i in range(size)])


def then(value, *earlier):
    return lax.optimization_barrier((value, *earlier))[0]


def quarter(half, axis):
    rows = half.shape[axis] // 2
    return lax.dynamic_slice_in_dim(half, (lax.axis_index("dp") % 2) * rows, rows, axis)


class Halving:
    def __init__(self, total, rows, bit, beside=None):
        self.mine = (lax.axis_index("dp") // bit) % 2
        self.g = total.astype(BF).reshape(-1, 2, rows, total.shape[-1])
        self.sent = lax.dynamic_index_in_dim(self.g, 1 - self.mine, 1, keepdims=False)
        self.beside = beside
        if beside is not None:
            self.sent = jnp.concatenate([self.sent.reshape(-1, total.shape[-1]), beside])
        self.got = swap(self.sent, "dp", bit)

    def total(self, *earlier):
        keep = lax.dynamic_index_in_dim(self.g, self.mine, 1, keepdims=False)
        got = (then(self.got, *earlier) if earlier else self.got).astype(F32)
        if self.beside is None:
            total = keep.astype(F32) + got
            return total.reshape(-1, total.shape[-1])
        keep = keep.astype(F32).reshape(-1, got.shape[-1])
        more = self.beside.shape[0]
        return keep + got[:-more], self.beside.astype(F32) + got[-more:]


def sum_from(total, rows, bit, size):
    while bit < size:
        total = Halving(total, rows, bit).total()
        bit *= 2
    return total


def sorted_halves(keep, send, block, size):
    if block is not None:
        return keep, send
    n, half, cols = keep.shape
    g = jnp.concatenate([keep, send], axis=1).reshape(n, size // 2, 2, 2 * half // size, cols)
    parity = lax.axis_index("dp") % 2
    keep = lax.dynamic_index_in_dim(g, parity, 2, keepdims=False)
    send = lax.dynamic_index_in_dim(g, 1 - parity, 2, keepdims=False)
    return keep.reshape(n, half, cols), send.reshape(n, half, cols)


def on_device(
    inputs, positions, cotangent, gain_attn, gain_ffn, w_qkv, w_out, w_in, down_projection_weight
):
    batches, row_count, width = inputs.shape
    parts, t = lax.axis_size("tensor"), lax.axis_index("tensor")
    dp = lax.axis_size("dp")
    rows = row_count // parts
    ext = rows + 2 * REACH
    cols = w_qkv.shape[2]
    units = w_in.shape[2]
    place = jnp.stack([t, lax.axis_index("dp") % 2]).astype(jnp.int32)
    mine = width // dp
    block = mine if mine % 16 == 0 else None

    qkv = w_qkv.transpose(1, 0, 2)
    w_in = w_in.transpose(1, 2, 0)
    w_down = down_projection_weight
    out_mine = quarter(w_out, 0)
    qkv_mine = jnp.concatenate(
        [
            quarter(qkv, 1),
            jnp.concatenate([out_mine[:, :cols], out_mine[:, cols:]])[None],
        ]
    )
    at = jnp.where(t == 0, row_count - REACH, 0)
    edge = lax.dynamic_slice_in_dim(positions, at, REACH, 1)
    digits = jnp.concatenate([edge // DIGIT, edge % DIGIT], axis=1).astype(BF)
    digits = jnp.pad(digits, ((0, 0), (0, width - 2 * REACH)))
    edge = jnp.concatenate(
        [
            lax.dynamic_slice_in_dim(then(inputs, qkv_mine), at, REACH, 1),
            jnp.broadcast_to(digits[:, None, :], (batches, MORE, width)),
        ],
        axis=1,
    )
    qkv_mine = swap(qkv_mine, "tensor", 1)
    perm = [(2 * i, 2 * i + 2) for i in range(dp - 1)]
    perm += [(2 * i + 3, 2 * i + 1) for i in range(dp - 1)]
    x_outer = lax.ppermute(edge, ("dp", "tensor"), perm)
    freq = jnp.asarray(
        np.power(
            np.float32(rope_base),
            -np.arange(HEAD_DIM // 2, dtype=np.float32) * np.float32(2.0 / HEAD_DIM),
        )[:, None]
    )

    work = 2 * batches * ext * width * 3 * cols + 8 * batches * rows * cols * SPAN
    s = Specs(batches)
    s.per(inputs)
    s.per(x_outer)
    s.per(positions[:, None, :])
    s.whole(gain_attn[None, :], qkv, freq)
    s.after(w_in, w_down)
    s.out(ext, width)
    s.out_columns(width, ext)
    s.out(1, ext, dtype=jnp.int32)
    s.out(ext, LANES, dtype=F32)
    s.out(ext, LANES, dtype=F32)
    s.out_any(units + units // 2, width)
    attention_outs(s, rows, ext, cols)
    normed, normed_t, pos_ext, cos, sin, rest_mine, q0, k0, v0, p0, ctx0 = s.call(
        functools.partial(forward_own, block), place, "attn_fwd_own",
        scratch=[
            pltpu.VMEM((ext, width), BF),
            pltpu.VMEM((units + units // 2, width), BF),
            pltpu.SemaphoreType.DMA((6,)),
        ],
        flops=work, moved=20 * batches * ext * width,
    )

    qkv_other = swap(then(qkv_mine, ctx0), "dp", 1)
    rest_mine = swap(rest_mine, "tensor", 1)
    s = Specs(batches)
    for a in (normed, pos_ext, cos, sin):
        s.per(a)
    s.whole(qkv_mine, qkv_other)
    attention_outs(s, rows, ext, cols)
    q1, k1, v1, p1, ctx1 = s.call(
        forward_peer, place, "attn_fwd_peer",
        scratch=[pltpu.VMEM((3, width, cols), BF)], flops=work, moved=20 * batches * ext * cols,
    )

    own_block = (rows, width)
    group = 2 if batches % 2 == 0 else 1
    main, rest = split_units(units)
    in_cols = 2 * main
    own_place = lambda place: (place[0], 0)
    s = Specs(batches, group)
    s.per(inputs, own_block, own_place)
    s.per(cotangent, own_block, own_place)
    s.per(ctx0)
    s.per(ctx1)
    s.whole(gain_ffn[None, :], w_out)
    s.ins.append(pl.BlockSpec((2, main, width), lambda m, place: (0, 0, 0)))
    s.ins.append(pl.BlockSpec((main, width), lambda m, place: (0, 0)))
    s.args += [w_in, w_down]
    for a in (qkv_mine, qkv_other):
        s.ins.append(pl.BlockSpec((1, cols, cols), lambda m, place: (3, 0, 0)))
        s.args.append(a)
    s.out(rows, width, dtype=F32)
    s.out(rows, width)
    s.out(rows, width)
    for _ in range(2):
        s.out_whole(width // 2, 3 * main)
    state, part_out, part_grad, keep, send = s.call(
        functools.partial(ffn_own_kernel, block), place, "ffn_own", steps=s.batches + 1,
        scratch=[pltpu.VMEM((2 * cols, width), BF)]
        + [pltpu.VMEM((width, batches * rows), BF)] * 2
        + [pltpu.VMEM((batches * rows, main), BF)] * 3,
        flops=2 * batches * rows * width * (9 * main + 2 * cols), moved=3 * 10**7,
    )
    own_keep, send = sorted_halves(keep[None], send[None], block, dp)
    own_got = swap(send[0], "dp", 1)
    rest_other = swap(then(rest_mine, state), "dp", 1)
    own_sum = (own_keep[0].astype(F32) + then(own_got, state).astype(F32)).astype(BF)

    s = Specs(batches, group)
    for a in (state, part_out, part_grad):
        s.per(a)
    s.per(cotangent, own_block, own_place)
    s.per(ctx0)
    s.per(ctx1)
    s.whole(gain_ffn[None, :])
    s.ins.append(pl.BlockSpec((2, rest, width), lambda m, place: (0, main // rest, 0)))
    s.ins.append(pl.BlockSpec((rest, width), lambda m, place: (main // rest, 0)))
    s.args += [w_in, w_down]
    s.whole(rest_mine, rest_other)
    s.after(own_sum)
    s.out(rows, width)
    s.out(rows, width)
    s.out_whole(1, width, dtype=F32)
    for _ in range(2):
        s.out_whole(width // 2, 3 * main + 2 * (cols + 4 * rest))
    y, mix, gain_ffn_part, keep, send = s.call(
        functools.partial(ffn_peer_kernel, block), place, "ffn_peer", steps=s.batches + 1,
        scratch=[pltpu.VMEM((units, width), BF)]
        + [pltpu.VMEM((main + 2 * rest, width), BF)] * 3
        + [pltpu.VMEM((width, batches * rows), BF)] * 3
        + [pltpu.VMEM((batches * rows, main + 2 * rest), BF)] * 3
        + [pltpu.VMEM((batches * rows, 2 * cols), BF)],
        flops=2 * batches * rows * width * (9 * (main + 2 * rest) + 2 * cols), moved=4 * 10**7,
    )
    keep, send = sorted_halves(keep[None], send[None], block, dp)
    got = swap(send[0], "dp", 1)

    def backward(name, peer, batch, pairs, nag=None, into=None, sums=False, gm=None, after=(), gains=()):
        start, stop = batch
        part, count = stop - start, pairs[1] - pairs[0]
        n, at, all_pairs = count * LANES, pairs[0] // count, cols // LANES
        ends = not peer and pairs[1] == all_pairs
        s = Specs(part)
        s.per(mix, start=start)
        if peer:
            s.whole(qkv_mine, qkv_other)
        else:
            s.ins.append(pl.BlockSpec((n, width), lambda m, place: (at, 0)))
            s.ins.append(pl.BlockSpec((3, width, n), lambda m, place: (0, 0, at)))
            s.args += [w_out, qkv]
        q, k, v, p = (q1, k1, v1, p1) if peer else (q0, k0, v0, p0)
        for a in (q, k, v):
            s.per(a, (a.shape[1], n), lambda place: (0, at), start=start)
        s.per(p, (p.shape[1], count) + p.shape[3:], lambda place: (0, at, 0, 0), start=start)
        s.per(cos, start=start)
        s.per(sin, start=start)
        if nag is not None:
            s.per(nag, start=start)
        if ends:
            s.per(normed, start=start)
        if sums:
            s.whole(normed_t)
        if gm is not None:
            s.whole(gm)
        s.whole(*gains)
        s.after(*after)
        scratch = [pltpu.VMEM((part, ext, 3 * n), BF)]
        alias = None
        if into is not None:
            s.after(into)
            alias = {len(s.args): 0}
        if ends:
            s.out(rows, width)
            s.out(REACH, width)
            s.out(REACH, width)
            s.out_whole(1, width, dtype=F32)
        else:
            s.out_part(batches, start, ext, width)
        if sums:
            more = MORE * width // (3 * n) if gains else 0
            s.out_whole(width // 2 + more, 3 * n)
            s.out_whole(width // 2 + more, 3 * n)
        else:
            s.out(ext, 3 * n)
        if peer:
            scratch += [pltpu.VMEM((cols, width), BF), pltpu.VMEM((3, width, cols), BF)]
        plan = dict(
            peer=peer, sums=sums, ends=ends, adds=nag is not None, earlier=gm is not None,
            gains=bool(gains), after=len(after) + (into is not None),
            order=((0, all_pairs - 1), (all_pairs - 1, all_pairs)) if peer else ((0, count),),
        )
        return s.call(
            functools.partial(backward_kernel, plan), place, name,
            steps=part + 1 if sums else None, scratch=scratch, alias=alias,
            flops=(2 * ext * width * 4 * n + 20 * rows * n * SPAN) * part,
            moved=30 * part * ext * n,
        )

    def halos(inner, outer):
        pairs = [(2 * i + 1, 2 * i + 2) for i in range(dp - 1)]
        pairs += [(j, i) for i, j in pairs]
        return swap(inner, "tensor", 1), lax.ppermute(outer, ("dp", "tensor"), pairs)

    pairs, part = cols // LANES, batches // 2
    nag1, gm1 = backward("attn_bwd_peer_a", True, (0, 1), (0, pairs))
    got = then(got, gm1)

    def cores(*at):
        at = slice(*at)
        return (keep[0, :, at].astype(F32) + got[:, at].astype(F32)).astype(BF)

    own_at = 3 * main + cols + 4 * rest
    a_peer = cores(0, in_cols)
    a_from_peer = swap(a_peer, "tensor", 1)
    b_own = [own_sum[:, in_cols:], cores(own_at, None)]
    b_peer = cores(in_cols, own_at)
    b_sum = Halving(jnp.concatenate([jnp.concatenate(b_own, axis=1), b_peer]), mine, 2)
    nag1, keep1, send1 = backward(
        "attn_bwd_peer_b", True, (1, batches), (0, pairs), into=nag1, sums=True, gm=gm1,
        after=(a_peer, b_sum.sent),
    )
    keep1, send1 = sorted_halves(keep1[None], send1[None], block, dp)
    got1 = swap(send1[0], "dp", 1)
    a_own = own_sum[:, :in_cols].astype(F32)
    a_sum = Halving(a_own + then(a_from_peer, send1).astype(F32), mine, 2)
    b_sum = b_sum.total(send1).reshape(2, width // 4, -1)
    b_peer = b_sum[1].astype(BF)
    b_from_peer = swap(b_peer, "tensor", 1)
    got1 = then(got1, a_sum.sent, b_peer)
    peer_sum = Halving(keep1[0].astype(F32) + got1.astype(F32), mine, 2)
    first = (0, pairs - 1)
    nag0, keep2, send2 = backward(
        "attn_bwd_own_a", False, (0, batches), first, nag=nag1, sums=True,
        after=(a_sum.sent, b_peer, peer_sum.sent),
    )
    keep2, send2 = sorted_halves(keep2[None], send2[None], block, dp)
    got2 = swap(send2[0], "dp", 1)
    b_sum = b_sum[0] + then(b_from_peer, send2).astype(F32)
    f_sum = Halving(jnp.concatenate([a_sum.total(send2), b_sum], axis=1), mine, 4)
    peer_sum = peer_sum.total(send2).astype(BF)
    qkv_from_peer = swap(peer_sum, "tensor", 1)
    second = (pairs - 1, pairs)
    nag_a, to_inner, to_outer, gain_a, gm0 = backward(
        "attn_bwd_own_b", False, (0, part), second, nag=nag0, after=(f_sum.sent, peer_sum)
    )
    halos_a = halos(to_inner, to_outer)
    got2, f_sum.got = lax.optimization_barrier((got2, f_sum.got, gm0))[:2]
    own_first = Halving(keep2[0].astype(F32) + got2.astype(F32), mine, 2)
    f_sum = Halving(f_sum.total(), mine, 8)
    nag_b, to_inner, to_outer, _, keep3, send3 = backward(
        "attn_bwd_own_c", False, (part, batches), second, nag=nag0, sums=True, gm=gm0,
        after=(own_first.sent, f_sum.sent), gains=(gain_attn[None, :], gain_a, gain_ffn_part),
    )
    beside = keep3[width // 2 :]
    keep3, sorted3 = sorted_halves(
        keep3[None, : width // 2], send3[None, : width // 2], block, dp
    )
    if block is None:
        send3 = jnp.concatenate([sorted3[0], beside])
    got3 = swap(send3, "dp", 1)
    halos_b = halos(to_inner, to_outer)
    def finish(nag, halos, start, after, into, name):
        s = Specs(part)
        s.per(inputs, own_block, own_place, start=start)
        for a in (nag, *halos):
            s.per(a)
        s.per(mix, start=start)
        s.whole(gain_attn[None, :])
        s.after(*after)
        if into is not None:
            s.after(into)
        s.outs.append(pl.BlockSpec((1, rows, width), lambda m, place: (m + start, 0, 0)))
        s.shapes.append(jax.ShapeDtypeStruct((batches, rows, width), F32))
        return s.call(
            last_kernel, place, name, flops=10**7, moved=8 * part * rows * width,
            alias=None if into is None else {len(s.args): 0},
        )[0]

    columns = [LANES * (pairs - 1), LANES]
    wide = [3 * n for n in columns]
    own_first.got, qkv_from_peer, f_sum.got = lax.optimization_barrier(
        (own_first.got, qkv_from_peer, f_sum.got, send3)
    )[:3]
    from_first = qkv_from_peer[:, : wide[0]].astype(F32)
    own_first = Halving(own_first.total() + from_first, mine, 4)
    f_sum = sum_from(f_sum.total(), mine, 16, dp)
    got3 = then(got3, own_first.sent)
    got3, gains = got3[: width // 2].astype(F32), got3[width // 2 :].astype(F32)
    gains = (beside.astype(F32) + gains).astype(BF)
    own_second = Halving(keep3[0].astype(F32) + got3, mine, 2, gains)
    input_grad = finish(
        nag_a, halos_a, 0, (own_first.sent, own_second.sent, f_sum), None, "input_grad_a"
    )
    own_first.got, own_second.got = lax.optimization_barrier(
        (own_first.got, own_second.got, input_grad)
    )[:2]
    own_first = Halving(own_first.total(), mine, 8)
    total, gains = own_second.total()
    gains = gains.astype(BF)
    own_second = Halving(
        total + qkv_from_peer[:, wide[0] :].astype(F32), mine, 4, gains
    )
    gains_peer = swap(gains, "tensor", 1)
    index = [2 * i + j for i in range(dp) for j in range(2)]
    gains_both = lax.ppermute(gains, ("dp", "tensor"), [(i, (i ^ 1) ^ 8) for i in index])
    input_grad = finish(
        nag_b, halos_b, part, (own_first.sent, own_second.sent), input_grad, "input_grad_b"
    )
    own_first.got, own_second.got, gains_peer, gains_both = lax.optimization_barrier(
        (own_first.got, own_second.got, gains_peer, gains_both, input_grad)
    )[:4]
    total, gains = own_second.total()
    gains = gains + (gains_peer.astype(F32) + gains_both.astype(F32))
    bit = 8
    while bit < dp:
        own_second = Halving(total, mine, bit, gains.astype(BF))
        total, gains = own_second.total()
        bit *= 2
    second_sum = total
    gains = gains.reshape(-1, MORE, wide[1])[:, :2].transpose(1, 0, 2).reshape(2, width)
    first_sum = sum_from(own_first.total(), mine, 16, dp)
    qkv_sum = jnp.stack(
        [
            jnp.concatenate(
                [a[:, j * n : (j + 1) * n] for a, n in zip((first_sum, second_sum), columns)], axis=1
            )
            for j in range(3)
        ]
    ).transpose(1, 0, 2)

    def unit_columns(j):
        tail = 3 * main + cols + j * rest
        return jnp.concatenate(
            [f_sum[:, j * main : (j + 1) * main], f_sum[:, tail : tail + rest]], axis=1
        )

    return (
        y,
        input_grad,
        qkv_sum,
        f_sum[:, 3 * main : 3 * main + cols].T,
        jnp.stack([unit_columns(0), unit_columns(1)], axis=1),
        unit_columns(2).T,
        gains[0],
        gains[1],
    )


def solution(mesh):
    placed = (
        P(None, "dp", None),
        P(None, "dp"),
        P(None, "dp", None),
        P(),
        P(),
        P(None, None, "tensor"),
        P("tensor", None),
        P(None, None, "tensor"),
        P("tensor", None),
    )
    return jax.shard_map(
        on_device,
        mesh=mesh,
        in_specs=placed,
        out_specs=(
            P(None, ("dp", "tensor"), None),
            P(None, ("dp", "tensor"), None),
            P("dp", None, "tensor"),
            P("tensor", "dp"),
            P("dp", None, "tensor"),
            P("tensor", "dp"),
            P(),
            P(),
        ),
        check_vma=False,
    )
```

```python
import functools

import jax
import jax.numpy as jnp
import numpy as np
from jax import lax
from jax.experimental import pallas as pl
from jax.experimental.pallas import tpu as pltpu
from jax.sharding import PartitionSpec as P

HEAD_DIM = 64
WINDOW = 128
REACH = WINDOW // 2
LANES = 128
SPAN = LANES + 2 * REACH
SCALE = HEAD_DIM**-0.5
DIGIT = 64
MORE = 16

norm_eps = 1e-05
rope_base = 10000.0
masked_score = -1e30

BF = jnp.bfloat16
F32 = jnp.float32
MIB = 2**20


def mm(a, b, ca, cb):
    return lax.dot_general(a, b, (((ca,), (cb,)), ((), ())), preferred_element_type=F32)


def turned(v):
    lane = lax.broadcasted_iota(jnp.int32, v.shape, 1)
    low = (lane & 63) < 32
    return jnp.where(low, pltpu.roll(v, 96, 1), pltpu.roll(v, 32, 1))


def both_heads(v):
    lane = lax.broadcasted_iota(jnp.int32, v.shape, 1)
    zero = jnp.zeros_like(v)
    return jnp.concatenate(
        [jnp.where(lane < HEAD_DIM, v, zero), jnp.where(lane >= HEAD_DIM, v, zero)], axis=0
    )


def one_row_each(v):
    rows = v.shape[0] // 2
    lane = lax.broadcasted_iota(jnp.int32, (rows, v.shape[1]), 1)
    return jnp.where(lane < HEAD_DIM, v[:rows], v[rows:])


def norm_parts(v):
    centred = v - jnp.mean(v, axis=1, keepdims=True)
    spread = jnp.mean(centred * centred, axis=1, keepdims=True)
    r = lax.rsqrt(spread + norm_eps)
    return centred * r, r


def norm_back(xhat, r, e):
    return r * (
        e - jnp.mean(e, axis=1, keepdims=True) - xhat * jnp.mean(e * xhat, axis=1, keepdims=True)
    )


def transpose_into(at_ref, at, v, block, parity):
    vt = v.T
    width = vt.shape[0]
    if block is None:
        at_ref[:, at] = vt
        return
    for i in range(width // block):
        odd = parity if i % 2 == 0 else 1 - parity
        to = pl.multiple_of((i // 2) * block + odd * (width // 2), 16)
        at_ref[pl.ds(to, block), at] = vt[i * block : (i + 1) * block]


def join(own_ref, mine_ref, other_ref, parity, rows):
    own_ref[..., pl.ds(pl.multiple_of(parity * rows, 16), rows), :] = mine_ref[...]
    own_ref[..., pl.ds(pl.multiple_of((1 - parity) * rows, 16), rows), :] = other_ref[...]


def join_out(own_ref, mine_ref, other_ref, parity):
    rows = mine_ref.shape[0] // 2
    for ref, place in ((mine_ref, parity), (other_ref, 1 - parity)):
        at = pl.ds(pl.multiple_of(place * rows, 16), rows)
        own_ref[at, : 2 * rows] = ref[:rows]
        own_ref[at, 2 * rows :] = ref[rows:]


class Specs:
    def __init__(self, batches, group=1):
        self.batches = batches // group
        self.group = group
        self.ins, self.args, self.outs, self.shapes = [], [], [], []

    def per(self, a, block=None, at=None, start=0):
        block = (self.group,) + (a.shape[1:] if block is None else block)
        last = self.batches - 1

        def index(m, place):
            m = jnp.minimum(m, last)
            rest = (0,) * (len(block) - 1) if at is None else at(place)
            return (m + start,) + rest

        self.ins.append(pl.BlockSpec(block, index))
        self.args.append(a)

    def whole(self, *arrays):
        for a in arrays:
            self.ins.append(
                pl.BlockSpec(
                    a.shape, lambda m, place, n=a.ndim: (0,) * n, pipeline_mode=pl.Buffered(1)
                )
            )
            self.args.append(a)

    def after(self, *arrays):
        for a in arrays:
            self.ins.append(pl.BlockSpec(memory_space=pl.ANY))
            self.args.append(a)

    def out_part(self, batches, start, *dims, dtype=BF):
        last = self.batches - 1
        n = len(dims)
        self.outs.append(
            pl.BlockSpec(
                (1,) + dims, lambda m, place: (jnp.minimum(m, last) + start,) + (0,) * n
            )
        )
        self.shapes.append(jax.ShapeDtypeStruct((batches,) + dims, dtype))

    def out(self, *dims, dtype=BF):
        last = self.batches - 1
        n = len(dims)
        self.outs.append(
            pl.BlockSpec(
                (self.group,) + dims, lambda m, place: (jnp.minimum(m, last),) + (0,) * n
            )
        )
        self.shapes.append(jax.ShapeDtypeStruct((self.batches * self.group,) + dims, dtype))

    def out_columns(self, rows, cols, dtype=BF):
        last = self.batches - 1
        self.outs.append(pl.BlockSpec((rows, cols), lambda m, place: (0, jnp.minimum(m, last))))
        self.shapes.append(jax.ShapeDtypeStruct((rows, self.batches * cols), dtype))

    def out_any(self, *dims, dtype=BF):
        self.outs.append(pl.BlockSpec(memory_space=pl.ANY))
        self.shapes.append(jax.ShapeDtypeStruct(dims, dtype))

    def out_whole(self, *dims, dtype=BF):
        self.outs.append(
            pl.BlockSpec(
                dims, lambda m, place: (0,) * len(dims), pipeline_mode=pl.Buffered(1)
            )
        )
        self.shapes.append(jax.ShapeDtypeStruct(dims, dtype))

    def call(self, kernel, place, name, vmem, steps=None, scratch=(), flops=0, moved=0, alias=None):
        return pl.pallas_call(
            kernel,
            grid_spec=pltpu.PrefetchScalarGridSpec(
                num_scalar_prefetch=1,
                grid=(self.batches if steps is None else steps,),
                in_specs=self.ins,
                out_specs=self.outs,
                scratch_shapes=list(scratch),
            ),
            out_shape=self.shapes,
            input_output_aliases={} if alias is None else alias,
            compiler_params=pltpu.CompilerParams(vmem_limit_bytes=vmem * MIB),
            cost_estimate=pl.CostEstimate(
                flops=flops // 10, bytes_accessed=moved // 10, transcendentals=0
            ),
            name=name,
        )(place, *self.args)


def in_turn(units, first, mid, last):
    begun, middle, n = {}, {}, len(units)
    for i in range(-1, n + 1):
        if i + 1 < n:
            begun[i + 1] = first(*units[i + 1])
        if i >= 1:
            last(*units[i - 1], begun.pop(i - 1), middle.pop(i - 1))
        if 0 <= i < n:
            middle[i] = mid(*units[i], begun[i])


def places(b, p):
    here = slice(b * LANES, (b + 1) * LANES)
    return here, slice(b * LANES, b * LANES + SPAN), slice(p * LANES, (p + 1) * LANES)


def attend(q_ref, k_ref, v_ref, p_ref, ctx_ref, pos_row):
    rows, cols = q_ref.shape[1:]
    pos_col = jnp.broadcast_to(pos_row, (LANES, pos_row.shape[1])).T
    biases = []
    for b in range(rows // LANES):
        rel = (
            lax.broadcasted_iota(jnp.int32, (SPAN, LANES), 0)
            - REACH
            - lax.broadcasted_iota(jnp.int32, (SPAN, LANES), 1)
        )
        q_pos = pos_row[:, b * LANES + REACH : (b + 1) * LANES + REACH]
        since = jnp.where(rel > 0, pos_col[b * LANES : b * LANES + SPAN], q_pos)
        far = jnp.abs(rel)
        bias = jnp.where((far <= REACH) & (since >= far), 0.0, masked_score).astype(F32)
        biases.append(jnp.concatenate([bias, bias], axis=1))

    def first(b, p):
        here, span, at = places(b, p)
        return mm(k_ref[0, span, at], both_heads(q_ref[0, here, at]), 1, 1)

    def mid(b, p, scores):
        scores = scores + biases[b]
        e = jnp.exp(scores - jnp.max(scores, axis=0, keepdims=True))
        probs = (e * (1.0 / jnp.sum(e, axis=0, keepdims=True))).astype(BF)
        p_ref[0, b, p] = probs
        return probs

    def last(b, p, _, probs):
        here, span, at = places(b, p)
        ctx_ref[0, here, at] = one_row_each(mm(probs, v_ref[0, span, at], 0, 0)).astype(BF)

    units = [(b, p) for b in range(rows // LANES) for p in range(cols // LANES)]
    in_turn(units, first, mid, last)


def project(normed, w_ref, cos, sin, q_ref, k_ref, v_ref):
    rows, cols = q_ref.shape[1:]
    own = slice(REACH, REACH + rows)
    mixed_q = mm(normed[own], w_ref[0], 1, 0)
    mixed_k = mm(normed, w_ref[1], 1, 0)
    v_ref[0] = mm(normed, w_ref[2], 1, 0).astype(BF)
    for p in range(cols // LANES):
        at = slice(p * LANES, (p + 1) * LANES)
        mq, mk = mixed_q[:, at], mixed_k[:, at]
        q_ref[0, :, at] = (mq * cos[own] + turned(mq) * sin[own]).astype(BF) * SCALE
        k_ref[0, :, at] = (mk * cos + turned(mk) * sin).astype(BF)


def forward_own(
    block, place, x_ref, outer_ref, pos_ref, gain_ref, w_ref, freq_ref, wi_ref, wd_ref,
    normed_ref, at_ref, pos_out_ref, cos_ref, sin_ref, rest_ref,
    q_ref, k_ref, v_ref, p_ref, ctx_ref, x_scr, half_scr, sems,
):
    t, parity = place[0], place[1]
    more = wi_ref.shape[1] // 2
    part = pl.ds(pl.multiple_of(parity * more, 16), more)
    sources = [wi_ref.at[0, part], wi_ref.at[1, part], wd_ref.at[part]]
    held = [half_scr.at[i * more : (i + 1) * more] for i in range(3)]
    targets = [rest_ref.at[i * more : (i + 1) * more] for i in range(3)]
    reads = [pltpu.make_async_copy(a, b, sems.at[i]) for i, (a, b) in enumerate(zip(sources, held))]
    writes = [
        pltpu.make_async_copy(a, b, sems.at[3 + i]) for i, (a, b) in enumerate(zip(held, targets))
    ]
    m = pl.program_id(0)

    @pl.when(m == 0)
    def _():
        for copy in reads:
            copy.start()

    @pl.when(m == 1)
    def _():
        for copy in reads:
            copy.wait()
        for copy in writes:
            copy.start()

    @pl.when(m == pl.num_programs(0) - 1)
    def _():
        for copy in writes:
            copy.wait()

    rows, ext = q_ref.shape[1], k_ref.shape[1]
    inner = rows + REACH
    x_scr[pl.ds(pl.multiple_of((1 - t) * REACH, 16), inner), :] = x_ref[
        0, pl.ds(pl.multiple_of(t * (rows - REACH), 16), inner), :
    ]
    x_scr[pl.ds(pl.multiple_of(t * inner, 16), REACH), :] = outer_ref[0, :REACH]
    pos = pos_ref[0]
    digits = outer_ref[0, REACH:].astype(F32)[:1, : 2 * REACH]
    pos_outer = (digits[:, :REACH] * DIGIT + digits[:, REACH:]).astype(jnp.int32)
    pos_row = jnp.where(
        t == 0,
        jnp.concatenate([pos_outer, pos[:, :inner]], axis=1),
        jnp.concatenate([pos[:, rows - REACH :], pos_outer], axis=1),
    )
    pos_out_ref[0] = pos_row
    xhat, _ = norm_parts(x_scr[...].astype(F32))
    normed = (xhat * gain_ref[...]).astype(BF)
    normed_ref[0] = normed
    transpose_into(at_ref, slice(None), normed, block, parity)
    angles = freq_ref[...] * pos_row.astype(F32)
    c, s = jnp.cos(angles), jnp.sin(angles)
    cos = jnp.concatenate([c, c, c, c], axis=0).T
    sin = jnp.concatenate([-s, s, -s, s], axis=0).T
    cos_ref[0] = cos
    sin_ref[0] = sin
    project(normed, w_ref, cos, sin, q_ref, k_ref, v_ref)
    attend(q_ref, k_ref, v_ref, p_ref, ctx_ref, pos_row)


def forward_peer(
    place, normed_ref, pos_ref, cos_ref, sin_ref, mine_ref, other_ref,
    q_ref, k_ref, v_ref, p_ref, ctx_ref, w_scr,
):
    @pl.when(pl.program_id(0) == 0)
    def _():
        join(w_scr, mine_ref.at[:3], other_ref.at[:3], place[1], mine_ref.shape[1])

    project(normed_ref[0], w_scr, cos_ref[0], sin_ref[0], q_ref, k_ref, v_ref)
    attend(q_ref, k_ref, v_ref, p_ref, ctx_ref, pos_ref[0])


def attention_outs(s, rows, ext, cols):
    s.out(rows, cols)
    s.out(ext, cols)
    s.out(ext, cols)
    s.out(rows // LANES, cols // LANES, SPAN, 2 * LANES)
    s.out(rows, cols)


def split_units(units):
    return units // LANES * LANES, units % LANES


def flat(ref):
    return ref[...].reshape(-1, ref.shape[2])


def hidden_units(nf, cot, gate_w, up_w, down_w, count, here, act_s, gg_s, gu_s):
    def first(at):
        return mm(nf, gate_w[at], 1, 1), mm(nf, up_w[at], 1, 1), mm(cot, down_w[at], 1, 1)

    def mid(at, begun):
        g, u, ga = begun
        cdf = 0.5 * (1.0 + lax.erf(g * 0.5**0.5))
        gelu = g * cdf
        slope = cdf + g * jnp.exp(-0.5 * g * g) * 0.3989422804014327
        act_s[here, at] = (gelu * u).astype(BF)
        gg_s[here, at] = (ga * u * slope).astype(BF)
        gu_s[here, at] = (ga * gelu).astype(BF)

    step = 2 * LANES
    chunks = [(slice(c, min(c + step, count)),) for c in range(0, count, step)]
    in_turn(chunks, first, mid, lambda *_: None)


def ffn_own_kernel(
    block, place, x_ref, cot_ref, ctx0_ref, ctx1_ref, gain_ref, wo_ref, wi_ref, wd_ref,
    wo_mine, wo_other, state_ref, out_ref, grad_ref, keep_ref, send_ref,
    wo, nft, cott, gg_s, gu_s, act_s,
):
    m = pl.program_id(0)
    parity = place[1]
    steps = pl.num_programs(0) - 1
    main = gg_s.shape[1]
    group, rows, width = x_ref.shape
    rows = group * rows

    @pl.when(m == 0)
    def _():
        cols = wo_ref.shape[0]
        wo[:cols] = wo_ref[...]
        join_out(wo.at[cols:], wo_mine.at[0], wo_other.at[0], parity)

    @pl.when(m < steps)
    def _():
        here = pl.ds(pl.multiple_of(m * rows, 16), rows)
        along = pl.ds(pl.multiple_of(m * rows, LANES), rows)
        ctx = jnp.concatenate([flat(ctx0_ref), flat(ctx1_ref)], axis=1)
        state = flat(x_ref).astype(F32) + mm(ctx, wo[...], 1, 0)
        state_ref[...] = state.reshape(state_ref.shape)
        nf = (norm_parts(state)[0] * gain_ref[...]).astype(BF)
        transpose_into(nft, along, nf, block, parity)
        cot = flat(cot_ref)
        transpose_into(cott, along, cot, block, parity)
        hidden_units(nf, cot, wi_ref.at[0], wi_ref.at[1], wd_ref, main, here, act_s, gg_s, gu_s)
        out = mm(act_s[here, :], wd_ref[:main], 1, 0)
        out_ref[...] = out.astype(BF).reshape(out_ref.shape)
        grad = mm(gg_s[here, :], wi_ref[0, :main], 1, 0) + mm(gu_s[here, :], wi_ref[1, :main], 1, 0)
        grad_ref[...] = grad.astype(BF).reshape(grad_ref.shape)

    @pl.when(m == steps)
    def _():
        for j, to_ref in ((0, keep_ref), (1, send_ref)):
            at = slice(j * width // 2, (j + 1) * width // 2)
            for i, (at_ref, b_ref) in enumerate(((nft, gg_s), (nft, gu_s), (cott, act_s))):
                to_ref[:, i * main : (i + 1) * main] = mm(at_ref[at], b_ref[...], 1, 0).astype(BF)


def ffn_peer_kernel(
    block, place, state_ref, out_ref, grad_ref, cot_ref, ctx0_ref, ctx1_ref, gain_ref,
    wi_tail, wd_tail, mine_ref, other_ref, _, y_ref, mix_ref, gain_out, keep_ref, send_ref,
    half, gate_w, up_w, down_w, nft, cott, mixt, gg_s, gu_s, act_s, ctx_s,
):
    m = pl.program_id(0)
    parity = place[1]
    steps = pl.num_programs(0) - 1
    units = half.shape[0]
    main, rest = split_units(units)
    group, rows, width = state_ref.shape
    rows = group * rows

    @pl.when(m == 0)
    def _():
        for j, (full, own) in enumerate(
            ((gate_w, wi_tail.at[0]), (up_w, wi_tail.at[1]), (down_w, wd_tail))
        ):
            part = slice(j * (units // 2), (j + 1) * (units // 2))
            join(half, mine_ref.at[part], other_ref.at[part], parity, units // 2)
            full[:main] = half[:main]
            full[main : main + rest] = own[...]
            full[main + rest :] = half[main:]
        gain_out[...] = jnp.zeros_like(gain_out)

    @pl.when(m < steps)
    def _():
        here = pl.ds(pl.multiple_of(m * rows, 16), rows)
        along = pl.ds(pl.multiple_of(m * rows, LANES), rows)
        ctx_s[here, :] = jnp.concatenate([flat(ctx0_ref), flat(ctx1_ref)], axis=1)
        state = flat(state_ref)
        xhat, r = norm_parts(state)
        gain = gain_ref[...]
        nf = (xhat * gain).astype(BF)
        transpose_into(nft, along, nf, block, parity)
        cot = flat(cot_ref)
        transpose_into(cott, along, cot, block, parity)
        hidden_units(nf, cot, gate_w, up_w, down_w, main + 2 * rest, here, act_s, gg_s, gu_s)
        out = state + flat(out_ref).astype(F32) + mm(act_s[here, :], down_w[...], 1, 0)
        y_ref[...] = out.astype(BF).reshape(y_ref.shape)
        grad = flat(grad_ref).astype(F32) + mm(gg_s[here, :], gate_w[...], 1, 0)
        grad = grad + mm(gu_s[here, :], up_w[...], 1, 0)
        gain_out[...] += jnp.sum(grad * xhat, axis=0, keepdims=True)
        mix = (cot.astype(F32) + norm_back(xhat, r, grad * gain)).astype(BF)
        mix_ref[...] = mix.reshape(mix_ref.shape)
        transpose_into(mixt, along, mix, block, parity)

    @pl.when(m == steps)
    def _():
        cols = ctx0_ref.shape[2]
        own_at = 3 * main + cols + 4 * rest
        zero = jnp.zeros((width // 2, rest), BF)
        for j, to_ref in ((0, keep_ref), (1, send_ref)):
            at = slice(j * width // 2, (j + 1) * width // 2)
            ends = []
            for i, (at_ref, b_ref) in enumerate(((nft, gg_s), (nft, gu_s), (cott, act_s))):
                to = slice(i * main, (i + 1) * main)
                to_ref[:, to] = mm(at_ref[at], b_ref[:, :main], 1, 0).astype(BF)
                ends.append(mm(at_ref[at], b_ref[:, main:], 1, 0).astype(BF))
            out = mm(mixt[at], ctx_s[...], 1, 0).astype(BF)
            for out_at, out_cols, part in (
                (own_at, slice(0, cols), slice(0, rest)),
                (3 * main, slice(cols, 2 * cols), slice(rest, 2 * rest)),
            ):
                to_ref[:, out_at : out_at + cols] = out[:, out_cols]
                to_ref[:, out_at + cols : out_at + cols + 4 * rest] = jnp.concatenate(
                    [end[:, part] for end in ends] + [zero], axis=1
                )


def backward_kernel(plan, place, mix_ref, *rest):
    peer, sums, ends = plan["peer"], plan["sums"], plan["ends"]
    rest = list(rest)
    first_ref, second_ref = rest.pop(0), rest.pop(0)
    q_ref, k_ref, v_ref, p_ref, cos_ref, sin_ref = rest[:6]
    rest = rest[6:]
    before_ref = rest.pop(0) if plan["adds"] else None
    if ends:
        normed_ref = rest.pop(0)
    if sums:
        at_ref = rest.pop(0)
    gm_before = rest.pop(0) if plan["earlier"] else None
    gain_sums = None
    if plan["gains"]:
        gain_sums = rest.pop(0), rest.pop(0)
    rest = rest[plan["after"] :]
    nag_ref = rest.pop(0)
    if ends:
        inner_ref, outer_ref = rest.pop(0), rest.pop(0)
    if sums:
        keep_ref, send_ref = rest.pop(0), rest.pop(0)
    else:
        gm_out = rest.pop(0)
    gm_ref = rest.pop(0)
    if ends:
        gain_out = rest.pop(0)
    m = pl.program_id(0)
    if peer:
        wo_scr, w_scr = rest

        @pl.when(m == 0)
        def _():
            join_out(wo_scr, first_ref.at[3], second_ref.at[3], place[1])
            rows = first_ref.shape[1]
            join(w_scr, first_ref.at[:3], second_ref.at[:3], place[1], rows)

        wo_ref, w_ref = wo_scr, w_scr
    else:
        wo_ref, w_ref = first_ref, second_ref
    rows, cols = q_ref.shape[1:]
    ext = k_ref.shape[1]
    own = slice(REACH, REACH + rows)

    def one_batch():
        dctx = mm(mix_ref[0], wo_ref[...], 1, 1).astype(BF)
        cos, sin = cos_ref[0], sin_ref[0]
        gm_ref[m, :REACH, :cols] = jnp.zeros((REACH, cols), BF)
        gm_ref[m, REACH + rows :, :cols] = jnp.zeros((REACH, cols), BF)
        blocks = rows // LANES
        key_parts, value_parts = {}, {}

        def first(b, p):
            here, span, at = places(b, p)
            grad = both_heads(dctx[here, at])
            return grad, mm(v_ref[0, span, at], grad, 1, 1)

        def mid(b, p, begun):
            probs = p_ref[0, b, p].astype(F32)
            weighted = probs * begun[1]
            balance = jnp.sum(weighted, axis=0, keepdims=True)
            return (weighted - probs * balance).astype(BF)

        def over_blocks(parts, p):
            out = []
            for b in range(blocks + 1):
                piece = None
                if b < blocks:
                    piece = parts[b, p][:LANES]
                if b > 0:
                    more = parts[b - 1, p][LANES:]
                    piece = more if piece is None else piece + more
                out.append(piece)
            return jnp.concatenate(out, axis=0)

        def end(b, p, begun, grad_scores):
            here, span, at = places(b, p)
            there = slice(b * LANES + REACH, (b + 1) * LANES + REACH)
            value_parts[b, p] = mm(p_ref[0, b, p], begun[0], 1, 0)
            key_parts[b, p] = mm(grad_scores, both_heads(q_ref[0, here, at]), 1, 0)
            dq = one_row_each(mm(grad_scores, k_ref[0, span, at], 0, 0)) * SCALE
            gm_ref[m, there, at] = (dq * cos[there] - turned(dq) * sin[there]).astype(BF)
            if b == blocks - 1:
                dk = over_blocks(key_parts, p)
                gm_ref[m, :, cols + p * LANES : cols + (p + 1) * LANES] = (
                    dk * cos - turned(dk) * sin
                ).astype(BF)
                dv = over_blocks(value_parts, p).astype(BF)
                gm_ref[m, :, 2 * cols + p * LANES : 2 * cols + (p + 1) * LANES] = dv

        units = [(b, p) for p in range(cols // LANES) for b in range(blocks)]
        in_turn(units, first, mid, end)
        nag = mm(gm_ref[m, :, cols : 2 * cols], w_ref[1], 1, 1)
        nag = nag + mm(gm_ref[m, :, 2 * cols :], w_ref[2], 1, 1)
        nag_q = mm(gm_ref[m, own, :cols], w_ref[0], 1, 1)
        if before_ref is not None:
            nag = nag + before_ref[0].astype(F32)
        if not ends:
            nag_ref[0, :REACH] = nag[:REACH].astype(BF)
            nag_ref[0, own] = (nag[own] + nag_q).astype(BF)
            nag_ref[0, REACH + rows :] = nag[REACH + rows :].astype(BF)
        else:
            left = nag[:REACH].astype(BF)
            right = nag[REACH + rows :].astype(BF)
            inner_ref[0] = jnp.where(place[0] == 0, right, left)
            outer_ref[0] = jnp.where(place[0] == 0, left, right)
            nag_own = nag[own] + nag_q
            nag_ref[0] = nag_own.astype(BF)
            normed = normed_ref[0].astype(F32)
            total = (
                jnp.sum(nag[:REACH] * normed[:REACH], axis=0, keepdims=True)
                + jnp.sum(nag_own * normed[own], axis=0, keepdims=True)
                + jnp.sum(nag[REACH + rows :] * normed[REACH + rows :], axis=0, keepdims=True)
            )

            @pl.when(m == 0)
            def _():
                gain_out[...] = total

            @pl.when(m > 0)
            def _():
                gain_out[...] += total

        if not sums:
            gm_out[0] = gm_ref[m]

    if not sums:
        one_batch()
        return
    steps = pl.num_programs(0) - 1
    pl.when(m < steps)(one_batch)

    @pl.when(m == steps)
    def _():
        half = at_ref.shape[0] // 2
        two = gm_ref[...].reshape(-1, 3 * cols)
        earlier = at_ref.shape[1] - two.shape[0]
        moves = []
        for lo, hi in plan["order"]:
            for j in range(3):
                moves.append((j * cols + lo * LANES, j * cols + hi * LANES))
        for j, to in ((0, keep_ref), (1, send_ref)):
            at = slice(j * half, (j + 1) * half)
            total = mm(at_ref[at, earlier:], two, 1, 0)
            if gm_before is not None:
                one = gm_before[...].reshape(earlier, 3 * cols)
                total = total + mm(at_ref[at, :earlier], one, 1, 0)
            total = total.astype(BF)
            into = 0
            for lo, hi in moves:
                to[:half, into : into + hi - lo] = total[:, lo:hi]
                into += hi - lo
            if gain_sums is not None:
                gain_ref, ffn_ref = gain_sums
                width, wide = gain_ref.shape[1], to.shape[1]
                attn = gain_out[...] / gain_ref[...]
                zero = jnp.zeros((MORE - 2, width), F32)
                gains = jnp.concatenate([attn, ffn_ref[...], zero], axis=0).astype(BF)
                for i in range(width // wide):
                    to[half + i * MORE : half + (i + 1) * MORE] = gains[:, i * wide : (i + 1) * wide]


def last_kernel(edges, place, x_ref, nag_ref, mix_ref, gain_ref, *rest):
    out_ref = rest[-1]
    gain = gain_ref[...]
    if edges:
        inner_ref, outer_ref = rest[:2]
        use_inner = (place[0] == 0) == (pl.program_id(0) == 1)
    step = 32
    for i in range(nag_ref.shape[0]):
        for c in range(0, REACH, step):
            at = slice(c, c + step)
            xhat, r = norm_parts(x_ref[i, at].astype(F32))
            nag = nag_ref[i, at].astype(F32)
            if edges:
                nag = nag + jnp.where(use_inner, inner_ref[i, at], outer_ref[i, at]).astype(F32)
            out_ref[i, at] = mix_ref[i, at].astype(F32) + norm_back(xhat, r, nag * gain)


def swap(x, axis, bit):
    size = lax.axis_size(axis)
    return lax.ppermute(x, axis, [(i, i ^ bit) for i in range(size)])


def then(value, *earlier):
    return lax.optimization_barrier((value, *earlier))[0]


def quarter(half, axis):
    rows = half.shape[axis] // 2
    return lax.dynamic_slice_in_dim(half, (lax.axis_index("dp") % 2) * rows, rows, axis)


class Halving:
    def __init__(self, total, rows, bit, beside=None):
        self.mine = (lax.axis_index("dp") // bit) % 2
        self.g = total.astype(BF).reshape(-1, 2, rows, total.shape[-1])
        self.sent = lax.dynamic_index_in_dim(self.g, 1 - self.mine, 1, keepdims=False)
        self.beside = beside
        if beside is not None:
            self.sent = jnp.concatenate([self.sent.reshape(-1, total.shape[-1]), beside])
        self.got = swap(self.sent, "dp", bit)

    def total(self, *earlier):
        keep = lax.dynamic_index_in_dim(self.g, self.mine, 1, keepdims=False)
        got = (then(self.got, *earlier) if earlier else self.got).astype(F32)
        if self.beside is None:
            total = keep.astype(F32) + got
            return total.reshape(-1, total.shape[-1])
        keep = keep.astype(F32).reshape(-1, got.shape[-1])
        more = self.beside.shape[0]
        return keep + got[:-more], self.beside.astype(F32) + got[-more:]


def sum_from(total, rows, bit, size):
    while bit < size:
        total = Halving(total, rows, bit).total()
        bit *= 2
    return total


def sorted_halves(keep, send, block, size):
    if block is not None:
        return keep, send
    n, half, cols = keep.shape
    g = jnp.concatenate([keep, send], axis=1).reshape(n, size // 2, 2, 2 * half // size, cols)
    parity = lax.axis_index("dp") % 2
    keep = lax.dynamic_index_in_dim(g, parity, 2, keepdims=False)
    send = lax.dynamic_index_in_dim(g, 1 - parity, 2, keepdims=False)
    return keep.reshape(n, half, cols), send.reshape(n, half, cols)


def on_device(
    inputs, positions, cotangent, gain_attn, gain_ffn, w_qkv, w_out, w_in, down_projection_weight
):
    batches, row_count, width = inputs.shape
    parts, t = lax.axis_size("tensor"), lax.axis_index("tensor")
    dp = lax.axis_size("dp")
    rows = row_count // parts
    ext = rows + 2 * REACH
    cols = w_qkv.shape[2]
    units = w_in.shape[2]
    place = jnp.stack([t, lax.axis_index("dp") % 2]).astype(jnp.int32)
    mine = width // dp
    block = mine if mine % 16 == 0 else None

    qkv = w_qkv.transpose(1, 0, 2)
    w_in = w_in.transpose(1, 2, 0)
    w_down = down_projection_weight
    out_mine = quarter(w_out, 0)
    qkv_mine = jnp.concatenate(
        [
            quarter(qkv, 1),
            jnp.concatenate([out_mine[:, :cols], out_mine[:, cols:]])[None],
        ]
    )
    at = jnp.where(t == 0, row_count - REACH, 0)
    edge = lax.dynamic_slice_in_dim(positions, at, REACH, 1)
    digits = jnp.concatenate([edge // DIGIT, edge % DIGIT], axis=1).astype(BF)
    digits = jnp.pad(digits, ((0, 0), (0, width - 2 * REACH)))
    edge = jnp.concatenate(
        [
            lax.dynamic_slice_in_dim(then(inputs, qkv_mine), at, REACH, 1),
            jnp.broadcast_to(digits[:, None, :], (batches, MORE, width)),
        ],
        axis=1,
    )
    qkv_mine = swap(qkv_mine, "tensor", 1)
    perm = [(2 * i, 2 * i + 2) for i in range(dp - 1)]
    perm += [(2 * i + 3, 2 * i + 1) for i in range(dp - 1)]
    x_outer = lax.ppermute(edge, ("dp", "tensor"), perm)
    freq = jnp.asarray(
        np.power(
            np.float32(rope_base),
            -np.arange(HEAD_DIM // 2, dtype=np.float32) * np.float32(2.0 / HEAD_DIM),
        )[:, None]
    )

    work = 2 * batches * ext * width * 3 * cols + 8 * batches * rows * cols * SPAN
    s = Specs(batches)
    s.per(inputs)
    s.per(x_outer)
    s.per(positions[:, None, :])
    s.whole(gain_attn[None, :], qkv, freq)
    s.after(w_in, w_down)
    s.out(ext, width)
    s.out_columns(width, ext)
    s.out(1, ext, dtype=jnp.int32)
    s.out(ext, LANES, dtype=F32)
    s.out(ext, LANES, dtype=F32)
    s.out_any(units + units // 2, width)
    attention_outs(s, rows, ext, cols)
    normed, normed_t, pos_ext, cos, sin, rest_mine, q0, k0, v0, p0, ctx0 = s.call(
        functools.partial(forward_own, block), place, "attn_fwd_own", 60,
        scratch=[
            pltpu.VMEM((ext, width), BF),
            pltpu.VMEM((units + units // 2, width), BF),
            pltpu.SemaphoreType.DMA((6,)),
        ],
        flops=work, moved=20 * batches * ext * width,
    )

    qkv_other = swap(then(qkv_mine, ctx0), "dp", 1)
    rest_mine = swap(rest_mine, "tensor", 1)
    s = Specs(batches)
    for a in (normed, pos_ext, cos, sin):
        s.per(a)
    s.whole(qkv_mine, qkv_other)
    attention_outs(s, rows, ext, cols)
    q1, k1, v1, p1, ctx1 = s.call(
        forward_peer, place, "attn_fwd_peer", 60,
        scratch=[pltpu.VMEM((3, width, cols), BF)], flops=work, moved=20 * batches * ext * cols,
    )

    own_block = (rows, width)
    group = 2 if batches % 2 == 0 else 1
    main, rest = split_units(units)
    in_cols = 2 * main
    own_place = lambda place: (place[0], 0)
    s = Specs(batches, group)
    s.per(inputs, own_block, own_place)
    s.per(cotangent, own_block, own_place)
    s.per(ctx0)
    s.per(ctx1)
    s.whole(gain_ffn[None, :], w_out)
    s.ins.append(pl.BlockSpec((2, main, width), lambda m, place: (0, 0, 0)))
    s.ins.append(pl.BlockSpec((main, width), lambda m, place: (0, 0)))
    s.args += [w_in, w_down]
    for a in (qkv_mine, qkv_other):
        s.ins.append(pl.BlockSpec((1, cols, cols), lambda m, place: (3, 0, 0)))
        s.args.append(a)
    s.out(rows, width, dtype=F32)
    s.out(rows, width)
    s.out(rows, width)
    for _ in range(2):
        s.out_whole(width // 2, 3 * main)
    state, part_out, part_grad, keep, send = s.call(
        functools.partial(ffn_own_kernel, block), place, "ffn_own", 52, steps=s.batches + 1,
        scratch=[pltpu.VMEM((2 * cols, width), BF)]
        + [pltpu.VMEM((width, batches * rows), BF)] * 2
        + [pltpu.VMEM((batches * rows, main), BF)] * 3,
        flops=2 * batches * rows * width * (9 * main + 2 * cols), moved=3 * 10**7,
    )
    own_keep, send = sorted_halves(keep[None], send[None], block, dp)
    own_got = swap(send[0], "dp", 1)
    rest_other = swap(then(rest_mine, state), "dp", 1)
    own_sum = (own_keep[0].astype(F32) + then(own_got, state).astype(F32)).astype(BF)

    s = Specs(batches, group)
    for a in (state, part_out, part_grad):
        s.per(a)
    s.per(cotangent, own_block, own_place)
    s.per(ctx0)
    s.per(ctx1)
    s.whole(gain_ffn[None, :])
    s.ins.append(pl.BlockSpec((2, rest, width), lambda m, place: (0, main // rest, 0)))
    s.ins.append(pl.BlockSpec((rest, width), lambda m, place: (main // rest, 0)))
    s.args += [w_in, w_down]
    s.whole(rest_mine, rest_other)
    s.after(own_sum)
    s.out(rows, width)
    s.out(rows, width)
    s.out_whole(1, width, dtype=F32)
    for _ in range(2):
        s.out_whole(width // 2, 3 * main + 2 * (cols + 4 * rest))
    y, mix, gain_ffn_part, keep, send = s.call(
        functools.partial(ffn_peer_kernel, block), place, "ffn_peer", 52, steps=s.batches + 1,
        scratch=[pltpu.VMEM((units, width), BF)]
        + [pltpu.VMEM((main + 2 * rest, width), BF)] * 3
        + [pltpu.VMEM((width, batches * rows), BF)] * 3
        + [pltpu.VMEM((batches * rows, main + 2 * rest), BF)] * 3
        + [pltpu.VMEM((batches * rows, 2 * cols), BF)],
        flops=2 * batches * rows * width * (9 * (main + 2 * rest) + 2 * cols), moved=4 * 10**7,
    )
    keep, send = sorted_halves(keep[None], send[None], block, dp)
    got = swap(send[0], "dp", 1)

    def backward(name, peer, batch, pairs, nag=None, into=None, sums=False, gm=None, after=(), gains=()):
        start, stop = batch
        part, count = stop - start, pairs[1] - pairs[0]
        n, at, all_pairs = count * LANES, pairs[0] // count, cols // LANES
        ends = not peer and pairs[1] == all_pairs
        s = Specs(part)
        s.per(mix, start=start)
        if peer:
            s.whole(qkv_mine, qkv_other)
        else:
            s.ins.append(pl.BlockSpec((n, width), lambda m, place: (at, 0)))
            s.ins.append(pl.BlockSpec((3, width, n), lambda m, place: (0, 0, at)))
            s.args += [w_out, qkv]
        q, k, v, p = (q1, k1, v1, p1) if peer else (q0, k0, v0, p0)
        for a in (q, k, v):
            s.per(a, (a.shape[1], n), lambda place: (0, at), start=start)
        s.per(p, (p.shape[1], count) + p.shape[3:], lambda place: (0, at, 0, 0), start=start)
        s.per(cos, start=start)
        s.per(sin, start=start)
        if nag is not None:
            s.per(nag, start=start)
        if ends:
            s.per(normed, start=start)
        if sums:
            s.whole(normed_t)
        if gm is not None:
            s.whole(gm)
        s.whole(*gains)
        s.after(*after)
        scratch = [pltpu.VMEM((part, ext, 3 * n), BF)]
        alias = None
        if into is not None:
            s.after(into)
            alias = {len(s.args): 0}
        if ends:
            s.out(rows, width)
            s.out(REACH, width)
            s.out(REACH, width)
            scratch.append(pltpu.VMEM((1, width), F32))
        else:
            s.out_part(batches, start, ext, width)
        if sums:
            more = MORE * width // (3 * n) if gains else 0
            s.out_whole(width // 2 + more, 3 * n)
            s.out_whole(width // 2 + more, 3 * n)
        else:
            s.out(ext, 3 * n)
        if peer:
            scratch += [pltpu.VMEM((cols, width), BF), pltpu.VMEM((3, width, cols), BF)]
        plan = dict(
            peer=peer, sums=sums, ends=ends, adds=nag is not None, earlier=gm is not None,
            gains=bool(gains), after=len(after) + (into is not None),
            order=((0, all_pairs - 1), (all_pairs - 1, all_pairs)) if peer else ((0, count),),
        )
        return s.call(
            functools.partial(backward_kernel, plan), place, name, 52,
            steps=part + 1 if sums else None, scratch=scratch, alias=alias,
            flops=(2 * ext * width * 4 * n + 20 * rows * n * SPAN) * part,
            moved=30 * part * ext * n,
        )

    def halos(inner, outer):
        pairs = [(2 * i + 1, 2 * i + 2) for i in range(dp - 1)]
        pairs += [(j, i) for i, j in pairs]
        return swap(inner, "tensor", 1), lax.ppermute(outer, ("dp", "tensor"), pairs)

    pairs, part = cols // LANES, batches // 2
    nag1, gm1 = backward("attn_bwd_peer_a", True, (0, 1), (0, pairs))
    got = then(got, gm1)

    def cores(*at):
        at = slice(*at)
        return (keep[0, :, at].astype(F32) + got[:, at].astype(F32)).astype(BF)

    own_at = 3 * main + cols + 4 * rest
    a_peer = cores(0, in_cols)
    a_from_peer = swap(a_peer, "tensor", 1)
    b_own = [own_sum[:, in_cols:], cores(own_at, None)]
    b_peer = cores(in_cols, own_at)
    b_sum = Halving(jnp.concatenate([jnp.concatenate(b_own, axis=1), b_peer]), mine, 2)
    nag1, keep1, send1 = backward(
        "attn_bwd_peer_b", True, (1, batches), (0, pairs), into=nag1, sums=True, gm=gm1,
        after=(a_peer, b_sum.sent),
    )
    keep1, send1 = sorted_halves(keep1[None], send1[None], block, dp)
    got1 = swap(send1[0], "dp", 1)
    a_own = own_sum[:, :in_cols].astype(F32)
    a_sum = Halving(a_own + then(a_from_peer, send1).astype(F32), mine, 2)
    b_sum = b_sum.total(send1).reshape(2, width // 4, -1)
    b_peer = b_sum[1].astype(BF)
    b_from_peer = swap(b_peer, "tensor", 1)
    got1 = then(got1, a_sum.sent, b_peer)
    peer_sum = Halving(keep1[0].astype(F32) + got1.astype(F32), mine, 2)
    first = (0, pairs - 1)
    nag0, keep2, send2 = backward(
        "attn_bwd_own_a", False, (0, batches), first, nag=nag1, sums=True,
        after=(a_sum.sent, b_peer, peer_sum.sent),
    )
    keep2, send2 = sorted_halves(keep2[None], send2[None], block, dp)
    got2 = swap(send2[0], "dp", 1)
    b_sum = b_sum[0] + then(b_from_peer, send2).astype(F32)
    f_sum = Halving(jnp.concatenate([a_sum.total(send2), b_sum], axis=1), mine, 4)
    peer_sum = peer_sum.total(send2).astype(BF)
    qkv_from_peer = swap(peer_sum, "tensor", 1)
    got2 = then(got2, f_sum.sent, peer_sum)
    own_first = Halving(keep2[0].astype(F32) + got2.astype(F32), mine, 2)
    second = (pairs - 1, pairs)
    nag, to_inner, to_outer, keep3, send3 = backward(
        "attn_bwd_own_b", False, (0, batches), second, nag=nag0, sums=True,
        after=(f_sum.sent, peer_sum, own_first.sent), gains=(gain_attn[None, :], gain_ffn_part),
    )
    beside = keep3[width // 2 :]
    keep3, sorted3 = sorted_halves(
        keep3[None, : width // 2], send3[None, : width // 2], block, dp
    )
    if block is None:
        send3 = jnp.concatenate([sorted3[0], beside])
    gains_peer = swap(beside, "tensor", 1)
    index = [2 * i + j for i in range(dp) for j in range(2)]
    gains_both = lax.ppermute(beside, ("dp", "tensor"), [(i, i ^ 3) for i in index])
    got3 = swap(send3, "dp", 1)
    from_inner = swap(to_inner, "tensor", 1)
    neighbours = [(2 * i + 1, 2 * i + 2) for i in range(dp - 1)]
    neighbours += [(j, i) for i, j in neighbours]
    from_outer = lax.ppermute(to_outer, ("dp", "tensor"), neighbours)

    columns = [LANES * (pairs - 1), LANES]
    wide = [3 * n for n in columns]
    own_first.got, qkv_from_peer, f_sum.got = lax.optimization_barrier(
        (own_first.got, qkv_from_peer, f_sum.got, send3)
    )[:3]
    from_first = qkv_from_peer[:, : wide[0]].astype(F32)
    own_first = Halving(own_first.total() + from_first, mine, 4)
    f_sum = Halving(f_sum.total(), mine, 8)
    got3 = then(got3, own_first.sent, f_sum.sent)
    got3, gains = got3[: width // 2].astype(F32), got3[width // 2 :].astype(F32)
    gains = beside.astype(F32) + gains
    gains = (gains + (gains_peer.astype(F32) + gains_both.astype(F32))).astype(BF)
    own_second = Halving(keep3[0].astype(F32) + got3, mine, 2, gains)

    def finish(edges, after, into, name):
        blocks = rows // REACH
        count, step = (2, blocks - 1) if edges else (blocks - 2, 1)
        begin = 0 if edges else 1

        def spec(arrays, first):
            return pl.BlockSpec(
                (batches, REACH, width), lambda j, place: (0, first(place) + begin + step * j, 0)
            )

        fixed = pl.BlockSpec((batches, REACH, width), lambda j, place: (0, 0, 0))
        args = [inputs, nag, mix, gain_attn[None, :]]
        specs = [
            spec(inputs, lambda place: place[0] * blocks),
            spec(nag, lambda place: 0),
            spec(mix, lambda place: 0),
            pl.BlockSpec((1, width), lambda j, place: (0, 0)),
        ]
        if edges:
            args += [from_inner, from_outer]
            specs += [fixed, fixed]
        more = [*after] if into is None else [*after, into]
        args += more
        specs += [pl.BlockSpec(memory_space=pl.ANY)] * len(more)
        return pl.pallas_call(
            functools.partial(last_kernel, edges),
            grid_spec=pltpu.PrefetchScalarGridSpec(
                num_scalar_prefetch=1,
                grid=(count,),
                in_specs=specs,
                out_specs=spec(nag, lambda place: 0),
            ),
            out_shape=jax.ShapeDtypeStruct((batches, rows, width), F32),
            input_output_aliases={} if into is None else {len(args): 0},
            compiler_params=pltpu.CompilerParams(vmem_limit_bytes=48 * MIB),
            cost_estimate=pl.CostEstimate(flops=10**8, bytes_accessed=10**6, transcendentals=0),
            name=name,
        )(place, *args)

    input_grad = finish(False, (own_second.sent,), None, "input_grad_inside")
    own_first.got, own_second.got = lax.optimization_barrier(
        (own_first.got, own_second.got, input_grad)
    )[:2]
    total, gains = own_second.total()
    gains = gains.astype(BF)
    own_second = Halving(
        total + qkv_from_peer[:, wide[0] :].astype(F32), mine, 4, gains
    )
    own_first = Halving(then(own_first.total(), own_second.sent), mine, 8)
    total, gains = own_second.total()
    bit = 8
    while bit < dp:
        own_second = Halving(total, mine, bit, gains.astype(BF))
        last_sent = own_second.sent
        total, gains = own_second.total()
        bit *= 2
    second_sum = total
    gains = gains.reshape(-1, MORE, wide[1])[:, :2].transpose(1, 0, 2).reshape(2, width)

    input_grad = finish(True, (last_sent, own_first.sent), input_grad, "input_grad_edges")
    own_first.got, f_sum.got = lax.optimization_barrier(
        (own_first.got, f_sum.got, last_sent)
    )[:2]
    first_sum = sum_from(own_first.total(), mine, 16, dp)
    f_sum = sum_from(f_sum.total(), mine, 16, dp)
    qkv_sum = jnp.stack(
        [
            jnp.concatenate(
                [a[:, j * n : (j + 1) * n] for a, n in zip((first_sum, second_sum), columns)], axis=1
            )
            for j in range(3)
        ]
    ).transpose(1, 0, 2)

    def unit_columns(j):
        tail = 3 * main + cols + j * rest
        return jnp.concatenate(
            [f_sum[:, j * main : (j + 1) * main], f_sum[:, tail : tail + rest]], axis=1
        )

    return (
        y,
        input_grad,
        qkv_sum,
        f_sum[:, 3 * main : 3 * main + cols].T,
        jnp.stack([unit_columns(0), unit_columns(1)], axis=1),
        unit_columns(2).T,
        gains[0],
        gains[1],
    )


def solution(mesh):
    placed = (
        P(None, "dp", None),
        P(None, "dp"),
        P(None, "dp", None),
        P(),
        P(),
        P(None, None, "tensor"),
        P("tensor", None),
        P(None, None, "tensor"),
        P("tensor", None),
    )
    return jax.shard_map(
        on_device,
        mesh=mesh,
        in_specs=placed,
        out_specs=(
            P(None, ("dp", "tensor"), None),
            P(None, ("dp", "tensor"), None),
            P("dp", None, "tensor"),
            P("tensor", "dp"),
            P("dp", None, "tensor"),
            P("tensor", "dp"),
            P(),
            P(),
        ),
        check_vma=False,
    )
```

```python
import functools

import jax
import jax.numpy as jnp
import numpy as np
from jax import lax
from jax.experimental import pallas as pl
from jax.experimental.pallas import tpu as pltpu
from jax.sharding import PartitionSpec as P

HEAD_DIM = 64
WINDOW = 128
REACH = WINDOW // 2
LANES = 128
SPAN = LANES + 2 * REACH
SCALE = HEAD_DIM**-0.5
DIGIT = 64
MORE = 16

norm_eps = 1e-05
rope_base = 10000.0
masked_score = -1e30

BF = jnp.bfloat16
F32 = jnp.float32
MIB = 2**20


def mm(a, b, ca, cb):
    return lax.dot_general(a, b, (((ca,), (cb,)), ((), ())), preferred_element_type=F32)


def turned(v):
    lane = lax.broadcasted_iota(jnp.int32, v.shape, 1)
    low = (lane & 63) < 32
    return jnp.where(low, pltpu.roll(v, 96, 1), pltpu.roll(v, 32, 1))


def both_heads(v):
    lane = lax.broadcasted_iota(jnp.int32, v.shape, 1)
    zero = jnp.zeros_like(v)
    return jnp.concatenate(
        [jnp.where(lane < HEAD_DIM, v, zero), jnp.where(lane >= HEAD_DIM, v, zero)], axis=0
    )


def one_row_each(v):
    rows = v.shape[0] // 2
    lane = lax.broadcasted_iota(jnp.int32, (rows, v.shape[1]), 1)
    return jnp.where(lane < HEAD_DIM, v[:rows], v[rows:])


def norm_parts(v):
    centred = v - jnp.mean(v, axis=1, keepdims=True)
    spread = jnp.mean(centred * centred, axis=1, keepdims=True)
    r = lax.rsqrt(spread + norm_eps)
    return centred * r, r


def norm_back(xhat, r, e):
    return r * (
        e - jnp.mean(e, axis=1, keepdims=True) - xhat * jnp.mean(e * xhat, axis=1, keepdims=True)
    )


def transpose_into(at_ref, at, v, block, parity):
    vt = v.T
    width = vt.shape[0]
    if block is None:
        at_ref[:, at] = vt
        return
    for i in range(width // block):
        odd = parity if i % 2 == 0 else 1 - parity
        to = pl.multiple_of((i // 2) * block + odd * (width // 2), 16)
        at_ref[pl.ds(to, block), at] = vt[i * block : (i + 1) * block]


def join(own_ref, mine_ref, other_ref, parity, rows):
    own_ref[..., pl.ds(pl.multiple_of(parity * rows, 16), rows), :] = mine_ref[...]
    own_ref[..., pl.ds(pl.multiple_of((1 - parity) * rows, 16), rows), :] = other_ref[...]


def join_out(own_ref, mine_ref, other_ref, parity):
    rows = mine_ref.shape[0] // 2
    for ref, place in ((mine_ref, parity), (other_ref, 1 - parity)):
        at = pl.ds(pl.multiple_of(place * rows, 16), rows)
        own_ref[at, : 2 * rows] = ref[:rows]
        own_ref[at, 2 * rows :] = ref[rows:]


class Specs:
    def __init__(self, batches, group=1):
        self.batches = batches // group
        self.group = group
        self.ins, self.args, self.outs, self.shapes = [], [], [], []

    def per(self, a, block=None, at=None, start=0):
        block = (self.group,) + (a.shape[1:] if block is None else block)
        last = self.batches - 1

        def index(m, place):
            m = jnp.minimum(m, last)
            rest = (0,) * (len(block) - 1) if at is None else at(place)
            return (m + start,) + rest

        self.ins.append(pl.BlockSpec(block, index))
        self.args.append(a)

    def whole(self, *arrays):
        for a in arrays:
            self.ins.append(
                pl.BlockSpec(
                    a.shape, lambda m, place, n=a.ndim: (0,) * n, pipeline_mode=pl.Buffered(1)
                )
            )
            self.args.append(a)

    def after(self, *arrays):
        for a in arrays:
            self.ins.append(pl.BlockSpec(memory_space=pl.ANY))
            self.args.append(a)

    def out_part(self, batches, start, *dims, dtype=BF):
        last = self.batches - 1
        n = len(dims)
        self.outs.append(
            pl.BlockSpec(
                (1,) + dims, lambda m, place: (jnp.minimum(m, last) + start,) + (0,) * n
            )
        )
        self.shapes.append(jax.ShapeDtypeStruct((batches,) + dims, dtype))

    def out(self, *dims, dtype=BF):
        last = self.batches - 1
        n = len(dims)
        self.outs.append(
            pl.BlockSpec(
                (self.group,) + dims, lambda m, place: (jnp.minimum(m, last),) + (0,) * n
            )
        )
        self.shapes.append(jax.ShapeDtypeStruct((self.batches * self.group,) + dims, dtype))

    def out_columns(self, rows, cols, dtype=BF):
        last = self.batches - 1
        self.outs.append(pl.BlockSpec((rows, cols), lambda m, place: (0, jnp.minimum(m, last))))
        self.shapes.append(jax.ShapeDtypeStruct((rows, self.batches * cols), dtype))

    def out_any(self, *dims, dtype=BF):
        self.outs.append(pl.BlockSpec(memory_space=pl.ANY))
        self.shapes.append(jax.ShapeDtypeStruct(dims, dtype))

    def out_whole(self, *dims, dtype=BF):
        self.outs.append(
            pl.BlockSpec(
                dims, lambda m, place: (0,) * len(dims), pipeline_mode=pl.Buffered(1)
            )
        )
        self.shapes.append(jax.ShapeDtypeStruct(dims, dtype))

    def call(self, kernel, place, name, vmem, steps=None, scratch=(), flops=0, moved=0, alias=None):
        return pl.pallas_call(
            kernel,
            grid_spec=pltpu.PrefetchScalarGridSpec(
                num_scalar_prefetch=1,
                grid=(self.batches if steps is None else steps,),
                in_specs=self.ins,
                out_specs=self.outs,
                scratch_shapes=list(scratch),
            ),
            out_shape=self.shapes,
            input_output_aliases={} if alias is None else alias,
            compiler_params=pltpu.CompilerParams(vmem_limit_bytes=vmem * MIB),
            cost_estimate=pl.CostEstimate(
                flops=flops // 10, bytes_accessed=moved // 10, transcendentals=0
            ),
            name=name,
        )(place, *self.args)


def in_turn(units, first, mid, last):
    begun, middle, n = {}, {}, len(units)
    for i in range(-1, n + 1):
        if i + 1 < n:
            begun[i + 1] = first(*units[i + 1])
        if i >= 1:
            last(*units[i - 1], begun.pop(i - 1), middle.pop(i - 1))
        if 0 <= i < n:
            middle[i] = mid(*units[i], begun[i])


def places(b, p):
    here = slice(b * LANES, (b + 1) * LANES)
    return here, slice(b * LANES, b * LANES + SPAN), slice(p * LANES, (p + 1) * LANES)


def attend(q_ref, k_ref, v_ref, p_ref, ctx_ref, pos_row):
    rows, cols = q_ref.shape[1:]
    pos_col = jnp.broadcast_to(pos_row, (LANES, pos_row.shape[1])).T
    biases = []
    for b in range(rows // LANES):
        rel = (
            lax.broadcasted_iota(jnp.int32, (SPAN, LANES), 0)
            - REACH
            - lax.broadcasted_iota(jnp.int32, (SPAN, LANES), 1)
        )
        q_pos = pos_row[:, b * LANES + REACH : (b + 1) * LANES + REACH]
        since = jnp.where(rel > 0, pos_col[b * LANES : b * LANES + SPAN], q_pos)
        far = jnp.abs(rel)
        bias = jnp.where((far <= REACH) & (since >= far), 0.0, masked_score).astype(F32)
        biases.append(jnp.concatenate([bias, bias], axis=1))

    def first(b, p):
        here, span, at = places(b, p)
        return mm(k_ref[0, span, at], both_heads(q_ref[0, here, at]), 1, 1)

    def mid(b, p, scores):
        scores = scores + biases[b]
        e = jnp.exp(scores - jnp.max(scores, axis=0, keepdims=True))
        probs = (e * (1.0 / jnp.sum(e, axis=0, keepdims=True))).astype(BF)
        p_ref[0, b, p] = probs
        return probs

    def last(b, p, _, probs):
        here, span, at = places(b, p)
        ctx_ref[0, here, at] = one_row_each(mm(probs, v_ref[0, span, at], 0, 0)).astype(BF)

    units = [(b, p) for b in range(rows // LANES) for p in range(cols // LANES)]
    in_turn(units, first, mid, last)


def project(normed, w_ref, cos, sin, q_ref, k_ref, v_ref):
    rows, cols = q_ref.shape[1:]
    own = slice(REACH, REACH + rows)
    mixed_q = mm(normed[own], w_ref[0], 1, 0)
    mixed_k = mm(normed, w_ref[1], 1, 0)
    v_ref[0] = mm(normed, w_ref[2], 1, 0).astype(BF)
    for p in range(cols // LANES):
        at = slice(p * LANES, (p + 1) * LANES)
        mq, mk = mixed_q[:, at], mixed_k[:, at]
        q_ref[0, :, at] = (mq * cos[own] + turned(mq) * sin[own]).astype(BF) * SCALE
        k_ref[0, :, at] = (mk * cos + turned(mk) * sin).astype(BF)


def forward_own(
    block, place, x_ref, outer_ref, pos_ref, gain_ref, w_ref, freq_ref, wi_ref, wd_ref,
    normed_ref, at_ref, pos_out_ref, cos_ref, sin_ref, rest_ref,
    q_ref, k_ref, v_ref, p_ref, ctx_ref, x_scr, half_scr, sems,
):
    t, parity = place[0], place[1]
    more = wi_ref.shape[1] // 2
    part = pl.ds(pl.multiple_of(parity * more, 16), more)
    sources = [wi_ref.at[0, part], wi_ref.at[1, part], wd_ref.at[part]]
    held = [half_scr.at[i * more : (i + 1) * more] for i in range(3)]
    targets = [rest_ref.at[i * more : (i + 1) * more] for i in range(3)]
    reads = [pltpu.make_async_copy(a, b, sems.at[i]) for i, (a, b) in enumerate(zip(sources, held))]
    writes = [
        pltpu.make_async_copy(a, b, sems.at[3 + i]) for i, (a, b) in enumerate(zip(held, targets))
    ]
    m = pl.program_id(0)

    @pl.when(m == 0)
    def _():
        for copy in reads:
            copy.start()

    @pl.when(m == 1)
    def _():
        for copy in reads:
            copy.wait()
        for copy in writes:
            copy.start()

    @pl.when(m == pl.num_programs(0) - 1)
    def _():
        for copy in writes:
            copy.wait()

    rows, ext = q_ref.shape[1], k_ref.shape[1]
    inner = rows + REACH
    x_scr[pl.ds(pl.multiple_of((1 - t) * REACH, 16), inner), :] = x_ref[
        0, pl.ds(pl.multiple_of(t * (rows - REACH), 16), inner), :
    ]
    x_scr[pl.ds(pl.multiple_of(t * inner, 16), REACH), :] = outer_ref[0, :REACH]
    pos = pos_ref[0]
    digits = outer_ref[0, REACH:].astype(F32)[:1, : 2 * REACH]
    pos_outer = (digits[:, :REACH] * DIGIT + digits[:, REACH:]).astype(jnp.int32)
    pos_row = jnp.where(
        t == 0,
        jnp.concatenate([pos_outer, pos[:, :inner]], axis=1),
        jnp.concatenate([pos[:, rows - REACH :], pos_outer], axis=1),
    )
    pos_out_ref[0] = pos_row
    xhat, _ = norm_parts(x_scr[...].astype(F32))
    normed = (xhat * gain_ref[...]).astype(BF)
    normed_ref[0] = normed
    transpose_into(at_ref, slice(None), normed, block, parity)
    angles = freq_ref[...] * pos_row.astype(F32)
    c, s = jnp.cos(angles), jnp.sin(angles)
    cos = jnp.concatenate([c, c, c, c], axis=0).T
    sin = jnp.concatenate([-s, s, -s, s], axis=0).T
    cos_ref[0] = cos
    sin_ref[0] = sin
    project(normed, w_ref, cos, sin, q_ref, k_ref, v_ref)
    attend(q_ref, k_ref, v_ref, p_ref, ctx_ref, pos_row)


def forward_peer(
    place, normed_ref, pos_ref, cos_ref, sin_ref, mine_ref, other_ref,
    q_ref, k_ref, v_ref, p_ref, ctx_ref, w_scr,
):
    @pl.when(pl.program_id(0) == 0)
    def _():
        join(w_scr, mine_ref.at[:3], other_ref.at[:3], place[1], mine_ref.shape[1])

    project(normed_ref[0], w_scr, cos_ref[0], sin_ref[0], q_ref, k_ref, v_ref)
    attend(q_ref, k_ref, v_ref, p_ref, ctx_ref, pos_ref[0])


def attention_outs(s, rows, ext, cols):
    s.out(rows, cols)
    s.out(ext, cols)
    s.out(ext, cols)
    s.out(rows // LANES, cols // LANES, SPAN, 2 * LANES)
    s.out(rows, cols)


def split_units(units):
    return units // LANES * LANES, units % LANES


def flat(ref):
    return ref[...].reshape(-1, ref.shape[2])


def hidden_units(nf, cot, gate_w, up_w, down_w, count, here, act_s, gg_s, gu_s):
    def first(at):
        return mm(nf, gate_w[at], 1, 1), mm(nf, up_w[at], 1, 1), mm(cot, down_w[at], 1, 1)

    def mid(at, begun):
        g, u, ga = begun
        cdf = 0.5 * (1.0 + lax.erf(g * 0.5**0.5))
        gelu = g * cdf
        slope = cdf + g * jnp.exp(-0.5 * g * g) * 0.3989422804014327
        act_s[here, at] = (gelu * u).astype(BF)
        gg_s[here, at] = (ga * u * slope).astype(BF)
        gu_s[here, at] = (ga * gelu).astype(BF)

    step = 2 * LANES
    chunks = [(slice(c, min(c + step, count)),) for c in range(0, count, step)]
    in_turn(chunks, first, mid, lambda *_: None)


def ffn_own_kernel(
    block, place, x_ref, cot_ref, ctx0_ref, ctx1_ref, gain_ref, wo_ref, wi_ref, wd_ref,
    wo_mine, wo_other, state_ref, out_ref, grad_ref, keep_ref, send_ref, keep_down, send_down,
    wo, nft, cott, gg_s, gu_s, act_s,
):
    m = pl.program_id(0)
    parity = place[1]
    steps = pl.num_programs(0) - 1
    main = gg_s.shape[1]
    group, rows, width = x_ref.shape
    rows = group * rows

    @pl.when(m == 0)
    def _():
        cols = wo_ref.shape[0]
        wo[:cols] = wo_ref[...]
        join_out(wo.at[cols:], wo_mine.at[0], wo_other.at[0], parity)

    @pl.when(m < steps)
    def _():
        here = pl.ds(pl.multiple_of(m * rows, 16), rows)
        along = pl.ds(pl.multiple_of(m * rows, LANES), rows)
        ctx = jnp.concatenate([flat(ctx0_ref), flat(ctx1_ref)], axis=1)
        state = flat(x_ref).astype(F32) + mm(ctx, wo[...], 1, 0)
        state_ref[...] = state.reshape(state_ref.shape)
        nf = (norm_parts(state)[0] * gain_ref[...]).astype(BF)
        transpose_into(nft, along, nf, block, parity)
        cot = flat(cot_ref)
        transpose_into(cott, along, cot, block, parity)
        hidden_units(nf, cot, wi_ref.at[0], wi_ref.at[1], wd_ref, main, here, act_s, gg_s, gu_s)
        out = mm(act_s[here, :], wd_ref[:main], 1, 0)
        out_ref[...] = out.astype(BF).reshape(out_ref.shape)
        grad = mm(gg_s[here, :], wi_ref[0, :main], 1, 0) + mm(gu_s[here, :], wi_ref[1, :main], 1, 0)
        grad_ref[...] = grad.astype(BF).reshape(grad_ref.shape)

    @pl.when(m == steps)
    def _():
        for j, to_ref, down_ref in ((0, keep_ref, keep_down), (1, send_ref, send_down)):
            at = slice(j * width // 2, (j + 1) * width // 2)
            to_ref[:, :main] = mm(nft[at], gg_s[...], 1, 0).astype(BF)
            to_ref[:, main:] = mm(nft[at], gu_s[...], 1, 0).astype(BF)
            down_ref[...] = mm(cott[at], act_s[...], 1, 0).astype(BF)


def ffn_peer_kernel(
    block, place, state_ref, out_ref, grad_ref, cot_ref, ctx0_ref, ctx1_ref, gain_ref,
    wi_tail, wd_tail, mine_ref, other_ref, keep_down, send_down, y_ref, mix_ref, gain_out,
    keep_a, keep_b, send_a, send_b,
    half, gate_w, up_w, down_w, nft, cott, mixt, gg_s, gu_s, act_s, ctx_s,
):
    m = pl.program_id(0)
    parity = place[1]
    steps = pl.num_programs(0) - 1
    units = half.shape[0]
    main, rest = split_units(units)
    group, rows, width = state_ref.shape
    rows = group * rows

    @pl.when(m == 0)
    def _():
        for j, (full, own) in enumerate(
            ((gate_w, wi_tail.at[0]), (up_w, wi_tail.at[1]), (down_w, wd_tail))
        ):
            part = slice(j * (units // 2), (j + 1) * (units // 2))
            join(half, mine_ref.at[part], other_ref.at[part], parity, units // 2)
            full[:main] = half[:main]
            full[main : main + rest] = own[...]
            full[main + rest :] = half[main:]
        gain_out[...] = jnp.zeros_like(gain_out)

    @pl.when(m < steps)
    def _():
        here = pl.ds(pl.multiple_of(m * rows, 16), rows)
        along = pl.ds(pl.multiple_of(m * rows, LANES), rows)
        ctx_s[here, :] = jnp.concatenate([flat(ctx0_ref), flat(ctx1_ref)], axis=1)
        state = flat(state_ref)
        xhat, r = norm_parts(state)
        gain = gain_ref[...]
        nf = (xhat * gain).astype(BF)
        transpose_into(nft, along, nf, block, parity)
        cot = flat(cot_ref)
        transpose_into(cott, along, cot, block, parity)
        hidden_units(nf, cot, gate_w, up_w, down_w, main + 2 * rest, here, act_s, gg_s, gu_s)
        out = state + flat(out_ref).astype(F32) + mm(act_s[here, :], down_w[...], 1, 0)
        y_ref[...] = out.astype(BF).reshape(y_ref.shape)
        grad = flat(grad_ref).astype(F32) + mm(gg_s[here, :], gate_w[...], 1, 0)
        grad = grad + mm(gu_s[here, :], up_w[...], 1, 0)
        gain_out[...] += jnp.sum(grad * xhat, axis=0, keepdims=True)
        mix = (cot.astype(F32) + norm_back(xhat, r, grad * gain)).astype(BF)
        mix_ref[...] = mix.reshape(mix_ref.shape)
        transpose_into(mixt, along, mix, block, parity)

    @pl.when(m == steps)
    def _():
        cols = ctx0_ref.shape[2]
        zero = jnp.zeros((width // 2, rest), BF)
        for j, a_ref, b_ref, down_ref in (
            (0, keep_a, keep_b, keep_down),
            (1, send_a, send_b, send_down),
        ):
            at = slice(j * width // 2, (j + 1) * width // 2)
            ends = []
            for at_ref, hidden, to_ref in (
                (nft, gg_s, a_ref.at[:, :main]),
                (nft, gu_s, a_ref.at[:, main:]),
                (cott, act_s, b_ref.at[1, :, :main]),
            ):
                to_ref[...] = mm(at_ref[at], hidden[:, :main], 1, 0).astype(BF)
                ends.append(mm(at_ref[at], hidden[:, main:], 1, 0).astype(BF))
            b_ref[0, :, :main] = down_ref[...]
            out = mm(mixt[at], ctx_s[...], 1, 0).astype(BF)
            for i in range(2):
                part = slice(i * rest, (i + 1) * rest)
                b_ref[i, :, main : main + cols] = out[:, i * cols : (i + 1) * cols]
                b_ref[i, :, main + cols :] = jnp.concatenate(
                    [end[:, part] for end in ends] + [zero], axis=1
                )


def backward_kernel(plan, place, mix_ref, *rest):
    peer, sums, ends = plan["peer"], plan["sums"], plan["ends"]
    rest = list(rest)
    first_ref, second_ref = rest.pop(0), rest.pop(0)
    q_ref, k_ref, v_ref, p_ref, cos_ref, sin_ref = rest[:6]
    rest = rest[6:]
    before_ref = rest.pop(0) if plan["adds"] else None
    if ends:
        normed_ref = rest.pop(0)
    if sums:
        at_ref = rest.pop(0)
    gm_before = rest.pop(0) if plan["earlier"] else None
    gain_sums = None
    if plan["gains"]:
        gain_sums = rest.pop(0), rest.pop(0)
    rest = rest[plan["after"] :]
    nag_ref = rest.pop(0)
    if ends:
        inner_ref, outer_ref = rest.pop(0), rest.pop(0)
    if sums:
        keep_ref, send_ref = rest.pop(0), rest.pop(0)
    else:
        gm_out = rest.pop(0)
    gm_ref = rest.pop(0)
    if ends:
        gain_out = rest.pop(0)
    m = pl.program_id(0)
    if peer:
        wo_scr, w_scr = rest

        @pl.when(m == 0)
        def _():
            join_out(wo_scr, first_ref.at[3], second_ref.at[3], place[1])
            rows = first_ref.shape[1]
            join(w_scr, first_ref.at[:3], second_ref.at[:3], place[1], rows)

        wo_ref, w_ref = wo_scr, w_scr
    else:
        wo_ref, w_ref = first_ref, second_ref
    rows, cols = q_ref.shape[1:]
    ext = k_ref.shape[1]
    own = slice(REACH, REACH + rows)

    def one_batch():
        dctx = mm(mix_ref[0], wo_ref[...], 1, 1).astype(BF)
        cos, sin = cos_ref[0], sin_ref[0]
        gm_ref[m, :REACH, :cols] = jnp.zeros((REACH, cols), BF)
        gm_ref[m, REACH + rows :, :cols] = jnp.zeros((REACH, cols), BF)
        blocks = rows // LANES
        key_parts, value_parts = {}, {}

        def first(b, p):
            here, span, at = places(b, p)
            grad = both_heads(dctx[here, at])
            return grad, mm(v_ref[0, span, at], grad, 1, 1)

        def mid(b, p, begun):
            probs = p_ref[0, b, p].astype(F32)
            weighted = probs * begun[1]
            balance = jnp.sum(weighted, axis=0, keepdims=True)
            return (weighted - probs * balance).astype(BF)

        def over_blocks(parts, p):
            out = []
            for b in range(blocks + 1):
                piece = None
                if b < blocks:
                    piece = parts[b, p][:LANES]
                if b > 0:
                    more = parts[b - 1, p][LANES:]
                    piece = more if piece is None else piece + more
                out.append(piece)
            return jnp.concatenate(out, axis=0)

        def end(b, p, begun, grad_scores):
            here, span, at = places(b, p)
            there = slice(b * LANES + REACH, (b + 1) * LANES + REACH)
            value_parts[b, p] = mm(p_ref[0, b, p], begun[0], 1, 0)
            key_parts[b, p] = mm(grad_scores, both_heads(q_ref[0, here, at]), 1, 0)
            dq = one_row_each(mm(grad_scores, k_ref[0, span, at], 0, 0)) * SCALE
            gm_ref[m, there, at] = (dq * cos[there] - turned(dq) * sin[there]).astype(BF)
            if b == blocks - 1:
                dk = over_blocks(key_parts, p)
                gm_ref[m, :, cols + p * LANES : cols + (p + 1) * LANES] = (
                    dk * cos - turned(dk) * sin
                ).astype(BF)
                dv = over_blocks(value_parts, p).astype(BF)
                gm_ref[m, :, 2 * cols + p * LANES : 2 * cols + (p + 1) * LANES] = dv

        units = [(b, p) for p in range(cols // LANES) for b in range(blocks)]
        in_turn(units, first, mid, end)
        nag = mm(gm_ref[m, :, cols : 2 * cols], w_ref[1], 1, 1)
        nag = nag + mm(gm_ref[m, :, 2 * cols :], w_ref[2], 1, 1)
        nag_q = mm(gm_ref[m, own, :cols], w_ref[0], 1, 1)
        if before_ref is not None:
            nag = nag + before_ref[0].astype(F32)
        if not ends:
            nag_ref[0, :REACH] = nag[:REACH].astype(BF)
            nag_ref[0, own] = (nag[own] + nag_q).astype(BF)
            nag_ref[0, REACH + rows :] = nag[REACH + rows :].astype(BF)
        else:
            left = nag[:REACH].astype(BF)
            right = nag[REACH + rows :].astype(BF)
            inner_ref[0] = jnp.where(place[0] == 0, right, left)
            outer_ref[0] = jnp.where(place[0] == 0, left, right)
            nag_own = nag[own] + nag_q
            nag_ref[0] = nag_own.astype(BF)
            normed = normed_ref[0].astype(F32)
            total = (
                jnp.sum(nag[:REACH] * normed[:REACH], axis=0, keepdims=True)
                + jnp.sum(nag_own * normed[own], axis=0, keepdims=True)
                + jnp.sum(nag[REACH + rows :] * normed[REACH + rows :], axis=0, keepdims=True)
            )

            @pl.when(m == 0)
            def _():
                gain_out[...] = total

            @pl.when(m > 0)
            def _():
                gain_out[...] += total

        if not sums:
            gm_out[0] = gm_ref[m]

    if not sums:
        one_batch()
        return
    steps = pl.num_programs(0) - 1
    pl.when(m < steps)(one_batch)

    @pl.when(m == steps)
    def _():
        half = at_ref.shape[0] // 2
        two = gm_ref[...].reshape(-1, 3 * cols)
        earlier = at_ref.shape[1] - two.shape[0]
        moves = []
        for lo, hi in plan["order"]:
            for j in range(3):
                moves.append((j * cols + lo * LANES, j * cols + hi * LANES))
        for j, to in ((0, keep_ref), (1, send_ref)):
            at = slice(j * half, (j + 1) * half)
            total = mm(at_ref[at, earlier:], two, 1, 0)
            if gm_before is not None:
                one = gm_before[...].reshape(earlier, 3 * cols)
                total = total + mm(at_ref[at, :earlier], one, 1, 0)
            total = total.astype(BF)
            into = 0
            for lo, hi in moves:
                to[:half, into : into + hi - lo] = total[:, lo:hi]
                into += hi - lo
            if gain_sums is not None:
                gain_ref, ffn_ref = gain_sums
                width, wide = gain_ref.shape[1], to.shape[1]
                attn = gain_out[...] / gain_ref[...]
                zero = jnp.zeros((MORE - 2, width), F32)
                gains = jnp.concatenate([attn, ffn_ref[...], zero], axis=0).astype(BF)
                for i in range(width // wide):
                    to[half + i * MORE : half + (i + 1) * MORE] = gains[:, i * wide : (i + 1) * wide]


def last_kernel(edges, place, x_ref, nag_ref, mix_ref, gain_ref, *rest):
    out_ref = rest[-1]
    gain = gain_ref[...]
    if edges:
        inner_ref, outer_ref = rest[:2]
        use_inner = (place[0] == 0) == (pl.program_id(0) == 1)
    step = 32
    for i in range(nag_ref.shape[0]):
        for c in range(0, REACH, step):
            at = slice(c, c + step)
            xhat, r = norm_parts(x_ref[i, at].astype(F32))
            nag = nag_ref[i, at].astype(F32)
            if edges:
                nag = nag + jnp.where(use_inner, inner_ref[i, at], outer_ref[i, at]).astype(F32)
            out_ref[i, at] = mix_ref[i, at].astype(F32) + norm_back(xhat, r, nag * gain)


def swap(x, axis, bit):
    size = lax.axis_size(axis)
    return lax.ppermute(x, axis, [(i, i ^ bit) for i in range(size)])


def then(value, *earlier):
    return lax.optimization_barrier((value, *earlier))[0]


def quarter(half, axis):
    rows = half.shape[axis] // 2
    return lax.dynamic_slice_in_dim(half, (lax.axis_index("dp") % 2) * rows, rows, axis)


class Halving:
    def __init__(self, total, rows, bit, beside=None):
        self.mine = (lax.axis_index("dp") // bit) % 2
        self.g = total.astype(BF).reshape(-1, 2, rows, total.shape[-1])
        self.sent = lax.dynamic_index_in_dim(self.g, 1 - self.mine, 1, keepdims=False)
        self.beside = beside
        if beside is not None:
            self.sent = jnp.concatenate([self.sent.reshape(-1, total.shape[-1]), beside])
        self.got = swap(self.sent, "dp", bit)

    def total(self, *earlier):
        keep = lax.dynamic_index_in_dim(self.g, self.mine, 1, keepdims=False)
        got = (then(self.got, *earlier) if earlier else self.got).astype(F32)
        if self.beside is None:
            total = keep.astype(F32) + got
            return total.reshape(-1, total.shape[-1])
        keep = keep.astype(F32).reshape(-1, got.shape[-1])
        more = self.beside.shape[0]
        return keep + got[:-more], self.beside.astype(F32) + got[-more:]


def sum_from(total, rows, bit, size):
    while bit < size:
        total = Halving(total, rows, bit).total()
        bit *= 2
    return total


def sorted_halves(keep, send, block, size):
    if block is not None:
        return keep, send
    n, half, cols = keep.shape
    g = jnp.concatenate([keep, send], axis=1).reshape(n, size // 2, 2, 2 * half // size, cols)
    parity = lax.axis_index("dp") % 2
    keep = lax.dynamic_index_in_dim(g, parity, 2, keepdims=False)
    send = lax.dynamic_index_in_dim(g, 1 - parity, 2, keepdims=False)
    return keep.reshape(n, half, cols), send.reshape(n, half, cols)


def on_device(
    inputs, positions, cotangent, gain_attn, gain_ffn, w_qkv, w_out, w_in, down_projection_weight
):
    batches, row_count, width = inputs.shape
    parts, t = lax.axis_size("tensor"), lax.axis_index("tensor")
    dp = lax.axis_size("dp")
    rows = row_count // parts
    ext = rows + 2 * REACH
    cols = w_qkv.shape[2]
    units = w_in.shape[2]
    place = jnp.stack([t, lax.axis_index("dp") % 2]).astype(jnp.int32)
    mine = width // dp
    block = mine if mine % 16 == 0 else None

    qkv = w_qkv.transpose(1, 0, 2)
    w_in = w_in.transpose(1, 2, 0)
    w_down = down_projection_weight
    out_mine = quarter(w_out, 0)
    qkv_mine = jnp.concatenate(
        [
            quarter(qkv, 1),
            jnp.concatenate([out_mine[:, :cols], out_mine[:, cols:]])[None],
        ]
    )
    at = jnp.where(t == 0, row_count - REACH, 0)
    edge = lax.dynamic_slice_in_dim(positions, at, REACH, 1)
    digits = jnp.concatenate([edge // DIGIT, edge % DIGIT], axis=1).astype(BF)
    digits = jnp.pad(digits, ((0, 0), (0, width - 2 * REACH)))
    edge = jnp.concatenate(
        [
            lax.dynamic_slice_in_dim(then(inputs, qkv_mine), at, REACH, 1),
            jnp.broadcast_to(digits[:, None, :], (batches, MORE, width)),
        ],
        axis=1,
    )
    qkv_mine = swap(qkv_mine, "tensor", 1)
    perm = [(2 * i, 2 * i + 2) for i in range(dp - 1)]
    perm += [(2 * i + 3, 2 * i + 1) for i in range(dp - 1)]
    x_outer = lax.ppermute(edge, ("dp", "tensor"), perm)
    freq = jnp.asarray(
        np.power(
            np.float32(rope_base),
            -np.arange(HEAD_DIM // 2, dtype=np.float32) * np.float32(2.0 / HEAD_DIM),
        )[:, None]
    )

    work = 2 * batches * ext * width * 3 * cols + 8 * batches * rows * cols * SPAN
    s = Specs(batches)
    s.per(inputs)
    s.per(x_outer)
    s.per(positions[:, None, :])
    s.whole(gain_attn[None, :], qkv, freq)
    s.after(w_in, w_down)
    s.out(ext, width)
    s.out_columns(width, ext)
    s.out(1, ext, dtype=jnp.int32)
    s.out(ext, LANES, dtype=F32)
    s.out(ext, LANES, dtype=F32)
    s.out_any(units + units // 2, width)
    attention_outs(s, rows, ext, cols)
    normed, normed_t, pos_ext, cos, sin, rest_mine, q0, k0, v0, p0, ctx0 = s.call(
        functools.partial(forward_own, block), place, "attn_fwd_own", 60,
        scratch=[
            pltpu.VMEM((ext, width), BF),
            pltpu.VMEM((units + units // 2, width), BF),
            pltpu.SemaphoreType.DMA((6,)),
        ],
        flops=work, moved=20 * batches * ext * width,
    )

    qkv_other = swap(then(qkv_mine, ctx0), "dp", 1)
    rest_mine = swap(rest_mine, "tensor", 1)
    s = Specs(batches)
    for a in (normed, pos_ext, cos, sin):
        s.per(a)
    s.whole(qkv_mine, qkv_other)
    attention_outs(s, rows, ext, cols)
    q1, k1, v1, p1, ctx1 = s.call(
        forward_peer, place, "attn_fwd_peer", 60,
        scratch=[pltpu.VMEM((3, width, cols), BF)], flops=work, moved=20 * batches * ext * cols,
    )

    own_block = (rows, width)
    group = 2 if batches % 2 == 0 else 1
    main, rest = split_units(units)
    in_cols = 2 * main
    own_place = lambda place: (place[0], 0)
    s = Specs(batches, group)
    s.per(inputs, own_block, own_place)
    s.per(cotangent, own_block, own_place)
    s.per(ctx0)
    s.per(ctx1)
    s.whole(gain_ffn[None, :], w_out)
    s.ins.append(pl.BlockSpec((2, main, width), lambda m, place: (0, 0, 0)))
    s.ins.append(pl.BlockSpec((main, width), lambda m, place: (0, 0)))
    s.args += [w_in, w_down]
    for a in (qkv_mine, qkv_other):
        s.ins.append(pl.BlockSpec((1, cols, cols), lambda m, place: (3, 0, 0)))
        s.args.append(a)
    s.out(rows, width, dtype=F32)
    s.out(rows, width)
    s.out(rows, width)
    for cols_of in (2 * main, 2 * main, main, main):
        s.out_whole(width // 2, cols_of)
    state, part_out, part_grad, keep, send, keep_down, send_down = s.call(
        functools.partial(ffn_own_kernel, block), place, "ffn_own", 52, steps=s.batches + 1,
        scratch=[pltpu.VMEM((2 * cols, width), BF)]
        + [pltpu.VMEM((width, batches * rows), BF)] * 2
        + [pltpu.VMEM((batches * rows, main), BF)] * 3,
        flops=2 * batches * rows * width * (9 * main + 2 * cols), moved=3 * 10**7,
    )
    own_keep, send = sorted_halves(keep[None], send[None], block, dp)
    own_got = swap(send[0], "dp", 1)
    rest_other = swap(then(rest_mine, state), "dp", 1)
    s = Specs(batches, group)
    for a in (state, part_out, part_grad):
        s.per(a)
    s.per(cotangent, own_block, own_place)
    s.per(ctx0)
    s.per(ctx1)
    s.whole(gain_ffn[None, :])
    s.ins.append(pl.BlockSpec((2, rest, width), lambda m, place: (0, main // rest, 0)))
    s.ins.append(pl.BlockSpec((rest, width), lambda m, place: (main // rest, 0)))
    s.args += [w_in, w_down]
    s.whole(rest_mine, rest_other, keep_down, send_down)
    s.out(rows, width)
    s.out(rows, width)
    s.out_whole(1, width, dtype=F32)
    for _ in range(2):
        s.out_whole(width // 2, in_cols)
        s.out_whole(2, width // 2, main + cols + 4 * rest)
    y, mix, gain_ffn_part, keep_a, keep_b, send_a, send_b = s.call(
        functools.partial(ffn_peer_kernel, block), place, "ffn_peer", 52, steps=s.batches + 1,
        scratch=[pltpu.VMEM((units, width), BF)]
        + [pltpu.VMEM((main + 2 * rest, width), BF)] * 3
        + [pltpu.VMEM((width, batches * rows), BF)] * 3
        + [pltpu.VMEM((batches * rows, main + 2 * rest), BF)] * 3
        + [pltpu.VMEM((batches * rows, 2 * cols), BF)],
        flops=2 * batches * rows * width * (9 * (main + 2 * rest) + 2 * cols), moved=4 * 10**7,
    )
    keep_a, send_a = sorted_halves(keep_a[None], send_a[None], block, dp)
    keep_b, send_b = sorted_halves(keep_b, send_b, block, dp)
    got_a, got_b = swap(send_a[0], "dp", 1), swap(send_b, "dp", 1)

    def backward(name, peer, batch, pairs, nag=None, into=None, sums=False, gm=None, after=(), gains=()):
        start, stop = batch
        part, count = stop - start, pairs[1] - pairs[0]
        n, at, all_pairs = count * LANES, pairs[0] // count, cols // LANES
        ends = not peer and pairs[1] == all_pairs
        s = Specs(part)
        s.per(mix, start=start)
        if peer:
            s.whole(qkv_mine, qkv_other)
        else:
            s.ins.append(pl.BlockSpec((n, width), lambda m, place: (at, 0)))
            s.ins.append(pl.BlockSpec((3, width, n), lambda m, place: (0, 0, at)))
            s.args += [w_out, qkv]
        q, k, v, p = (q1, k1, v1, p1) if peer else (q0, k0, v0, p0)
        for a in (q, k, v):
            s.per(a, (a.shape[1], n), lambda place: (0, at), start=start)
        s.per(p, (p.shape[1], count) + p.shape[3:], lambda place: (0, at, 0, 0), start=start)
        s.per(cos, start=start)
        s.per(sin, start=start)
        if nag is not None:
            s.per(nag, start=start)
        if ends:
            s.per(normed, start=start)
        if sums:
            s.whole(normed_t)
        if gm is not None:
            s.whole(gm)
        s.whole(*gains)
        s.after(*after)
        scratch = [pltpu.VMEM((part, ext, 3 * n), BF)]
        alias = None
        if into is not None:
            s.after(into)
            alias = {len(s.args): 0}
        if ends:
            s.out(rows, width)
            s.out(REACH, width)
            s.out(REACH, width)
            scratch.append(pltpu.VMEM((1, width), F32))
        else:
            s.out_part(batches, start, ext, width)
        if sums:
            more = MORE * width // (3 * n) if gains else 0
            s.out_whole(width // 2 + more, 3 * n)
            s.out_whole(width // 2 + more, 3 * n)
        else:
            s.out(ext, 3 * n)
        if peer:
            scratch += [pltpu.VMEM((cols, width), BF), pltpu.VMEM((3, width, cols), BF)]
        plan = dict(
            peer=peer, sums=sums, ends=ends, adds=nag is not None, earlier=gm is not None,
            gains=bool(gains), after=len(after) + (into is not None),
            order=((0, all_pairs - 1), (all_pairs - 1, all_pairs)) if peer else ((0, count),),
        )
        return s.call(
            functools.partial(backward_kernel, plan), place, name, 52,
            steps=part + 1 if sums else None, scratch=scratch, alias=alias,
            flops=(2 * ext * width * 4 * n + 20 * rows * n * SPAN) * part,
            moved=30 * part * ext * n,
        )

    def halos(inner, outer):
        pairs = [(2 * i + 1, 2 * i + 2) for i in range(dp - 1)]
        pairs += [(j, i) for i, j in pairs]
        return swap(inner, "tensor", 1), lax.ppermute(outer, ("dp", "tensor"), pairs)

    pairs, part = cols // LANES, batches // 2
    nag1, gm1 = backward("attn_bwd_peer_a", True, (0, 1), (0, pairs))
    got_a, got_b, own_got = lax.optimization_barrier((got_a, got_b, own_got, gm1))[:3]
    a_peer = (keep_a[0].astype(F32) + got_a.astype(F32)).astype(BF)
    a_from_peer = swap(a_peer, "tensor", 1)
    b_sum = Halving((keep_b.astype(F32) + got_b.astype(F32)).reshape(width, -1), mine, 2)
    nag1, keep1, send1 = backward(
        "attn_bwd_peer_b", True, (1, batches), (0, pairs), into=nag1, sums=True, gm=gm1,
        after=(a_peer, b_sum.sent),
    )
    keep1, send1 = sorted_halves(keep1[None], send1[None], block, dp)
    got1 = swap(send1[0], "dp", 1)
    a_from_peer, own_got = lax.optimization_barrier((a_from_peer, own_got, send1))[:2]
    a_sum = own_keep[0].astype(F32) + own_got.astype(F32) + a_from_peer.astype(F32)
    a_sum = Halving(a_sum, mine, 2)
    b_sum = b_sum.total(send1).reshape(2, width // 4, -1)
    b_peer = b_sum[1].astype(BF)
    b_from_peer = swap(b_peer, "tensor", 1)
    got1 = then(got1, a_sum.sent, b_peer)
    peer_sum = Halving(keep1[0].astype(F32) + got1.astype(F32), mine, 2)
    first = (0, pairs - 1)
    nag0, keep2, send2 = backward(
        "attn_bwd_own_a", False, (0, batches), first, nag=nag1, sums=True,
        after=(a_sum.sent, b_peer, peer_sum.sent),
    )
    keep2, send2 = sorted_halves(keep2[None], send2[None], block, dp)
    got2 = swap(send2[0], "dp", 1)
    b_sum = b_sum[0] + then(b_from_peer, send2).astype(F32)
    f_sum = Halving(jnp.concatenate([a_sum.total(send2), b_sum], axis=1), mine, 4)
    peer_sum = peer_sum.total(send2).astype(BF)
    qkv_from_peer = swap(peer_sum, "tensor", 1)
    got2 = then(got2, f_sum.sent, peer_sum)
    own_first = Halving(keep2[0].astype(F32) + got2.astype(F32), mine, 2)
    second = (pairs - 1, pairs)
    nag, to_inner, to_outer, keep3, send3 = backward(
        "attn_bwd_own_b", False, (0, batches), second, nag=nag0, sums=True,
        after=(f_sum.sent, peer_sum, own_first.sent), gains=(gain_attn[None, :], gain_ffn_part),
    )
    beside = keep3[width // 2 :]
    keep3, sorted3 = sorted_halves(
        keep3[None, : width // 2], send3[None, : width // 2], block, dp
    )
    if block is None:
        send3 = jnp.concatenate([sorted3[0], beside])
    gains_peer = swap(beside, "tensor", 1)
    index = [2 * i + j for i in range(dp) for j in range(2)]
    gains_both = lax.ppermute(beside, ("dp", "tensor"), [(i, i ^ 3) for i in index])
    got3 = swap(send3, "dp", 1)
    from_inner = swap(to_inner, "tensor", 1)
    neighbours = [(2 * i + 1, 2 * i + 2) for i in range(dp - 1)]
    neighbours += [(j, i) for i, j in neighbours]
    from_outer = lax.ppermute(to_outer, ("dp", "tensor"), neighbours)

    columns = [LANES * (pairs - 1), LANES]
    wide = [3 * n for n in columns]
    own_first.got, qkv_from_peer, f_sum.got = lax.optimization_barrier(
        (own_first.got, qkv_from_peer, f_sum.got, send3)
    )[:3]
    from_first = qkv_from_peer[:, : wide[0]].astype(F32)
    own_first = Halving(own_first.total() + from_first, mine, 4)
    f_sum = Halving(f_sum.total(), mine, 8)
    got3 = then(got3, own_first.sent, f_sum.sent)
    got3, gains = got3[: width // 2].astype(F32), got3[width // 2 :].astype(F32)
    gains = beside.astype(F32) + gains
    gains = (gains + (gains_peer.astype(F32) + gains_both.astype(F32))).astype(BF)
    own_second = Halving(keep3[0].astype(F32) + got3, mine, 2, gains)

    def finish(edges, after, into, name):
        blocks = rows // REACH
        count, step = (2, blocks - 1) if edges else (blocks - 2, 1)
        begin = 0 if edges else 1

        def spec(arrays, first):
            return pl.BlockSpec(
                (batches, REACH, width), lambda j, place: (0, first(place) + begin + step * j, 0)
            )

        fixed = pl.BlockSpec((batches, REACH, width), lambda j, place: (0, 0, 0))
        args = [inputs, nag, mix, gain_attn[None, :]]
        specs = [
            spec(inputs, lambda place: place[0] * blocks),
            spec(nag, lambda place: 0),
            spec(mix, lambda place: 0),
            pl.BlockSpec((1, width), lambda j, place: (0, 0)),
        ]
        if edges:
            args += [from_inner, from_outer]
            specs += [fixed, fixed]
        more = [*after] if into is None else [*after, into]
        args += more
        specs += [pl.BlockSpec(memory_space=pl.ANY)] * len(more)
        return pl.pallas_call(
            functools.partial(last_kernel, edges),
            grid_spec=pltpu.PrefetchScalarGridSpec(
                num_scalar_prefetch=1,
                grid=(count,),
                in_specs=specs,
                out_specs=spec(nag, lambda place: 0),
            ),
            out_shape=jax.ShapeDtypeStruct((batches, rows, width), F32),
            input_output_aliases={} if into is None else {len(args): 0},
            compiler_params=pltpu.CompilerParams(vmem_limit_bytes=48 * MIB),
            cost_estimate=pl.CostEstimate(flops=10**8, bytes_accessed=10**6, transcendentals=0),
            name=name,
        )(place, *args)

    input_grad = finish(False, (own_second.sent,), None, "input_grad_inside")
    own_first.got, own_second.got = lax.optimization_barrier(
        (own_first.got, own_second.got, input_grad)
    )[:2]
    total, gains = own_second.total()
    gains = gains.astype(BF)
    own_second = Halving(
        total + qkv_from_peer[:, wide[0] :].astype(F32), mine, 4, gains
    )
    own_first = Halving(then(own_first.total(), own_second.sent), mine, 8)
    total, gains = own_second.total()
    bit = 8
    while bit < dp:
        own_second = Halving(total, mine, bit, gains.astype(BF))
        last_sent = own_second.sent
        total, gains = own_second.total()
        bit *= 2
    second_sum = total
    gains = gains.reshape(-1, MORE, wide[1])[:, :2].transpose(1, 0, 2).reshape(2, width)

    input_grad = finish(True, (last_sent, own_first.sent), input_grad, "input_grad_edges")
    own_first.got, f_sum.got = lax.optimization_barrier(
        (own_first.got, f_sum.got, last_sent)
    )[:2]
    first_sum = sum_from(own_first.total(), mine, 16, dp)
    f_sum = sum_from(f_sum.total(), mine, 16, dp)
    qkv_sum = jnp.stack(
        [
            jnp.concatenate(
                [a[:, j * n : (j + 1) * n] for a, n in zip((first_sum, second_sum), columns)], axis=1
            )
            for j in range(3)
        ]
    ).transpose(1, 0, 2)

    def unit_columns(j):
        tail = 3 * main + cols + j * rest
        return jnp.concatenate(
            [f_sum[:, j * main : (j + 1) * main], f_sum[:, tail : tail + rest]], axis=1
        )

    return (
        y,
        input_grad,
        qkv_sum,
        f_sum[:, 3 * main : 3 * main + cols].T,
        jnp.stack([unit_columns(0), unit_columns(1)], axis=1),
        unit_columns(2).T,
        gains[0],
        gains[1],
    )


def solution(mesh):
    placed = (
        P(None, "dp", None),
        P(None, "dp"),
        P(None, "dp", None),
        P(),
        P(),
        P(None, None, "tensor"),
        P("tensor", None),
        P(None, None, "tensor"),
        P("tensor", None),
    )
    return jax.shard_map(
        on_device,
        mesh=mesh,
        in_specs=placed,
        out_specs=(
            P(None, ("dp", "tensor"), None),
            P(None, ("dp", "tensor"), None),
            P("dp", None, "tensor"),
            P("tensor", "dp"),
            P("dp", None, "tensor"),
            P("tensor", "dp"),
            P(),
            P(),
        ),
        check_vma=False,
    )
```

```python
import functools

import jax
import jax.numpy as jnp
import numpy as np
from jax import lax
from jax.experimental import pallas as pl
from jax.experimental.pallas import tpu as pltpu
from jax.sharding import PartitionSpec as P

HEAD_DIM = 64
WINDOW = 128
REACH = WINDOW // 2
LANES = 128
SPAN = LANES + 2 * REACH
SCALE = HEAD_DIM**-0.5
DIGIT = 64
MORE = 16

norm_eps = 1e-05
rope_base = 10000.0
masked_score = -1e30

BF = jnp.bfloat16
F32 = jnp.float32
MIB = 2**20


def mm(a, b, ca, cb):
    return lax.dot_general(a, b, (((ca,), (cb,)), ((), ())), preferred_element_type=F32)


def turned(v):
    lane = lax.broadcasted_iota(jnp.int32, v.shape, 1)
    low = (lane & 63) < 32
    return jnp.where(low, pltpu.roll(v, 96, 1), pltpu.roll(v, 32, 1))


def both_heads(v):
    lane = lax.broadcasted_iota(jnp.int32, v.shape, 1)
    zero = jnp.zeros_like(v)
    return jnp.concatenate(
        [jnp.where(lane < HEAD_DIM, v, zero), jnp.where(lane >= HEAD_DIM, v, zero)], axis=0
    )


def one_row_each(v):
    rows = v.shape[0] // 2
    lane = lax.broadcasted_iota(jnp.int32, (rows, v.shape[1]), 1)
    return jnp.where(lane < HEAD_DIM, v[:rows], v[rows:])


def norm_parts(v):
    centred = v - jnp.mean(v, axis=1, keepdims=True)
    spread = jnp.mean(centred * centred, axis=1, keepdims=True)
    r = lax.rsqrt(spread + norm_eps)
    return centred * r, r


def norm_back(xhat, r, e):
    return r * (
        e - jnp.mean(e, axis=1, keepdims=True) - xhat * jnp.mean(e * xhat, axis=1, keepdims=True)
    )


def transpose_into(at_ref, at, v, block, parity):
    vt = v.T
    width = vt.shape[0]
    if block is None:
        at_ref[:, at] = vt
        return
    for i in range(width // block):
        odd = parity if i % 2 == 0 else 1 - parity
        to = pl.multiple_of((i // 2) * block + odd * (width // 2), 16)
        at_ref[pl.ds(to, block), at] = vt[i * block : (i + 1) * block]


def join(own_ref, mine_ref, other_ref, parity, rows):
    own_ref[..., pl.ds(pl.multiple_of(parity * rows, 16), rows), :] = mine_ref[...]
    own_ref[..., pl.ds(pl.multiple_of((1 - parity) * rows, 16), rows), :] = other_ref[...]


def join_out(own_ref, mine_ref, other_ref, parity):
    rows = mine_ref.shape[0] // 2
    for ref, place in ((mine_ref, parity), (other_ref, 1 - parity)):
        at = pl.ds(pl.multiple_of(place * rows, 16), rows)
        own_ref[at, : 2 * rows] = ref[:rows]
        own_ref[at, 2 * rows :] = ref[rows:]


class Specs:
    def __init__(self, batches, group=1):
        self.batches = batches // group
        self.group = group
        self.ins, self.args, self.outs, self.shapes = [], [], [], []

    def per(self, a, block=None, at=None, start=0):
        block = (self.group,) + (a.shape[1:] if block is None else block)
        last = self.batches - 1

        def index(m, place):
            m = jnp.minimum(m, last)
            rest = (0,) * (len(block) - 1) if at is None else at(place)
            return (m + start,) + rest

        self.ins.append(pl.BlockSpec(block, index))
        self.args.append(a)

    def whole(self, *arrays):
        for a in arrays:
            self.ins.append(
                pl.BlockSpec(
                    a.shape, lambda m, place, n=a.ndim: (0,) * n, pipeline_mode=pl.Buffered(1)
                )
            )
            self.args.append(a)

    def after(self, *arrays):
        for a in arrays:
            self.ins.append(pl.BlockSpec(memory_space=pl.ANY))
            self.args.append(a)

    def out_part(self, batches, start, *dims, dtype=BF):
        last = self.batches - 1
        n = len(dims)
        self.outs.append(
            pl.BlockSpec(
                (1,) + dims, lambda m, place: (jnp.minimum(m, last) + start,) + (0,) * n
            )
        )
        self.shapes.append(jax.ShapeDtypeStruct((batches,) + dims, dtype))

    def out(self, *dims, dtype=BF):
        last = self.batches - 1
        n = len(dims)
        self.outs.append(
            pl.BlockSpec(
                (self.group,) + dims, lambda m, place: (jnp.minimum(m, last),) + (0,) * n
            )
        )
        self.shapes.append(jax.ShapeDtypeStruct((self.batches * self.group,) + dims, dtype))

    def out_columns(self, rows, cols, dtype=BF):
        last = self.batches - 1
        self.outs.append(pl.BlockSpec((rows, cols), lambda m, place: (0, jnp.minimum(m, last))))
        self.shapes.append(jax.ShapeDtypeStruct((rows, self.batches * cols), dtype))

    def out_any(self, *dims, dtype=BF):
        self.outs.append(pl.BlockSpec(memory_space=pl.ANY))
        self.shapes.append(jax.ShapeDtypeStruct(dims, dtype))

    def out_whole(self, *dims, dtype=BF):
        self.outs.append(
            pl.BlockSpec(
                dims, lambda m, place: (0,) * len(dims), pipeline_mode=pl.Buffered(1)
            )
        )
        self.shapes.append(jax.ShapeDtypeStruct(dims, dtype))

    def call(self, kernel, place, name, vmem, steps=None, scratch=(), flops=0, moved=0, alias=None):
        return pl.pallas_call(
            kernel,
            grid_spec=pltpu.PrefetchScalarGridSpec(
                num_scalar_prefetch=1,
                grid=(self.batches if steps is None else steps,),
                in_specs=self.ins,
                out_specs=self.outs,
                scratch_shapes=list(scratch),
            ),
            out_shape=self.shapes,
            input_output_aliases={} if alias is None else alias,
            compiler_params=pltpu.CompilerParams(vmem_limit_bytes=vmem * MIB),
            cost_estimate=pl.CostEstimate(
                flops=flops // 10, bytes_accessed=moved // 10, transcendentals=0
            ),
            name=name,
        )(place, *self.args)


def in_turn(units, first, mid, last):
    begun, middle, n = {}, {}, len(units)
    for i in range(-1, n + 1):
        if i + 1 < n:
            begun[i + 1] = first(*units[i + 1])
        if i >= 1:
            last(*units[i - 1], begun.pop(i - 1), middle.pop(i - 1))
        if 0 <= i < n:
            middle[i] = mid(*units[i], begun[i])


def places(b, p):
    here = slice(b * LANES, (b + 1) * LANES)
    return here, slice(b * LANES, b * LANES + SPAN), slice(p * LANES, (p + 1) * LANES)


def attend(q_ref, k_ref, v_ref, p_ref, ctx_ref, pos_row):
    rows, cols = q_ref.shape[1:]
    pos_col = jnp.broadcast_to(pos_row, (LANES, pos_row.shape[1])).T
    biases = []
    for b in range(rows // LANES):
        rel = (
            lax.broadcasted_iota(jnp.int32, (SPAN, LANES), 0)
            - REACH
            - lax.broadcasted_iota(jnp.int32, (SPAN, LANES), 1)
        )
        q_pos = pos_row[:, b * LANES + REACH : (b + 1) * LANES + REACH]
        since = jnp.where(rel > 0, pos_col[b * LANES : b * LANES + SPAN], q_pos)
        far = jnp.abs(rel)
        bias = jnp.where((far <= REACH) & (since >= far), 0.0, masked_score).astype(F32)
        biases.append(jnp.concatenate([bias, bias], axis=1))

    def first(b, p):
        here, span, at = places(b, p)
        return mm(k_ref[0, span, at], both_heads(q_ref[0, here, at]), 1, 1)

    def mid(b, p, scores):
        scores = scores + biases[b]
        e = jnp.exp(scores - jnp.max(scores, axis=0, keepdims=True))
        probs = (e * (1.0 / jnp.sum(e, axis=0, keepdims=True))).astype(BF)
        p_ref[0, b, p] = probs
        return probs

    def last(b, p, _, probs):
        here, span, at = places(b, p)
        ctx_ref[0, here, at] = one_row_each(mm(probs, v_ref[0, span, at], 0, 0)).astype(BF)

    units = [(b, p) for b in range(rows // LANES) for p in range(cols // LANES)]
    in_turn(units, first, mid, last)


def project(normed, w_ref, cos, sin, q_ref, k_ref, v_ref):
    rows, cols = q_ref.shape[1:]
    own = slice(REACH, REACH + rows)
    mixed_q = mm(normed[own], w_ref[0], 1, 0)
    mixed_k = mm(normed, w_ref[1], 1, 0)
    v_ref[0] = mm(normed, w_ref[2], 1, 0).astype(BF)
    for p in range(cols // LANES):
        at = slice(p * LANES, (p + 1) * LANES)
        mq, mk = mixed_q[:, at], mixed_k[:, at]
        q_ref[0, :, at] = (mq * cos[own] + turned(mq) * sin[own]).astype(BF) * SCALE
        k_ref[0, :, at] = (mk * cos + turned(mk) * sin).astype(BF)


def forward_own(
    block, place, x_ref, outer_ref, pos_ref, gain_ref, w_ref, freq_ref, wi_ref, wd_ref,
    normed_ref, at_ref, pos_out_ref, cos_ref, sin_ref, rest_ref,
    q_ref, k_ref, v_ref, p_ref, ctx_ref, x_scr, half_scr, sems,
):
    t, parity = place[0], place[1]
    more = wi_ref.shape[1] // 2
    part = pl.ds(pl.multiple_of(parity * more, 16), more)
    sources = [wi_ref.at[0, part], wi_ref.at[1, part], wd_ref.at[part]]
    held = [half_scr.at[i * more : (i + 1) * more] for i in range(3)]
    targets = [rest_ref.at[i * more : (i + 1) * more] for i in range(3)]
    reads = [pltpu.make_async_copy(a, b, sems.at[i]) for i, (a, b) in enumerate(zip(sources, held))]
    writes = [
        pltpu.make_async_copy(a, b, sems.at[3 + i]) for i, (a, b) in enumerate(zip(held, targets))
    ]
    m = pl.program_id(0)

    @pl.when(m == 0)
    def _():
        for copy in reads:
            copy.start()

    @pl.when(m == 1)
    def _():
        for copy in reads:
            copy.wait()
        for copy in writes:
            copy.start()

    @pl.when(m == pl.num_programs(0) - 1)
    def _():
        for copy in writes:
            copy.wait()

    rows, ext = q_ref.shape[1], k_ref.shape[1]
    inner = rows + REACH
    x_scr[pl.ds(pl.multiple_of((1 - t) * REACH, 16), inner), :] = x_ref[
        0, pl.ds(pl.multiple_of(t * (rows - REACH), 16), inner), :
    ]
    x_scr[pl.ds(pl.multiple_of(t * inner, 16), REACH), :] = outer_ref[0, :REACH]
    pos = pos_ref[0]
    digits = outer_ref[0, REACH:].astype(F32)[:1, : 2 * REACH]
    pos_outer = (digits[:, :REACH] * DIGIT + digits[:, REACH:]).astype(jnp.int32)
    pos_row = jnp.where(
        t == 0,
        jnp.concatenate([pos_outer, pos[:, :inner]], axis=1),
        jnp.concatenate([pos[:, rows - REACH :], pos_outer], axis=1),
    )
    pos_out_ref[0] = pos_row
    xhat, _ = norm_parts(x_scr[...].astype(F32))
    normed = (xhat * gain_ref[...]).astype(BF)
    normed_ref[0] = normed
    transpose_into(at_ref, slice(None), normed, block, parity)
    angles = freq_ref[...] * pos_row.astype(F32)
    c, s = jnp.cos(angles), jnp.sin(angles)
    cos = jnp.concatenate([c, c, c, c], axis=0).T
    sin = jnp.concatenate([-s, s, -s, s], axis=0).T
    cos_ref[0] = cos
    sin_ref[0] = sin
    project(normed, w_ref, cos, sin, q_ref, k_ref, v_ref)
    attend(q_ref, k_ref, v_ref, p_ref, ctx_ref, pos_row)


def forward_peer(
    place, normed_ref, pos_ref, cos_ref, sin_ref, mine_ref, other_ref,
    q_ref, k_ref, v_ref, p_ref, ctx_ref, w_scr,
):
    @pl.when(pl.program_id(0) == 0)
    def _():
        join(w_scr, mine_ref.at[:3], other_ref.at[:3], place[1], mine_ref.shape[1])

    project(normed_ref[0], w_scr, cos_ref[0], sin_ref[0], q_ref, k_ref, v_ref)
    attend(q_ref, k_ref, v_ref, p_ref, ctx_ref, pos_ref[0])


def attention_outs(s, rows, ext, cols):
    s.out(rows, cols)
    s.out(ext, cols)
    s.out(ext, cols)
    s.out(rows // LANES, cols // LANES, SPAN, 2 * LANES)
    s.out(rows, cols)


def split_units(units):
    return units // LANES * LANES, units % LANES


def flat(ref):
    return ref[...].reshape(-1, ref.shape[2])


def hidden_units(nf, cot, gate_w, up_w, down_w, count, here, act_s, gg_s, gu_s):
    def first(at):
        return mm(nf, gate_w[at], 1, 1), mm(nf, up_w[at], 1, 1), mm(cot, down_w[at], 1, 1)

    def mid(at, begun):
        g, u, ga = begun
        cdf = 0.5 * (1.0 + lax.erf(g * 0.5**0.5))
        gelu = g * cdf
        slope = cdf + g * jnp.exp(-0.5 * g * g) * 0.3989422804014327
        act_s[here, at] = (gelu * u).astype(BF)
        gg_s[here, at] = (ga * u * slope).astype(BF)
        gu_s[here, at] = (ga * gelu).astype(BF)

    step = 2 * LANES
    chunks = [(slice(c, min(c + step, count)),) for c in range(0, count, step)]
    in_turn(chunks, first, mid, lambda *_: None)


def ffn_own_kernel(
    block, place, x_ref, cot_ref, ctx0_ref, ctx1_ref, gain_ref, wo_ref, wi_ref, wd_ref,
    wo_mine, wo_other, state_ref, out_ref, grad_ref, keep_ref, send_ref, keep_down, send_down,
    wo, nft, cott, gg_s, gu_s, act_s,
):
    m = pl.program_id(0)
    parity = place[1]
    steps = pl.num_programs(0) - 1
    main = gg_s.shape[1]
    group, rows, width = x_ref.shape
    rows = group * rows

    @pl.when(m == 0)
    def _():
        cols = wo_ref.shape[0]
        wo[:cols] = wo_ref[...]
        join_out(wo.at[cols:], wo_mine.at[0], wo_other.at[0], parity)

    @pl.when(m < steps)
    def _():
        here = pl.ds(pl.multiple_of(m * rows, 16), rows)
        along = pl.ds(pl.multiple_of(m * rows, LANES), rows)
        ctx = jnp.concatenate([flat(ctx0_ref), flat(ctx1_ref)], axis=1)
        state = flat(x_ref).astype(F32) + mm(ctx, wo[...], 1, 0)
        state_ref[...] = state.reshape(state_ref.shape)
        nf = (norm_parts(state)[0] * gain_ref[...]).astype(BF)
        transpose_into(nft, along, nf, block, parity)
        cot = flat(cot_ref)
        transpose_into(cott, along, cot, block, parity)
        hidden_units(nf, cot, wi_ref.at[0], wi_ref.at[1], wd_ref, main, here, act_s, gg_s, gu_s)
        out = mm(act_s[here, :], wd_ref[:main], 1, 0)
        out_ref[...] = out.astype(BF).reshape(out_ref.shape)
        grad = mm(gg_s[here, :], wi_ref[0, :main], 1, 0) + mm(gu_s[here, :], wi_ref[1, :main], 1, 0)
        grad_ref[...] = grad.astype(BF).reshape(grad_ref.shape)

    @pl.when(m == steps)
    def _():
        for j, to_ref, down_ref in ((0, keep_ref, keep_down), (1, send_ref, send_down)):
            at = slice(j * width // 2, (j + 1) * width // 2)
            to_ref[:, :main] = mm(nft[at], gg_s[...], 1, 0).astype(BF)
            to_ref[:, main:] = mm(nft[at], gu_s[...], 1, 0).astype(BF)
            down_ref[...] = mm(cott[at], act_s[...], 1, 0).astype(BF)


def ffn_peer_kernel(
    block, place, state_ref, out_ref, grad_ref, cot_ref, ctx0_ref, ctx1_ref, gain_ref,
    wi_tail, wd_tail, mine_ref, other_ref, keep_down, send_down, y_ref, mix_ref, gain_out,
    keep_a, keep_b, send_a, send_b,
    half, gate_w, up_w, down_w, nft, cott, mixt, gg_s, gu_s, act_s, ctx_s,
):
    m = pl.program_id(0)
    parity = place[1]
    steps = pl.num_programs(0) - 1
    units = half.shape[0]
    main, rest = split_units(units)
    group, rows, width = state_ref.shape
    rows = group * rows

    @pl.when(m == 0)
    def _():
        for j, (full, own) in enumerate(
            ((gate_w, wi_tail.at[0]), (up_w, wi_tail.at[1]), (down_w, wd_tail))
        ):
            part = slice(j * (units // 2), (j + 1) * (units // 2))
            join(half, mine_ref.at[part], other_ref.at[part], parity, units // 2)
            full[:main] = half[:main]
            full[main : main + rest] = own[...]
            full[main + rest :] = half[main:]
        gain_out[...] = jnp.zeros_like(gain_out)

    @pl.when(m < steps)
    def _():
        here = pl.ds(pl.multiple_of(m * rows, 16), rows)
        along = pl.ds(pl.multiple_of(m * rows, LANES), rows)
        ctx_s[here, :] = jnp.concatenate([flat(ctx0_ref), flat(ctx1_ref)], axis=1)
        state = flat(state_ref)
        xhat, r = norm_parts(state)
        gain = gain_ref[...]
        nf = (xhat * gain).astype(BF)
        transpose_into(nft, along, nf, block, parity)
        cot = flat(cot_ref)
        transpose_into(cott, along, cot, block, parity)
        hidden_units(nf, cot, gate_w, up_w, down_w, main + 2 * rest, here, act_s, gg_s, gu_s)
        out = state + flat(out_ref).astype(F32) + mm(act_s[here, :], down_w[...], 1, 0)
        y_ref[...] = out.astype(BF).reshape(y_ref.shape)
        grad = flat(grad_ref).astype(F32) + mm(gg_s[here, :], gate_w[...], 1, 0)
        grad = grad + mm(gu_s[here, :], up_w[...], 1, 0)
        gain_out[...] += jnp.sum(grad * xhat, axis=0, keepdims=True)
        mix = (cot.astype(F32) + norm_back(xhat, r, grad * gain)).astype(BF)
        mix_ref[...] = mix.reshape(mix_ref.shape)
        transpose_into(mixt, along, mix, block, parity)

    @pl.when(m == steps)
    def _():
        cols = ctx0_ref.shape[2]
        zero = jnp.zeros((width // 2, rest), BF)
        for j, a_ref, b_ref, down_ref in (
            (0, keep_a, keep_b, keep_down),
            (1, send_a, send_b, send_down),
        ):
            at = slice(j * width // 2, (j + 1) * width // 2)
            ends = []
            for at_ref, hidden, to_ref in (
                (nft, gg_s, a_ref.at[:, :main]),
                (nft, gu_s, a_ref.at[:, main:]),
                (cott, act_s, b_ref.at[1, :, :main]),
            ):
                to_ref[...] = mm(at_ref[at], hidden[:, :main], 1, 0).astype(BF)
                ends.append(mm(at_ref[at], hidden[:, main:], 1, 0).astype(BF))
            b_ref[0, :, :main] = down_ref[...]
            out = mm(mixt[at], ctx_s[...], 1, 0).astype(BF)
            for i in range(2):
                part = slice(i * rest, (i + 1) * rest)
                b_ref[i, :, main : main + cols] = out[:, i * cols : (i + 1) * cols]
                b_ref[i, :, main + cols :] = jnp.concatenate(
                    [end[:, part] for end in ends] + [zero], axis=1
                )


def backward_kernel(plan, place, mix_ref, *rest):
    peer, sums, ends = plan["peer"], plan["sums"], plan["ends"]
    rest = list(rest)
    first_ref, second_ref = rest.pop(0), rest.pop(0)
    q_ref, k_ref, v_ref, p_ref, cos_ref, sin_ref = rest[:6]
    rest = rest[6:]
    before_ref = rest.pop(0) if plan["adds"] else None
    if ends:
        normed_ref = rest.pop(0)
    if sums:
        at_ref = rest.pop(0)
    gm_before = rest.pop(0) if plan["earlier"] else None
    gain_sums = None
    if plan["gains"]:
        gain_sums = rest.pop(0), rest.pop(0)
    rest = rest[plan["after"] :]
    nag_ref = rest.pop(0)
    if ends:
        inner_ref, outer_ref = rest.pop(0), rest.pop(0)
    if sums:
        keep_ref, send_ref = rest.pop(0), rest.pop(0)
    else:
        gm_out = rest.pop(0)
    gm_ref = rest.pop(0)
    if ends:
        gain_out = rest.pop(0)
    m = pl.program_id(0)
    if peer:
        wo_scr, w_scr = rest

        @pl.when(m == 0)
        def _():
            join_out(wo_scr, first_ref.at[3], second_ref.at[3], place[1])
            rows = first_ref.shape[1]
            join(w_scr, first_ref.at[:3], second_ref.at[:3], place[1], rows)

        wo_ref, w_ref = wo_scr, w_scr
    else:
        wo_ref, w_ref = first_ref, second_ref
    rows, cols = q_ref.shape[1:]
    ext = k_ref.shape[1]
    own = slice(REACH, REACH + rows)

    def one_batch():
        dctx = mm(mix_ref[0], wo_ref[...], 1, 1).astype(BF)
        cos, sin = cos_ref[0], sin_ref[0]
        gm_ref[m, :REACH, :cols] = jnp.zeros((REACH, cols), BF)
        gm_ref[m, REACH + rows :, :cols] = jnp.zeros((REACH, cols), BF)
        blocks = rows // LANES
        key_parts, value_parts = {}, {}

        def first(b, p):
            here, span, at = places(b, p)
            grad = both_heads(dctx[here, at])
            return grad, mm(v_ref[0, span, at], grad, 1, 1)

        def mid(b, p, begun):
            probs = p_ref[0, b, p].astype(F32)
            weighted = probs * begun[1]
            balance = jnp.sum(weighted, axis=0, keepdims=True)
            return (weighted - probs * balance).astype(BF)

        def over_blocks(parts, p):
            out = []
            for b in range(blocks + 1):
                piece = None
                if b < blocks:
                    piece = parts[b, p][:LANES]
                if b > 0:
                    more = parts[b - 1, p][LANES:]
                    piece = more if piece is None else piece + more
                out.append(piece)
            return jnp.concatenate(out, axis=0)

        def end(b, p, begun, grad_scores):
            here, span, at = places(b, p)
            there = slice(b * LANES + REACH, (b + 1) * LANES + REACH)
            value_parts[b, p] = mm(p_ref[0, b, p], begun[0], 1, 0)
            key_parts[b, p] = mm(grad_scores, both_heads(q_ref[0, here, at]), 1, 0)
            dq = one_row_each(mm(grad_scores, k_ref[0, span, at], 0, 0)) * SCALE
            gm_ref[m, there, at] = (dq * cos[there] - turned(dq) * sin[there]).astype(BF)
            if b == blocks - 1:
                dk = over_blocks(key_parts, p)
                gm_ref[m, :, cols + p * LANES : cols + (p + 1) * LANES] = (
                    dk * cos - turned(dk) * sin
                ).astype(BF)
                dv = over_blocks(value_parts, p).astype(BF)
                gm_ref[m, :, 2 * cols + p * LANES : 2 * cols + (p + 1) * LANES] = dv

        units = [(b, p) for p in range(cols // LANES) for b in range(blocks)]
        in_turn(units, first, mid, end)
        nag = mm(gm_ref[m, :, cols : 2 * cols], w_ref[1], 1, 1)
        nag = nag + mm(gm_ref[m, :, 2 * cols :], w_ref[2], 1, 1)
        nag_q = mm(gm_ref[m, own, :cols], w_ref[0], 1, 1)
        if before_ref is not None:
            nag = nag + before_ref[0].astype(F32)
        if not ends:
            nag_ref[0, :REACH] = nag[:REACH].astype(BF)
            nag_ref[0, own] = (nag[own] + nag_q).astype(BF)
            nag_ref[0, REACH + rows :] = nag[REACH + rows :].astype(BF)
        else:
            left = nag[:REACH].astype(BF)
            right = nag[REACH + rows :].astype(BF)
            inner_ref[0] = jnp.where(place[0] == 0, right, left)
            outer_ref[0] = jnp.where(place[0] == 0, left, right)
            nag_own = nag[own] + nag_q
            nag_ref[0] = nag_own.astype(BF)
            normed = normed_ref[0].astype(F32)
            total = (
                jnp.sum(nag[:REACH] * normed[:REACH], axis=0, keepdims=True)
                + jnp.sum(nag_own * normed[own], axis=0, keepdims=True)
                + jnp.sum(nag[REACH + rows :] * normed[REACH + rows :], axis=0, keepdims=True)
            )

            @pl.when(m == 0)
            def _():
                gain_out[...] = total

            @pl.when(m > 0)
            def _():
                gain_out[...] += total

        if not sums:
            gm_out[0] = gm_ref[m]

    if not sums:
        one_batch()
        return
    steps = pl.num_programs(0) - 1
    pl.when(m < steps)(one_batch)

    @pl.when(m == steps)
    def _():
        half = at_ref.shape[0] // 2
        two = gm_ref[...].reshape(-1, 3 * cols)
        earlier = at_ref.shape[1] - two.shape[0]
        moves = []
        for lo, hi in plan["order"]:
            for j in range(3):
                moves.append((j * cols + lo * LANES, j * cols + hi * LANES))
        for j, to in ((0, keep_ref), (1, send_ref)):
            at = slice(j * half, (j + 1) * half)
            total = mm(at_ref[at, earlier:], two, 1, 0)
            if gm_before is not None:
                one = gm_before[...].reshape(earlier, 3 * cols)
                total = total + mm(at_ref[at, :earlier], one, 1, 0)
            total = total.astype(BF)
            into = 0
            for lo, hi in moves:
                to[:half, into : into + hi - lo] = total[:, lo:hi]
                into += hi - lo
            if gain_sums is not None:
                gain_ref, ffn_ref = gain_sums
                width, wide = gain_ref.shape[1], to.shape[1]
                attn = gain_out[...] / gain_ref[...]
                zero = jnp.zeros((MORE - 2, width), F32)
                gains = jnp.concatenate([attn, ffn_ref[...], zero], axis=0).astype(BF)
                for i in range(width // wide):
                    to[half + i * MORE : half + (i + 1) * MORE] = gains[:, i * wide : (i + 1) * wide]


def last_kernel(edges, place, x_ref, nag_ref, mix_ref, gain_ref, *rest):
    out_ref = rest[-1]
    gain = gain_ref[...]
    if edges:
        inner_ref, outer_ref = rest[:2]
        use_inner = (place[0] == 0) == (pl.program_id(0) == 1)
    step = 32
    for i in range(nag_ref.shape[0]):
        for c in range(0, REACH, step):
            at = slice(c, c + step)
            xhat, r = norm_parts(x_ref[i, at].astype(F32))
            nag = nag_ref[i, at].astype(F32)
            if edges:
                nag = nag + jnp.where(use_inner, inner_ref[i, at], outer_ref[i, at]).astype(F32)
            out_ref[i, at] = mix_ref[i, at].astype(F32) + norm_back(xhat, r, nag * gain)


def swap(x, axis, bit):
    size = lax.axis_size(axis)
    return lax.ppermute(x, axis, [(i, i ^ bit) for i in range(size)])


def then(value, *earlier):
    return lax.optimization_barrier((value, *earlier))[0]


def quarter(half, axis):
    rows = half.shape[axis] // 2
    return lax.dynamic_slice_in_dim(half, (lax.axis_index("dp") % 2) * rows, rows, axis)


class Halving:
    def __init__(self, total, rows, bit, beside=None):
        self.mine = (lax.axis_index("dp") // bit) % 2
        self.g = total.astype(BF).reshape(-1, 2, rows, total.shape[-1])
        self.sent = lax.dynamic_index_in_dim(self.g, 1 - self.mine, 1, keepdims=False)
        self.beside = beside
        if beside is not None:
            self.sent = jnp.concatenate([self.sent.reshape(-1, total.shape[-1]), beside])
        self.got = swap(self.sent, "dp", bit)

    def total(self, *earlier):
        keep = lax.dynamic_index_in_dim(self.g, self.mine, 1, keepdims=False)
        got = (then(self.got, *earlier) if earlier else self.got).astype(F32)
        if self.beside is None:
            total = keep.astype(F32) + got
            return total.reshape(-1, total.shape[-1])
        keep = keep.astype(F32).reshape(-1, got.shape[-1])
        more = self.beside.shape[0]
        return keep + got[:-more], self.beside.astype(F32) + got[-more:]


def sum_from(total, rows, bit, size):
    while bit < size:
        total = Halving(total, rows, bit).total()
        bit *= 2
    return total


def sorted_halves(keep, send, block, size):
    if block is not None:
        return keep, send
    n, half, cols = keep.shape
    g = jnp.concatenate([keep, send], axis=1).reshape(n, size // 2, 2, 2 * half // size, cols)
    parity = lax.axis_index("dp") % 2
    keep = lax.dynamic_index_in_dim(g, parity, 2, keepdims=False)
    send = lax.dynamic_index_in_dim(g, 1 - parity, 2, keepdims=False)
    return keep.reshape(n, half, cols), send.reshape(n, half, cols)


def on_device(
    inputs, positions, cotangent, gain_attn, gain_ffn, w_qkv, w_out, w_in, down_projection_weight
):
    batches, row_count, width = inputs.shape
    parts, t = lax.axis_size("tensor"), lax.axis_index("tensor")
    dp = lax.axis_size("dp")
    rows = row_count // parts
    ext = rows + 2 * REACH
    cols = w_qkv.shape[2]
    units = w_in.shape[2]
    place = jnp.stack([t, lax.axis_index("dp") % 2]).astype(jnp.int32)
    mine = width // dp
    block = mine if mine % 16 == 0 else None

    qkv = w_qkv.transpose(1, 0, 2)
    w_in = w_in.transpose(1, 2, 0)
    w_down = down_projection_weight
    out_mine = quarter(w_out, 0)
    qkv_mine = jnp.concatenate(
        [
            quarter(qkv, 1),
            jnp.concatenate([out_mine[:, :cols], out_mine[:, cols:]])[None],
        ]
    )
    at = jnp.where(t == 0, row_count - REACH, 0)
    edge = lax.dynamic_slice_in_dim(positions, at, REACH, 1)
    digits = jnp.concatenate([edge // DIGIT, edge % DIGIT], axis=1).astype(BF)
    digits = jnp.pad(digits, ((0, 0), (0, width - 2 * REACH)))
    edge = jnp.concatenate(
        [
            lax.dynamic_slice_in_dim(then(inputs, qkv_mine), at, REACH, 1),
            jnp.broadcast_to(digits[:, None, :], (batches, MORE, width)),
        ],
        axis=1,
    )
    qkv_mine = swap(qkv_mine, "tensor", 1)
    perm = [(2 * i, 2 * i + 2) for i in range(dp - 1)]
    perm += [(2 * i + 3, 2 * i + 1) for i in range(dp - 1)]
    x_outer = lax.ppermute(edge, ("dp", "tensor"), perm)
    freq = jnp.asarray(
        np.power(
            np.float32(rope_base),
            -np.arange(HEAD_DIM // 2, dtype=np.float32) * np.float32(2.0 / HEAD_DIM),
        )[:, None]
    )

    work = 2 * batches * ext * width * 3 * cols + 8 * batches * rows * cols * SPAN
    s = Specs(batches)
    s.per(inputs)
    s.per(x_outer)
    s.per(positions[:, None, :])
    s.whole(gain_attn[None, :], qkv, freq)
    s.after(w_in, w_down)
    s.out(ext, width)
    s.out_columns(width, ext)
    s.out(1, ext, dtype=jnp.int32)
    s.out(ext, LANES, dtype=F32)
    s.out(ext, LANES, dtype=F32)
    s.out_any(units + units // 2, width)
    attention_outs(s, rows, ext, cols)
    normed, normed_t, pos_ext, cos, sin, rest_mine, q0, k0, v0, p0, ctx0 = s.call(
        functools.partial(forward_own, block), place, "attn_fwd_own", 60,
        scratch=[
            pltpu.VMEM((ext, width), BF),
            pltpu.VMEM((units + units // 2, width), BF),
            pltpu.SemaphoreType.DMA((6,)),
        ],
        flops=work, moved=20 * batches * ext * width,
    )

    qkv_other = swap(then(qkv_mine, ctx0), "dp", 1)
    rest_mine = swap(rest_mine, "tensor", 1)
    s = Specs(batches)
    for a in (normed, pos_ext, cos, sin):
        s.per(a)
    s.whole(qkv_mine, qkv_other)
    attention_outs(s, rows, ext, cols)
    q1, k1, v1, p1, ctx1 = s.call(
        forward_peer, place, "attn_fwd_peer", 60,
        scratch=[pltpu.VMEM((3, width, cols), BF)], flops=work, moved=20 * batches * ext * cols,
    )

    own_block = (rows, width)
    group = 2 if batches % 2 == 0 else 1
    main, rest = split_units(units)
    in_cols = 2 * main
    own_place = lambda place: (place[0], 0)
    s = Specs(batches, group)
    s.per(inputs, own_block, own_place)
    s.per(cotangent, own_block, own_place)
    s.per(ctx0)
    s.per(ctx1)
    s.whole(gain_ffn[None, :], w_out)
    s.ins.append(pl.BlockSpec((2, main, width), lambda m, place: (0, 0, 0)))
    s.ins.append(pl.BlockSpec((main, width), lambda m, place: (0, 0)))
    s.args += [w_in, w_down]
    for a in (qkv_mine, qkv_other):
        s.ins.append(pl.BlockSpec((1, cols, cols), lambda m, place: (3, 0, 0)))
        s.args.append(a)
    s.out(rows, width, dtype=F32)
    s.out(rows, width)
    s.out(rows, width)
    for cols_of in (2 * main, 2 * main, main, main):
        s.out_whole(width // 2, cols_of)
    state, part_out, part_grad, keep, send, keep_down, send_down = s.call(
        functools.partial(ffn_own_kernel, block), place, "ffn_own", 52, steps=s.batches + 1,
        scratch=[pltpu.VMEM((2 * cols, width), BF)]
        + [pltpu.VMEM((width, batches * rows), BF)] * 2
        + [pltpu.VMEM((batches * rows, main), BF)] * 3,
        flops=2 * batches * rows * width * (9 * main + 2 * cols), moved=3 * 10**7,
    )
    own_keep, send = sorted_halves(keep[None], send[None], block, dp)
    own_got = swap(send[0], "dp", 1)
    rest_other = swap(then(rest_mine, state), "dp", 1)
    s = Specs(batches, group)
    for a in (state, part_out, part_grad):
        s.per(a)
    s.per(cotangent, own_block, own_place)
    s.per(ctx0)
    s.per(ctx1)
    s.whole(gain_ffn[None, :])
    s.ins.append(pl.BlockSpec((2, rest, width), lambda m, place: (0, main // rest, 0)))
    s.ins.append(pl.BlockSpec((rest, width), lambda m, place: (main // rest, 0)))
    s.args += [w_in, w_down]
    s.whole(rest_mine, rest_other, keep_down, send_down)
    s.out(rows, width)
    s.out(rows, width)
    s.out_whole(1, width, dtype=F32)
    for _ in range(2):
        s.out_whole(width // 2, in_cols)
        s.out_whole(2, width // 2, main + cols + 4 * rest)
    y, mix, gain_ffn_part, keep_a, keep_b, send_a, send_b = s.call(
        functools.partial(ffn_peer_kernel, block), place, "ffn_peer", 52, steps=s.batches + 1,
        scratch=[pltpu.VMEM((units, width), BF)]
        + [pltpu.VMEM((main + 2 * rest, width), BF)] * 3
        + [pltpu.VMEM((width, batches * rows), BF)] * 3
        + [pltpu.VMEM((batches * rows, main + 2 * rest), BF)] * 3
        + [pltpu.VMEM((batches * rows, 2 * cols), BF)],
        flops=2 * batches * rows * width * (9 * (main + 2 * rest) + 2 * cols), moved=4 * 10**7,
    )
    keep_a, send_a = sorted_halves(keep_a[None], send_a[None], block, dp)
    keep_b, send_b = sorted_halves(keep_b, send_b, block, dp)
    got_a, got_b = swap(send_a[0], "dp", 1), swap(send_b, "dp", 1)

    def backward(name, peer, batch, pairs, nag=None, into=None, sums=False, gm=None, after=(), gains=()):
        start, stop = batch
        part, count = stop - start, pairs[1] - pairs[0]
        n, at, all_pairs = count * LANES, pairs[0] // count, cols // LANES
        ends = not peer and pairs[1] == all_pairs
        s = Specs(part)
        s.per(mix, start=start)
        if peer:
            s.whole(qkv_mine, qkv_other)
        else:
            s.ins.append(pl.BlockSpec((n, width), lambda m, place: (at, 0)))
            s.ins.append(pl.BlockSpec((3, width, n), lambda m, place: (0, 0, at)))
            s.args += [w_out, qkv]
        q, k, v, p = (q1, k1, v1, p1) if peer else (q0, k0, v0, p0)
        for a in (q, k, v):
            s.per(a, (a.shape[1], n), lambda place: (0, at), start=start)
        s.per(p, (p.shape[1], count) + p.shape[3:], lambda place: (0, at, 0, 0), start=start)
        s.per(cos, start=start)
        s.per(sin, start=start)
        if nag is not None:
            s.per(nag, start=start)
        if ends:
            s.per(normed, start=start)
        if sums:
            s.whole(normed_t)
        if gm is not None:
            s.whole(gm)
        s.whole(*gains)
        s.after(*after)
        scratch = [pltpu.VMEM((part, ext, 3 * n), BF)]
        alias = None
        if into is not None:
            s.after(into)
            alias = {len(s.args): 0}
        if ends:
            s.out(rows, width)
            s.out(REACH, width)
            s.out(REACH, width)
            scratch.append(pltpu.VMEM((1, width), F32))
        else:
            s.out_part(batches, start, ext, width)
        if sums:
            more = MORE * width // (3 * n) if gains else 0
            s.out_whole(width // 2 + more, 3 * n)
            s.out_whole(width // 2 + more, 3 * n)
        else:
            s.out(ext, 3 * n)
        if peer:
            scratch += [pltpu.VMEM((cols, width), BF), pltpu.VMEM((3, width, cols), BF)]
        plan = dict(
            peer=peer, sums=sums, ends=ends, adds=nag is not None, earlier=gm is not None,
            gains=bool(gains), after=len(after) + (into is not None),
            order=((0, all_pairs - 1), (all_pairs - 1, all_pairs)) if peer else ((0, count),),
        )
        return s.call(
            functools.partial(backward_kernel, plan), place, name, 52,
            steps=part + 1 if sums else None, scratch=scratch, alias=alias,
            flops=(2 * ext * width * 4 * n + 20 * rows * n * SPAN) * part,
            moved=30 * part * ext * n,
        )

    def halos(inner, outer):
        pairs = [(2 * i + 1, 2 * i + 2) for i in range(dp - 1)]
        pairs += [(j, i) for i, j in pairs]
        return swap(inner, "tensor", 1), lax.ppermute(outer, ("dp", "tensor"), pairs)

    pairs, part = cols // LANES, batches // 2
    nag1, gm1 = backward("attn_bwd_peer_a", True, (0, 1), (0, pairs))
    got_a, got_b, own_got = lax.optimization_barrier((got_a, got_b, own_got, gm1))[:3]
    a_peer = (keep_a[0].astype(F32) + got_a.astype(F32)).astype(BF)
    a_from_peer = swap(a_peer, "tensor", 1)
    b_sum = Halving((keep_b.astype(F32) + got_b.astype(F32)).reshape(width, -1), mine, 2)
    nag1, keep1, send1 = backward(
        "attn_bwd_peer_b", True, (1, batches), (0, pairs), into=nag1, sums=True, gm=gm1,
        after=(a_peer, b_sum.sent),
    )
    keep1, send1 = sorted_halves(keep1[None], send1[None], block, dp)
    got1 = swap(send1[0], "dp", 1)
    a_from_peer, own_got = lax.optimization_barrier((a_from_peer, own_got, send1))[:2]
    a_sum = own_keep[0].astype(F32) + own_got.astype(F32) + a_from_peer.astype(F32)
    a_sum = Halving(a_sum, mine, 2)
    b_sum = b_sum.total(send1).reshape(2, width // 4, -1)
    b_peer = b_sum[1].astype(BF)
    b_from_peer = swap(b_peer, "tensor", 1)
    got1 = then(got1, a_sum.sent, b_peer)
    peer_sum = Halving(keep1[0].astype(F32) + got1.astype(F32), mine, 2)
    first = (0, pairs - 1)
    nag0, keep2, send2 = backward(
        "attn_bwd_own_a", False, (0, batches), first, nag=nag1, sums=True,
        after=(a_sum.sent, b_peer, peer_sum.sent),
    )
    keep2, send2 = sorted_halves(keep2[None], send2[None], block, dp)
    got2 = swap(send2[0], "dp", 1)
    b_sum = b_sum[0] + then(b_from_peer, send2).astype(F32)
    f_sum = Halving(jnp.concatenate([a_sum.total(send2), b_sum], axis=1), mine, 4)
    peer_sum = peer_sum.total(send2).astype(BF)
    qkv_from_peer = swap(peer_sum, "tensor", 1)
    got2 = then(got2, f_sum.sent, peer_sum)
    own_first = Halving(keep2[0].astype(F32) + got2.astype(F32), mine, 2)
    second = (pairs - 1, pairs)
    nag, to_inner, to_outer, keep3, send3 = backward(
        "attn_bwd_own_b", False, (0, batches), second, nag=nag0, sums=True,
        after=(f_sum.sent, peer_sum, own_first.sent), gains=(gain_attn[None, :], gain_ffn_part),
    )
    beside = keep3[width // 2 :]
    keep3, sorted3 = sorted_halves(
        keep3[None, : width // 2], send3[None, : width // 2], block, dp
    )
    if block is None:
        send3 = jnp.concatenate([sorted3[0], beside])
    gains_peer = swap(beside, "tensor", 1)
    index = [2 * i + j for i in range(dp) for j in range(2)]
    gains_both = lax.ppermute(beside, ("dp", "tensor"), [(i, i ^ 3) for i in index])
    got3 = swap(send3, "dp", 1)
    from_inner = swap(to_inner, "tensor", 1)
    neighbours = [(2 * i + 1, 2 * i + 2) for i in range(dp - 1)]
    neighbours += [(j, i) for i, j in neighbours]
    from_outer = lax.ppermute(to_outer, ("dp", "tensor"), neighbours)

    columns = [LANES * (pairs - 1), LANES]
    wide = [3 * n for n in columns]
    own_first.got, qkv_from_peer, f_sum.got = lax.optimization_barrier(
        (own_first.got, qkv_from_peer, f_sum.got, send3)
    )[:3]
    from_first = qkv_from_peer[:, : wide[0]].astype(F32)
    own_first = Halving(own_first.total() + from_first, mine, 4)
    f_sum = f_sum.total().astype(BF)
    got3 = then(got3, own_first.sent, f_sum)
    got3, gains = got3[: width // 2].astype(F32), got3[width // 2 :].astype(F32)
    gains = beside.astype(F32) + gains
    gains = (gains + (gains_peer.astype(F32) + gains_both.astype(F32))).astype(BF)
    own_second = Halving(keep3[0].astype(F32) + got3, mine, 2, gains)

    def finish(edges, after, into, name):
        blocks = rows // REACH
        count, step = (2, blocks - 1) if edges else (blocks - 2, 1)
        begin = 0 if edges else 1

        def spec(arrays, first):
            return pl.BlockSpec(
                (batches, REACH, width), lambda j, place: (0, first(place) + begin + step * j, 0)
            )

        fixed = pl.BlockSpec((batches, REACH, width), lambda j, place: (0, 0, 0))
        args = [inputs, nag, mix, gain_attn[None, :]]
        specs = [
            spec(inputs, lambda place: place[0] * blocks),
            spec(nag, lambda place: 0),
            spec(mix, lambda place: 0),
            pl.BlockSpec((1, width), lambda j, place: (0, 0)),
        ]
        if edges:
            args += [from_inner, from_outer]
            specs += [fixed, fixed]
        more = [*after] if into is None else [*after, into]
        args += more
        specs += [pl.BlockSpec(memory_space=pl.ANY)] * len(more)
        return pl.pallas_call(
            functools.partial(last_kernel, edges),
            grid_spec=pltpu.PrefetchScalarGridSpec(
                num_scalar_prefetch=1,
                grid=(count,),
                in_specs=specs,
                out_specs=spec(nag, lambda place: 0),
            ),
            out_shape=jax.ShapeDtypeStruct((batches, rows, width), F32),
            input_output_aliases={} if into is None else {len(args): 0},
            compiler_params=pltpu.CompilerParams(vmem_limit_bytes=48 * MIB),
            cost_estimate=pl.CostEstimate(flops=10**8, bytes_accessed=10**6, transcendentals=0),
            name=name,
        )(place, *args)

    input_grad = finish(False, (own_second.sent,), None, "input_grad_inside")
    f_sum = Halving(then(f_sum, input_grad), mine, 8)
    own_first.got, own_second.got = lax.optimization_barrier(
        (own_first.got, own_second.got, input_grad, f_sum.sent)
    )[:2]
    total, gains = own_second.total()
    gains = gains.astype(BF)
    own_second = Halving(
        total + qkv_from_peer[:, wide[0] :].astype(F32), mine, 4, gains
    )
    own_first = Halving(then(own_first.total(), own_second.sent), mine, 8)
    total, gains = own_second.total()
    bit = 8
    while bit < dp:
        own_second = Halving(total, mine, bit, gains.astype(BF))
        last_sent = own_second.sent
        total, gains = own_second.total()
        bit *= 2
    second_sum = total
    gains = gains.reshape(-1, MORE, wide[1])[:, :2].transpose(1, 0, 2).reshape(2, width)

    input_grad = finish(True, (last_sent, own_first.sent), input_grad, "input_grad_edges")
    own_first.got, f_sum.got = lax.optimization_barrier(
        (own_first.got, f_sum.got, last_sent)
    )[:2]
    first_sum = sum_from(own_first.total(), mine, 16, dp)
    f_sum = sum_from(f_sum.total(), mine, 16, dp)
    qkv_sum = jnp.stack(
        [
            jnp.concatenate(
                [a[:, j * n : (j + 1) * n] for a, n in zip((first_sum, second_sum), columns)], axis=1
            )
            for j in range(3)
        ]
    ).transpose(1, 0, 2)

    def unit_columns(j):
        tail = 3 * main + cols + j * rest
        return jnp.concatenate(
            [f_sum[:, j * main : (j + 1) * main], f_sum[:, tail : tail + rest]], axis=1
        )

    return (
        y,
        input_grad,
        qkv_sum,
        f_sum[:, 3 * main : 3 * main + cols].T,
        jnp.stack([unit_columns(0), unit_columns(1)], axis=1),
        unit_columns(2).T,
        gains[0],
        gains[1],
    )


def solution(mesh):
    placed = (
        P(None, "dp", None),
        P(None, "dp"),
        P(None, "dp", None),
        P(),
        P(),
        P(None, None, "tensor"),
        P("tensor", None),
        P(None, None, "tensor"),
        P("tensor", None),
    )
    return jax.shard_map(
        on_device,
        mesh=mesh,
        in_specs=placed,
        out_specs=(
            P(None, ("dp", "tensor"), None),
            P(None, ("dp", "tensor"), None),
            P("dp", None, "tensor"),
            P("tensor", "dp"),
            P("dp", None, "tensor"),
            P("tensor", "dp"),
            P(),
            P(),
        ),
        check_vma=False,
    )
```

```python
import functools

import jax
import jax.numpy as jnp
import numpy as np
from jax import lax
from jax.experimental import pallas as pl
from jax.experimental.pallas import tpu as pltpu
from jax.sharding import PartitionSpec as P

HEAD_DIM = 64
WINDOW = 128
REACH = WINDOW // 2
LANES = 128
SPAN = LANES + 2 * REACH
SCALE = HEAD_DIM**-0.5
DIGIT = 64
MORE = 16

norm_eps = 1e-05
rope_base = 10000.0
masked_score = -1e30

BF = jnp.bfloat16
F32 = jnp.float32
MIB = 2**20


def mm(a, b, ca, cb):
    return lax.dot_general(a, b, (((ca,), (cb,)), ((), ())), preferred_element_type=F32)


def turned(v):
    lane = lax.broadcasted_iota(jnp.int32, v.shape, 1)
    low = (lane & 63) < 32
    return jnp.where(low, pltpu.roll(v, 96, 1), pltpu.roll(v, 32, 1))


def both_heads(v):
    lane = lax.broadcasted_iota(jnp.int32, v.shape, 1)
    zero = jnp.zeros_like(v)
    return jnp.concatenate(
        [jnp.where(lane < HEAD_DIM, v, zero), jnp.where(lane >= HEAD_DIM, v, zero)], axis=0
    )


def one_row_each(v):
    rows = v.shape[0] // 2
    lane = lax.broadcasted_iota(jnp.int32, (rows, v.shape[1]), 1)
    return jnp.where(lane < HEAD_DIM, v[:rows], v[rows:])


def norm_parts(v):
    centred = v - jnp.mean(v, axis=1, keepdims=True)
    spread = jnp.mean(centred * centred, axis=1, keepdims=True)
    r = lax.rsqrt(spread + norm_eps)
    return centred * r, r


def norm_back(xhat, r, e):
    return r * (
        e - jnp.mean(e, axis=1, keepdims=True) - xhat * jnp.mean(e * xhat, axis=1, keepdims=True)
    )


def transpose_into(at_ref, at, v, block, parity):
    vt = v.T
    width = vt.shape[0]
    if block is None:
        at_ref[:, at] = vt
        return
    for i in range(width // block):
        odd = parity if i % 2 == 0 else 1 - parity
        to = pl.multiple_of((i // 2) * block + odd * (width // 2), 16)
        at_ref[pl.ds(to, block), at] = vt[i * block : (i + 1) * block]


def join(own_ref, mine_ref, other_ref, parity, rows):
    own_ref[..., pl.ds(pl.multiple_of(parity * rows, 16), rows), :] = mine_ref[...]
    own_ref[..., pl.ds(pl.multiple_of((1 - parity) * rows, 16), rows), :] = other_ref[...]


def join_out(own_ref, mine_ref, other_ref, parity):
    rows = mine_ref.shape[0] // 2
    for ref, place in ((mine_ref, parity), (other_ref, 1 - parity)):
        at = pl.ds(pl.multiple_of(place * rows, 16), rows)
        own_ref[at, : 2 * rows] = ref[:rows]
        own_ref[at, 2 * rows :] = ref[rows:]


class Specs:
    def __init__(self, batches, group=1):
        self.batches = batches // group
        self.group = group
        self.ins, self.args, self.outs, self.shapes = [], [], [], []

    def per(self, a, block=None, at=None, start=0):
        block = (self.group,) + (a.shape[1:] if block is None else block)
        last = self.batches - 1

        def index(m, place):
            m = jnp.minimum(m, last)
            rest = (0,) * (len(block) - 1) if at is None else at(place)
            return (m + start,) + rest

        self.ins.append(pl.BlockSpec(block, index))
        self.args.append(a)

    def whole(self, *arrays):
        for a in arrays:
            self.ins.append(
                pl.BlockSpec(
                    a.shape, lambda m, place, n=a.ndim: (0,) * n, pipeline_mode=pl.Buffered(1)
                )
            )
            self.args.append(a)

    def after(self, *arrays):
        for a in arrays:
            self.ins.append(pl.BlockSpec(memory_space=pl.ANY))
            self.args.append(a)

    def out_part(self, batches, start, *dims, dtype=BF):
        last = self.batches - 1
        n = len(dims)
        self.outs.append(
            pl.BlockSpec(
                (1,) + dims, lambda m, place: (jnp.minimum(m, last) + start,) + (0,) * n
            )
        )
        self.shapes.append(jax.ShapeDtypeStruct((batches,) + dims, dtype))

    def out(self, *dims, dtype=BF):
        last = self.batches - 1
        n = len(dims)
        self.outs.append(
            pl.BlockSpec(
                (self.group,) + dims, lambda m, place: (jnp.minimum(m, last),) + (0,) * n
            )
        )
        self.shapes.append(jax.ShapeDtypeStruct((self.batches * self.group,) + dims, dtype))

    def out_columns(self, rows, cols, dtype=BF):
        last = self.batches - 1
        self.outs.append(pl.BlockSpec((rows, cols), lambda m, place: (0, jnp.minimum(m, last))))
        self.shapes.append(jax.ShapeDtypeStruct((rows, self.batches * cols), dtype))

    def out_any(self, *dims, dtype=BF):
        self.outs.append(pl.BlockSpec(memory_space=pl.ANY))
        self.shapes.append(jax.ShapeDtypeStruct(dims, dtype))

    def out_whole(self, *dims, dtype=BF):
        self.outs.append(
            pl.BlockSpec(
                dims, lambda m, place: (0,) * len(dims), pipeline_mode=pl.Buffered(1)
            )
        )
        self.shapes.append(jax.ShapeDtypeStruct(dims, dtype))

    def call(self, kernel, place, name, vmem, steps=None, scratch=(), flops=0, moved=0, alias=None):
        return pl.pallas_call(
            kernel,
            grid_spec=pltpu.PrefetchScalarGridSpec(
                num_scalar_prefetch=1,
                grid=(self.batches if steps is None else steps,),
                in_specs=self.ins,
                out_specs=self.outs,
                scratch_shapes=list(scratch),
            ),
            out_shape=self.shapes,
            input_output_aliases={} if alias is None else alias,
            compiler_params=pltpu.CompilerParams(vmem_limit_bytes=vmem * MIB),
            cost_estimate=pl.CostEstimate(
                flops=flops // 10, bytes_accessed=moved // 10, transcendentals=0
            ),
            name=name,
        )(place, *self.args)


def in_turn(units, first, mid, last):
    begun, middle, n = {}, {}, len(units)
    for i in range(-1, n + 1):
        if i + 1 < n:
            begun[i + 1] = first(*units[i + 1])
        if i >= 1:
            last(*units[i - 1], begun.pop(i - 1), middle.pop(i - 1))
        if 0 <= i < n:
            middle[i] = mid(*units[i], begun[i])


def places(b, p):
    here = slice(b * LANES, (b + 1) * LANES)
    return here, slice(b * LANES, b * LANES + SPAN), slice(p * LANES, (p + 1) * LANES)


def attend(q_ref, k_ref, v_ref, p_ref, ctx_ref, pos_row):
    rows, cols = q_ref.shape[1:]
    pos_col = jnp.broadcast_to(pos_row, (LANES, pos_row.shape[1])).T
    biases = []
    for b in range(rows // LANES):
        rel = (
            lax.broadcasted_iota(jnp.int32, (SPAN, LANES), 0)
            - REACH
            - lax.broadcasted_iota(jnp.int32, (SPAN, LANES), 1)
        )
        q_pos = pos_row[:, b * LANES + REACH : (b + 1) * LANES + REACH]
        since = jnp.where(rel > 0, pos_col[b * LANES : b * LANES + SPAN], q_pos)
        far = jnp.abs(rel)
        bias = jnp.where((far <= REACH) & (since >= far), 0.0, masked_score).astype(F32)
        biases.append(jnp.concatenate([bias, bias], axis=1))

    def first(b, p):
        here, span, at = places(b, p)
        return mm(k_ref[0, span, at], both_heads(q_ref[0, here, at]), 1, 1)

    def mid(b, p, scores):
        scores = scores + biases[b]
        e = jnp.exp(scores - jnp.max(scores, axis=0, keepdims=True))
        probs = (e * (1.0 / jnp.sum(e, axis=0, keepdims=True))).astype(BF)
        p_ref[0, b, p] = probs
        return probs

    def last(b, p, _, probs):
        here, span, at = places(b, p)
        ctx_ref[0, here, at] = one_row_each(mm(probs, v_ref[0, span, at], 0, 0)).astype(BF)

    units = [(b, p) for b in range(rows // LANES) for p in range(cols // LANES)]
    in_turn(units, first, mid, last)


def project(normed, w_ref, cos, sin, q_ref, k_ref, v_ref):
    rows, cols = q_ref.shape[1:]
    own = slice(REACH, REACH + rows)
    mixed_q = mm(normed[own], w_ref[0], 1, 0)
    mixed_k = mm(normed, w_ref[1], 1, 0)
    v_ref[0] = mm(normed, w_ref[2], 1, 0).astype(BF)
    for p in range(cols // LANES):
        at = slice(p * LANES, (p + 1) * LANES)
        mq, mk = mixed_q[:, at], mixed_k[:, at]
        q_ref[0, :, at] = (mq * cos[own] + turned(mq) * sin[own]).astype(BF) * SCALE
        k_ref[0, :, at] = (mk * cos + turned(mk) * sin).astype(BF)


def forward_own(
    block, place, x_ref, outer_ref, pos_ref, gain_ref, w_ref, freq_ref, wi_ref, wd_ref,
    normed_ref, at_ref, pos_out_ref, cos_ref, sin_ref, rest_ref,
    q_ref, k_ref, v_ref, p_ref, ctx_ref, x_scr, half_scr, sems,
):
    t, parity = place[0], place[1]
    more = wi_ref.shape[1] // 2
    part = pl.ds(pl.multiple_of(parity * more, 16), more)
    sources = [wi_ref.at[0, part], wi_ref.at[1, part], wd_ref.at[part]]
    held = [half_scr.at[i * more : (i + 1) * more] for i in range(3)]
    targets = [rest_ref.at[i * more : (i + 1) * more] for i in range(3)]
    reads = [pltpu.make_async_copy(a, b, sems.at[i]) for i, (a, b) in enumerate(zip(sources, held))]
    writes = [
        pltpu.make_async_copy(a, b, sems.at[3 + i]) for i, (a, b) in enumerate(zip(held, targets))
    ]
    m = pl.program_id(0)

    @pl.when(m == 0)
    def _():
        for copy in reads:
            copy.start()

    @pl.when(m == 1)
    def _():
        for copy in reads:
            copy.wait()
        for copy in writes:
            copy.start()

    @pl.when(m == pl.num_programs(0) - 1)
    def _():
        for copy in writes:
            copy.wait()

    rows, ext = q_ref.shape[1], k_ref.shape[1]
    inner = rows + REACH
    x_scr[pl.ds(pl.multiple_of((1 - t) * REACH, 16), inner), :] = x_ref[
        0, pl.ds(pl.multiple_of(t * (rows - REACH), 16), inner), :
    ]
    x_scr[pl.ds(pl.multiple_of(t * inner, 16), REACH), :] = outer_ref[0, :REACH]
    pos = pos_ref[0]
    digits = outer_ref[0, REACH:].astype(F32)[:1, : 2 * REACH]
    pos_outer = (digits[:, :REACH] * DIGIT + digits[:, REACH:]).astype(jnp.int32)
    pos_row = jnp.where(
        t == 0,
        jnp.concatenate([pos_outer, pos[:, :inner]], axis=1),
        jnp.concatenate([pos[:, rows - REACH :], pos_outer], axis=1),
    )
    pos_out_ref[0] = pos_row
    xhat, _ = norm_parts(x_scr[...].astype(F32))
    normed = (xhat * gain_ref[...]).astype(BF)
    normed_ref[0] = normed
    transpose_into(at_ref, slice(None), normed, block, parity)
    angles = freq_ref[...] * pos_row.astype(F32)
    c, s = jnp.cos(angles), jnp.sin(angles)
    cos = jnp.concatenate([c, c, c, c], axis=0).T
    sin = jnp.concatenate([-s, s, -s, s], axis=0).T
    cos_ref[0] = cos
    sin_ref[0] = sin
    project(normed, w_ref, cos, sin, q_ref, k_ref, v_ref)
    attend(q_ref, k_ref, v_ref, p_ref, ctx_ref, pos_row)


def forward_peer(
    place, normed_ref, pos_ref, cos_ref, sin_ref, mine_ref, other_ref,
    q_ref, k_ref, v_ref, p_ref, ctx_ref, w_scr,
):
    @pl.when(pl.program_id(0) == 0)
    def _():
        join(w_scr, mine_ref.at[:3], other_ref.at[:3], place[1], mine_ref.shape[1])

    project(normed_ref[0], w_scr, cos_ref[0], sin_ref[0], q_ref, k_ref, v_ref)
    attend(q_ref, k_ref, v_ref, p_ref, ctx_ref, pos_ref[0])


def attention_outs(s, rows, ext, cols):
    s.out(rows, cols)
    s.out(ext, cols)
    s.out(ext, cols)
    s.out(rows // LANES, cols // LANES, SPAN, 2 * LANES)
    s.out(rows, cols)


def split_units(units):
    return units // LANES * LANES, units % LANES


def flat(ref):
    return ref[...].reshape(-1, ref.shape[2])


def hidden_units(nf, cot, gate_w, up_w, down_w, count, here, act_s, gg_s, gu_s):
    def first(at):
        return mm(nf, gate_w[at], 1, 1), mm(nf, up_w[at], 1, 1), mm(cot, down_w[at], 1, 1)

    def mid(at, begun):
        g, u, ga = begun
        cdf = 0.5 * (1.0 + lax.erf(g * 0.5**0.5))
        gelu = g * cdf
        slope = cdf + g * jnp.exp(-0.5 * g * g) * 0.3989422804014327
        act_s[here, at] = (gelu * u).astype(BF)
        gg_s[here, at] = (ga * u * slope).astype(BF)
        gu_s[here, at] = (ga * gelu).astype(BF)

    step = 2 * LANES
    chunks = [(slice(c, min(c + step, count)),) for c in range(0, count, step)]
    in_turn(chunks, first, mid, lambda *_: None)


def ffn_own_kernel(
    block, place, x_ref, cot_ref, ctx0_ref, ctx1_ref, gain_ref, wo_ref, wi_ref, wd_ref,
    wo_mine, wo_other, state_ref, out_ref, grad_ref, keep_ref, send_ref, keep_down, send_down,
    wo, nft, cott, gg_s, gu_s, act_s,
):
    m = pl.program_id(0)
    parity = place[1]
    steps = pl.num_programs(0) - 1
    main = gg_s.shape[1]
    group, rows, width = x_ref.shape
    rows = group * rows

    @pl.when(m == 0)
    def _():
        cols = wo_ref.shape[0]
        wo[:cols] = wo_ref[...]
        join_out(wo.at[cols:], wo_mine.at[0], wo_other.at[0], parity)

    @pl.when(m < steps)
    def _():
        here = pl.ds(pl.multiple_of(m * rows, 16), rows)
        along = pl.ds(pl.multiple_of(m * rows, LANES), rows)
        ctx = jnp.concatenate([flat(ctx0_ref), flat(ctx1_ref)], axis=1)
        state = flat(x_ref).astype(F32) + mm(ctx, wo[...], 1, 0)
        state_ref[...] = state.reshape(state_ref.shape)
        nf = (norm_parts(state)[0] * gain_ref[...]).astype(BF)
        transpose_into(nft, along, nf, block, parity)
        cot = flat(cot_ref)
        transpose_into(cott, along, cot, block, parity)
        hidden_units(nf, cot, wi_ref.at[0], wi_ref.at[1], wd_ref, main, here, act_s, gg_s, gu_s)
        out = mm(act_s[here, :], wd_ref[:main], 1, 0)
        out_ref[...] = out.astype(BF).reshape(out_ref.shape)
        grad = mm(gg_s[here, :], wi_ref[0, :main], 1, 0) + mm(gu_s[here, :], wi_ref[1, :main], 1, 0)
        grad_ref[...] = grad.astype(BF).reshape(grad_ref.shape)

    @pl.when(m == steps)
    def _():
        for j, to_ref, down_ref in ((0, keep_ref, keep_down), (1, send_ref, send_down)):
            at = slice(j * width // 2, (j + 1) * width // 2)
            to_ref[:, :main] = mm(nft[at], gg_s[...], 1, 0).astype(BF)
            to_ref[:, main:] = mm(nft[at], gu_s[...], 1, 0).astype(BF)
            down_ref[...] = mm(cott[at], act_s[...], 1, 0).astype(BF)


def ffn_peer_kernel(
    block, place, state_ref, out_ref, grad_ref, cot_ref, ctx0_ref, ctx1_ref, gain_ref,
    wi_tail, wd_tail, mine_ref, other_ref, keep_down, send_down, y_ref, mix_ref, gain_out,
    keep_a, keep_b, send_a, send_b,
    half, gate_w, up_w, down_w, nft, cott, mixt, gg_s, gu_s, act_s, ctx_s,
):
    m = pl.program_id(0)
    parity = place[1]
    steps = pl.num_programs(0) - 1
    units = half.shape[0]
    main, rest = split_units(units)
    group, rows, width = state_ref.shape
    rows = group * rows

    @pl.when(m == 0)
    def _():
        for j, (full, own) in enumerate(
            ((gate_w, wi_tail.at[0]), (up_w, wi_tail.at[1]), (down_w, wd_tail))
        ):
            part = slice(j * (units // 2), (j + 1) * (units // 2))
            join(half, mine_ref.at[part], other_ref.at[part], parity, units // 2)
            full[:main] = half[:main]
            full[main : main + rest] = own[...]
            full[main + rest :] = half[main:]
        gain_out[...] = jnp.zeros_like(gain_out)

    @pl.when(m < steps)
    def _():
        here = pl.ds(pl.multiple_of(m * rows, 16), rows)
        along = pl.ds(pl.multiple_of(m * rows, LANES), rows)
        ctx_s[here, :] = jnp.concatenate([flat(ctx0_ref), flat(ctx1_ref)], axis=1)
        state = flat(state_ref)
        xhat, r = norm_parts(state)
        gain = gain_ref[...]
        nf = (xhat * gain).astype(BF)
        transpose_into(nft, along, nf, block, parity)
        cot = flat(cot_ref)
        transpose_into(cott, along, cot, block, parity)
        hidden_units(nf, cot, gate_w, up_w, down_w, main + 2 * rest, here, act_s, gg_s, gu_s)
        out = state + flat(out_ref).astype(F32) + mm(act_s[here, :], down_w[...], 1, 0)
        y_ref[...] = out.astype(BF).reshape(y_ref.shape)
        grad = flat(grad_ref).astype(F32) + mm(gg_s[here, :], gate_w[...], 1, 0)
        grad = grad + mm(gu_s[here, :], up_w[...], 1, 0)
        gain_out[...] += jnp.sum(grad * xhat, axis=0, keepdims=True)
        mix = (cot.astype(F32) + norm_back(xhat, r, grad * gain)).astype(BF)
        mix_ref[...] = mix.reshape(mix_ref.shape)
        transpose_into(mixt, along, mix, block, parity)

    @pl.when(m == steps)
    def _():
        cols = ctx0_ref.shape[2]
        zero = jnp.zeros((width // 2, rest), BF)
        for j, a_ref, b_ref, down_ref in (
            (0, keep_a, keep_b, keep_down),
            (1, send_a, send_b, send_down),
        ):
            at = slice(j * width // 2, (j + 1) * width // 2)
            ends = []
            for at_ref, hidden, to_ref in (
                (nft, gg_s, a_ref.at[:, :main]),
                (nft, gu_s, a_ref.at[:, main:]),
                (cott, act_s, b_ref.at[1, :, :main]),
            ):
                to_ref[...] = mm(at_ref[at], hidden[:, :main], 1, 0).astype(BF)
                ends.append(mm(at_ref[at], hidden[:, main:], 1, 0).astype(BF))
            b_ref[0, :, :main] = down_ref[...]
            out = mm(mixt[at], ctx_s[...], 1, 0).astype(BF)
            for i in range(2):
                part = slice(i * rest, (i + 1) * rest)
                b_ref[i, :, main : main + cols] = out[:, i * cols : (i + 1) * cols]
                b_ref[i, :, main + cols :] = jnp.concatenate(
                    [end[:, part] for end in ends] + [zero], axis=1
                )


def backward_kernel(plan, place, mix_ref, *rest):
    peer, sums, ends = plan["peer"], plan["sums"], plan["ends"]
    rest = list(rest)
    first_ref, second_ref = rest.pop(0), rest.pop(0)
    q_ref, k_ref, v_ref, p_ref, cos_ref, sin_ref = rest[:6]
    rest = rest[6:]
    before_ref = rest.pop(0) if plan["adds"] else None
    if ends:
        normed_ref = rest.pop(0)
    if sums:
        at_ref = rest.pop(0)
    gm_before = rest.pop(0) if plan["earlier"] else None
    gain_sums = None
    if plan["gains"]:
        gain_sums = rest.pop(0), rest.pop(0)
    rest = rest[plan["after"] :]
    nag_ref = rest.pop(0)
    if ends:
        inner_ref, outer_ref = rest.pop(0), rest.pop(0)
    if sums:
        keep_ref, send_ref = rest.pop(0), rest.pop(0)
    else:
        gm_out = rest.pop(0)
    gm_ref = rest.pop(0)
    if ends:
        gain_out = rest.pop(0)
    m = pl.program_id(0)
    if peer:
        wo_scr, w_scr = rest

        @pl.when(m == 0)
        def _():
            join_out(wo_scr, first_ref.at[3], second_ref.at[3], place[1])
            rows = first_ref.shape[1]
            join(w_scr, first_ref.at[:3], second_ref.at[:3], place[1], rows)

        wo_ref, w_ref = wo_scr, w_scr
    else:
        wo_ref, w_ref = first_ref, second_ref
    rows, cols = q_ref.shape[1:]
    ext = k_ref.shape[1]
    own = slice(REACH, REACH + rows)

    def one_batch():
        dctx = mm(mix_ref[0], wo_ref[...], 1, 1).astype(BF)
        cos, sin = cos_ref[0], sin_ref[0]
        gm_ref[m, :REACH, :cols] = jnp.zeros((REACH, cols), BF)
        gm_ref[m, REACH + rows :, :cols] = jnp.zeros((REACH, cols), BF)
        blocks = rows // LANES
        key_parts, value_parts = {}, {}

        def first(b, p):
            here, span, at = places(b, p)
            grad = both_heads(dctx[here, at])
            return grad, mm(v_ref[0, span, at], grad, 1, 1)

        def mid(b, p, begun):
            probs = p_ref[0, b, p].astype(F32)
            weighted = probs * begun[1]
            balance = jnp.sum(weighted, axis=0, keepdims=True)
            return (weighted - probs * balance).astype(BF)

        def over_blocks(parts, p):
            out = []
            for b in range(blocks + 1):
                piece = None
                if b < blocks:
                    piece = parts[b, p][:LANES]
                if b > 0:
                    more = parts[b - 1, p][LANES:]
                    piece = more if piece is None else piece + more
                out.append(piece)
            return jnp.concatenate(out, axis=0)

        def end(b, p, begun, grad_scores):
            here, span, at = places(b, p)
            there = slice(b * LANES + REACH, (b + 1) * LANES + REACH)
            value_parts[b, p] = mm(p_ref[0, b, p], begun[0], 1, 0)
            key_parts[b, p] = mm(grad_scores, both_heads(q_ref[0, here, at]), 1, 0)
            dq = one_row_each(mm(grad_scores, k_ref[0, span, at], 0, 0)) * SCALE
            gm_ref[m, there, at] = (dq * cos[there] - turned(dq) * sin[there]).astype(BF)
            if b == blocks - 1:
                dk = over_blocks(key_parts, p)
                gm_ref[m, :, cols + p * LANES : cols + (p + 1) * LANES] = (
                    dk * cos - turned(dk) * sin
                ).astype(BF)
                dv = over_blocks(value_parts, p).astype(BF)
                gm_ref[m, :, 2 * cols + p * LANES : 2 * cols + (p + 1) * LANES] = dv

        units = [(b, p) for p in range(cols // LANES) for b in range(blocks)]
        in_turn(units, first, mid, end)
        nag = mm(gm_ref[m, :, cols : 2 * cols], w_ref[1], 1, 1)
        nag = nag + mm(gm_ref[m, :, 2 * cols :], w_ref[2], 1, 1)
        nag_q = mm(gm_ref[m, own, :cols], w_ref[0], 1, 1)
        if before_ref is not None:
            nag = nag + before_ref[0].astype(F32)
        if not ends:
            nag_ref[0, :REACH] = nag[:REACH].astype(BF)
            nag_ref[0, own] = (nag[own] + nag_q).astype(BF)
            nag_ref[0, REACH + rows :] = nag[REACH + rows :].astype(BF)
        else:
            left = nag[:REACH].astype(BF)
            right = nag[REACH + rows :].astype(BF)
            inner_ref[0] = jnp.where(place[0] == 0, right, left)
            outer_ref[0] = jnp.where(place[0] == 0, left, right)
            nag_own = nag[own] + nag_q
            nag_ref[0] = nag_own.astype(BF)
            normed = normed_ref[0].astype(F32)
            total = (
                jnp.sum(nag[:REACH] * normed[:REACH], axis=0, keepdims=True)
                + jnp.sum(nag_own * normed[own], axis=0, keepdims=True)
                + jnp.sum(nag[REACH + rows :] * normed[REACH + rows :], axis=0, keepdims=True)
            )

            @pl.when(m == 0)
            def _():
                gain_out[...] = total

            @pl.when(m > 0)
            def _():
                gain_out[...] += total

        if not sums:
            gm_out[0] = gm_ref[m]

    if not sums:
        one_batch()
        return
    steps = pl.num_programs(0) - 1
    pl.when(m < steps)(one_batch)

    @pl.when(m == steps)
    def _():
        half = at_ref.shape[0] // 2
        two = gm_ref[...].reshape(-1, 3 * cols)
        earlier = at_ref.shape[1] - two.shape[0]
        moves = []
        for lo, hi in plan["order"]:
            for j in range(3):
                moves.append((j * cols + lo * LANES, j * cols + hi * LANES))
        for j, to in ((0, keep_ref), (1, send_ref)):
            at = slice(j * half, (j + 1) * half)
            total = mm(at_ref[at, earlier:], two, 1, 0)
            if gm_before is not None:
                one = gm_before[...].reshape(earlier, 3 * cols)
                total = total + mm(at_ref[at, :earlier], one, 1, 0)
            total = total.astype(BF)
            into = 0
            for lo, hi in moves:
                to[:half, into : into + hi - lo] = total[:, lo:hi]
                into += hi - lo
            if gain_sums is not None:
                gain_ref, ffn_ref = gain_sums
                width, wide = gain_ref.shape[1], to.shape[1]
                attn = gain_out[...] / gain_ref[...]
                zero = jnp.zeros((MORE - 2, width), F32)
                gains = jnp.concatenate([attn, ffn_ref[...], zero], axis=0).astype(BF)
                for i in range(width // wide):
                    to[half + i * MORE : half + (i + 1) * MORE] = gains[:, i * wide : (i + 1) * wide]


def last_kernel(edges, place, x_ref, nag_ref, mix_ref, gain_ref, *rest):
    out_ref = rest[-1]
    gain = gain_ref[...]
    if edges:
        inner_ref, outer_ref = rest[:2]
        use_inner = (place[0] == 0) == (pl.program_id(0) == 1)
    step = 32
    for i in range(nag_ref.shape[0]):
        for c in range(0, REACH, step):
            at = slice(c, c + step)
            xhat, r = norm_parts(x_ref[i, at].astype(F32))
            nag = nag_ref[i, at].astype(F32)
            if edges:
                nag = nag + jnp.where(use_inner, inner_ref[i, at], outer_ref[i, at]).astype(F32)
            out_ref[i, at] = mix_ref[i, at].astype(F32) + norm_back(xhat, r, nag * gain)


def swap(x, axis, bit):
    size = lax.axis_size(axis)
    return lax.ppermute(x, axis, [(i, i ^ bit) for i in range(size)])


def then(value, *earlier):
    return lax.optimization_barrier((value, *earlier))[0]


def quarter(half, axis):
    rows = half.shape[axis] // 2
    return lax.dynamic_slice_in_dim(half, (lax.axis_index("dp") % 2) * rows, rows, axis)


class Halving:
    def __init__(self, total, rows, bit, beside=None):
        self.mine = (lax.axis_index("dp") // bit) % 2
        self.g = total.astype(BF).reshape(-1, 2, rows, total.shape[-1])
        self.sent = lax.dynamic_index_in_dim(self.g, 1 - self.mine, 1, keepdims=False)
        self.beside = beside
        if beside is not None:
            self.sent = jnp.concatenate([self.sent.reshape(-1, total.shape[-1]), beside])
        self.got = swap(self.sent, "dp", bit)

    def total(self, *earlier):
        keep = lax.dynamic_index_in_dim(self.g, self.mine, 1, keepdims=False)
        got = (then(self.got, *earlier) if earlier else self.got).astype(F32)
        if self.beside is None:
            total = keep.astype(F32) + got
            return total.reshape(-1, total.shape[-1])
        keep = keep.astype(F32).reshape(-1, got.shape[-1])
        more = self.beside.shape[0]
        return keep + got[:-more], self.beside.astype(F32) + got[-more:]


def sum_from(total, rows, bit, size):
    while bit < size:
        total = Halving(total, rows, bit).total()
        bit *= 2
    return total


def sorted_halves(keep, send, block, size):
    if block is not None:
        return keep, send
    n, half, cols = keep.shape
    g = jnp.concatenate([keep, send], axis=1).reshape(n, size // 2, 2, 2 * half // size, cols)
    parity = lax.axis_index("dp") % 2
    keep = lax.dynamic_index_in_dim(g, parity, 2, keepdims=False)
    send = lax.dynamic_index_in_dim(g, 1 - parity, 2, keepdims=False)
    return keep.reshape(n, half, cols), send.reshape(n, half, cols)


def on_device(
    inputs, positions, cotangent, gain_attn, gain_ffn, w_qkv, w_out, w_in, down_projection_weight
):
    batches, row_count, width = inputs.shape
    parts, t = lax.axis_size("tensor"), lax.axis_index("tensor")
    dp = lax.axis_size("dp")
    rows = row_count // parts
    ext = rows + 2 * REACH
    cols = w_qkv.shape[2]
    units = w_in.shape[2]
    place = jnp.stack([t, lax.axis_index("dp") % 2]).astype(jnp.int32)
    mine = width // dp
    block = mine if mine % 16 == 0 else None

    qkv = w_qkv.transpose(1, 0, 2)
    w_in = w_in.transpose(1, 2, 0)
    w_down = down_projection_weight
    out_mine = quarter(w_out, 0)
    qkv_mine = jnp.concatenate(
        [
            quarter(qkv, 1),
            jnp.concatenate([out_mine[:, :cols], out_mine[:, cols:]])[None],
        ]
    )
    at = jnp.where(t == 0, row_count - REACH, 0)
    edge = lax.dynamic_slice_in_dim(positions, at, REACH, 1)
    digits = jnp.concatenate([edge // DIGIT, edge % DIGIT], axis=1).astype(BF)
    digits = jnp.pad(digits, ((0, 0), (0, width - 2 * REACH)))
    edge = jnp.concatenate(
        [
            lax.dynamic_slice_in_dim(then(inputs, qkv_mine), at, REACH, 1),
            jnp.broadcast_to(digits[:, None, :], (batches, MORE, width)),
        ],
        axis=1,
    )
    qkv_mine = swap(qkv_mine, "tensor", 1)
    perm = [(2 * i, 2 * i + 2) for i in range(dp - 1)]
    perm += [(2 * i + 3, 2 * i + 1) for i in range(dp - 1)]
    x_outer = lax.ppermute(edge, ("dp", "tensor"), perm)
    freq = jnp.asarray(
        np.power(
            np.float32(rope_base),
            -np.arange(HEAD_DIM // 2, dtype=np.float32) * np.float32(2.0 / HEAD_DIM),
        )[:, None]
    )

    work = 2 * batches * ext * width * 3 * cols + 8 * batches * rows * cols * SPAN
    s = Specs(batches)
    s.per(inputs)
    s.per(x_outer)
    s.per(positions[:, None, :])
    s.whole(gain_attn[None, :], qkv, freq)
    s.after(w_in, w_down)
    s.out(ext, width)
    s.out_columns(width, ext)
    s.out(1, ext, dtype=jnp.int32)
    s.out(ext, LANES, dtype=F32)
    s.out(ext, LANES, dtype=F32)
    s.out_any(units + units // 2, width)
    attention_outs(s, rows, ext, cols)
    normed, normed_t, pos_ext, cos, sin, rest_mine, q0, k0, v0, p0, ctx0 = s.call(
        functools.partial(forward_own, block), place, "attn_fwd_own", 60,
        scratch=[
            pltpu.VMEM((ext, width), BF),
            pltpu.VMEM((units + units // 2, width), BF),
            pltpu.SemaphoreType.DMA((6,)),
        ],
        flops=work, moved=20 * batches * ext * width,
    )

    qkv_other = swap(then(qkv_mine, ctx0), "dp", 1)
    rest_mine = swap(rest_mine, "tensor", 1)
    s = Specs(batches)
    for a in (normed, pos_ext, cos, sin):
        s.per(a)
    s.whole(qkv_mine, qkv_other)
    attention_outs(s, rows, ext, cols)
    q1, k1, v1, p1, ctx1 = s.call(
        forward_peer, place, "attn_fwd_peer", 60,
        scratch=[pltpu.VMEM((3, width, cols), BF)], flops=work, moved=20 * batches * ext * cols,
    )

    own_block = (rows, width)
    group = 2 if batches % 2 == 0 else 1
    main, rest = split_units(units)
    in_cols = 2 * main
    own_place = lambda place: (place[0], 0)
    s = Specs(batches, group)
    s.per(inputs, own_block, own_place)
    s.per(cotangent, own_block, own_place)
    s.per(ctx0)
    s.per(ctx1)
    s.whole(gain_ffn[None, :], w_out)
    s.ins.append(pl.BlockSpec((2, main, width), lambda m, place: (0, 0, 0)))
    s.ins.append(pl.BlockSpec((main, width), lambda m, place: (0, 0)))
    s.args += [w_in, w_down]
    for a in (qkv_mine, qkv_other):
        s.ins.append(pl.BlockSpec((1, cols, cols), lambda m, place: (3, 0, 0)))
        s.args.append(a)
    s.out(rows, width, dtype=F32)
    s.out(rows, width)
    s.out(rows, width)
    for cols_of in (2 * main, 2 * main, main, main):
        s.out_whole(width // 2, cols_of)
    state, part_out, part_grad, keep, send, keep_down, send_down = s.call(
        functools.partial(ffn_own_kernel, block), place, "ffn_own", 52, steps=s.batches + 1,
        scratch=[pltpu.VMEM((2 * cols, width), BF)]
        + [pltpu.VMEM((width, batches * rows), BF)] * 2
        + [pltpu.VMEM((batches * rows, main), BF)] * 3,
        flops=2 * batches * rows * width * (9 * main + 2 * cols), moved=3 * 10**7,
    )
    own_keep, send = sorted_halves(keep[None], send[None], block, dp)
    own_got = swap(send[0], "dp", 1)
    rest_other = swap(then(rest_mine, state), "dp", 1)
    s = Specs(batches, group)
    for a in (state, part_out, part_grad):
        s.per(a)
    s.per(cotangent, own_block, own_place)
    s.per(ctx0)
    s.per(ctx1)
    s.whole(gain_ffn[None, :])
    s.ins.append(pl.BlockSpec((2, rest, width), lambda m, place: (0, main // rest, 0)))
    s.ins.append(pl.BlockSpec((rest, width), lambda m, place: (main // rest, 0)))
    s.args += [w_in, w_down]
    s.whole(rest_mine, rest_other, keep_down, send_down)
    s.out(rows, width)
    s.out(rows, width)
    s.out_whole(1, width, dtype=F32)
    for _ in range(2):
        s.out_whole(width // 2, in_cols)
        s.out_whole(2, width // 2, main + cols + 4 * rest)
    y, mix, gain_ffn_part, keep_a, keep_b, send_a, send_b = s.call(
        functools.partial(ffn_peer_kernel, block), place, "ffn_peer", 52, steps=s.batches + 1,
        scratch=[pltpu.VMEM((units, width), BF)]
        + [pltpu.VMEM((main + 2 * rest, width), BF)] * 3
        + [pltpu.VMEM((width, batches * rows), BF)] * 3
        + [pltpu.VMEM((batches * rows, main + 2 * rest), BF)] * 3
        + [pltpu.VMEM((batches * rows, 2 * cols), BF)],
        flops=2 * batches * rows * width * (9 * (main + 2 * rest) + 2 * cols), moved=4 * 10**7,
    )
    keep_a, send_a = sorted_halves(keep_a[None], send_a[None], block, dp)
    keep_b, send_b = sorted_halves(keep_b, send_b, block, dp)
    got_a, got_b = swap(send_a[0], "dp", 1), swap(send_b, "dp", 1)

    def backward(name, peer, batch, pairs, nag=None, into=None, sums=False, gm=None, after=(), gains=()):
        start, stop = batch
        part, count = stop - start, pairs[1] - pairs[0]
        n, at, all_pairs = count * LANES, pairs[0] // count, cols // LANES
        ends = not peer and pairs[1] == all_pairs
        s = Specs(part)
        s.per(mix, start=start)
        if peer:
            s.whole(qkv_mine, qkv_other)
        else:
            s.ins.append(pl.BlockSpec((n, width), lambda m, place: (at, 0)))
            s.ins.append(pl.BlockSpec((3, width, n), lambda m, place: (0, 0, at)))
            s.args += [w_out, qkv]
        q, k, v, p = (q1, k1, v1, p1) if peer else (q0, k0, v0, p0)
        for a in (q, k, v):
            s.per(a, (a.shape[1], n), lambda place: (0, at), start=start)
        s.per(p, (p.shape[1], count) + p.shape[3:], lambda place: (0, at, 0, 0), start=start)
        s.per(cos, start=start)
        s.per(sin, start=start)
        if nag is not None:
            s.per(nag, start=start)
        if ends:
            s.per(normed, start=start)
        if sums:
            s.whole(normed_t)
        if gm is not None:
            s.whole(gm)
        s.whole(*gains)
        s.after(*after)
        scratch = [pltpu.VMEM((part, ext, 3 * n), BF)]
        alias = None
        if into is not None:
            s.after(into)
            alias = {len(s.args): 0}
        if ends:
            s.out(rows, width)
            s.out(REACH, width)
            s.out(REACH, width)
            scratch.append(pltpu.VMEM((1, width), F32))
        else:
            s.out_part(batches, start, ext, width)
        if sums:
            more = MORE * width // (3 * n) if gains else 0
            s.out_whole(width // 2 + more, 3 * n)
            s.out_whole(width // 2 + more, 3 * n)
        else:
            s.out(ext, 3 * n)
        if peer:
            scratch += [pltpu.VMEM((cols, width), BF), pltpu.VMEM((3, width, cols), BF)]
        plan = dict(
            peer=peer, sums=sums, ends=ends, adds=nag is not None, earlier=gm is not None,
            gains=bool(gains), after=len(after) + (into is not None),
            order=((0, all_pairs - 1), (all_pairs - 1, all_pairs)) if peer else ((0, count),),
        )
        return s.call(
            functools.partial(backward_kernel, plan), place, name, 52,
            steps=part + 1 if sums else None, scratch=scratch, alias=alias,
            flops=(2 * ext * width * 4 * n + 20 * rows * n * SPAN) * part,
            moved=30 * part * ext * n,
        )

    def halos(inner, outer):
        pairs = [(2 * i + 1, 2 * i + 2) for i in range(dp - 1)]
        pairs += [(j, i) for i, j in pairs]
        return swap(inner, "tensor", 1), lax.ppermute(outer, ("dp", "tensor"), pairs)

    pairs, part = cols // LANES, batches // 2
    nag1, gm1 = backward("attn_bwd_peer_a", True, (0, 1), (0, pairs))
    got_a, got_b, own_got = lax.optimization_barrier((got_a, got_b, own_got, gm1))[:3]
    a_peer = (keep_a[0].astype(F32) + got_a.astype(F32)).astype(BF)
    a_from_peer = swap(a_peer, "tensor", 1)
    b_sum = Halving((keep_b.astype(F32) + got_b.astype(F32)).reshape(width, -1), mine, 2)
    nag1, keep1, send1 = backward(
        "attn_bwd_peer_b", True, (1, batches), (0, pairs), into=nag1, sums=True, gm=gm1,
        after=(a_peer, b_sum.sent),
    )
    keep1, send1 = sorted_halves(keep1[None], send1[None], block, dp)
    got1 = swap(send1[0], "dp", 1)
    a_from_peer, own_got = lax.optimization_barrier((a_from_peer, own_got, send1))[:2]
    a_sum = own_keep[0].astype(F32) + own_got.astype(F32) + a_from_peer.astype(F32)
    a_sum = Halving(a_sum, mine, 2)
    b_sum = b_sum.total(send1).reshape(2, width // 4, -1)
    b_peer = b_sum[1].astype(BF)
    b_from_peer = swap(b_peer, "tensor", 1)
    got1 = then(got1, a_sum.sent, b_peer)
    peer_sum = Halving(keep1[0].astype(F32) + got1.astype(F32), mine, 2)
    first = (0, pairs - 1)
    nag0, keep2, send2 = backward(
        "attn_bwd_own_a", False, (0, batches), first, nag=nag1, sums=True,
        after=(a_sum.sent, b_peer, peer_sum.sent),
    )
    keep2, send2 = sorted_halves(keep2[None], send2[None], block, dp)
    got2 = swap(send2[0], "dp", 1)
    b_sum = b_sum[0] + then(b_from_peer, send2).astype(F32)
    f_sum = Halving(jnp.concatenate([a_sum.total(send2), b_sum], axis=1), mine, 4)
    peer_sum = peer_sum.total(send2).astype(BF)
    qkv_from_peer = swap(peer_sum, "tensor", 1)
    got2 = then(got2, f_sum.sent, peer_sum)
    own_first = Halving(keep2[0].astype(F32) + got2.astype(F32), mine, 2)
    second = (pairs - 1, pairs)
    nag, to_inner, to_outer, keep3, send3 = backward(
        "attn_bwd_own_b", False, (0, batches), second, nag=nag0, sums=True,
        after=(f_sum.sent, peer_sum, own_first.sent), gains=(gain_attn[None, :], gain_ffn_part),
    )
    beside = keep3[width // 2 :]
    keep3, sorted3 = sorted_halves(
        keep3[None, : width // 2], send3[None, : width // 2], block, dp
    )
    if block is None:
        send3 = jnp.concatenate([sorted3[0], beside])
    gains_peer = swap(beside, "tensor", 1)
    index = [2 * i + j for i in range(dp) for j in range(2)]
    gains_both = lax.ppermute(beside, ("dp", "tensor"), [(i, i ^ 3) for i in index])
    got3 = swap(send3, "dp", 1)
    from_inner = swap(to_inner, "tensor", 1)
    neighbours = [(2 * i + 1, 2 * i + 2) for i in range(dp - 1)]
    neighbours += [(j, i) for i, j in neighbours]
    from_outer = lax.ppermute(to_outer, ("dp", "tensor"), neighbours)

    columns = [LANES * (pairs - 1), LANES]
    wide = [3 * n for n in columns]
    own_first.got, qkv_from_peer, f_sum.got = lax.optimization_barrier(
        (own_first.got, qkv_from_peer, f_sum.got, send3)
    )[:3]
    from_first = qkv_from_peer[:, : wide[0]].astype(F32)
    own_first = Halving(own_first.total() + from_first, mine, 4)
    f_sum = f_sum.total().astype(BF)
    got3 = then(got3, own_first.sent, f_sum)
    got3, gains = got3[: width // 2].astype(F32), got3[width // 2 :].astype(F32)
    gains = beside.astype(F32) + gains
    gains = (gains + (gains_peer.astype(F32) + gains_both.astype(F32))).astype(BF)
    own_second = Halving(keep3[0].astype(F32) + got3, mine, 2, gains)

    def finish(edges, after, into, name):
        blocks = rows // REACH
        count, step = (2, blocks - 1) if edges else (blocks - 2, 1)
        begin = 0 if edges else 1

        def spec(arrays, first):
            return pl.BlockSpec(
                (batches, REACH, width), lambda j, place: (0, first(place) + begin + step * j, 0)
            )

        fixed = pl.BlockSpec((batches, REACH, width), lambda j, place: (0, 0, 0))
        args = [inputs, nag, mix, gain_attn[None, :]]
        specs = [
            spec(inputs, lambda place: place[0] * blocks),
            spec(nag, lambda place: 0),
            spec(mix, lambda place: 0),
            pl.BlockSpec((1, width), lambda j, place: (0, 0)),
        ]
        if edges:
            args += [from_inner, from_outer]
            specs += [fixed, fixed]
        more = [*after] if into is None else [*after, into]
        args += more
        specs += [pl.BlockSpec(memory_space=pl.ANY)] * len(more)
        return pl.pallas_call(
            functools.partial(last_kernel, edges),
            grid_spec=pltpu.PrefetchScalarGridSpec(
                num_scalar_prefetch=1,
                grid=(count,),
                in_specs=specs,
                out_specs=spec(nag, lambda place: 0),
            ),
            out_shape=jax.ShapeDtypeStruct((batches, rows, width), F32),
            input_output_aliases={} if into is None else {len(args): 0},
            compiler_params=pltpu.CompilerParams(vmem_limit_bytes=48 * MIB),
            cost_estimate=pl.CostEstimate(flops=10**8, bytes_accessed=10**6, transcendentals=0),
            name=name,
        )(place, *args)

    input_grad = finish(False, (own_second.sent,), None, "input_grad_inside")
    f_sum = Halving(then(f_sum, input_grad), mine, 8)
    own_first.got, own_second.got = lax.optimization_barrier(
        (own_first.got, own_second.got, input_grad, f_sum.sent)
    )[:2]
    total, gains = own_second.total()
    gains = gains.astype(BF)
    own_second = Halving(
        total + qkv_from_peer[:, wide[0] :].astype(F32), mine, 4, gains
    )
    first_sum = own_first.total().astype(BF)
    total, gains = own_second.total()
    bit = 8
    while bit < dp:
        own_second = Halving(total, mine, bit, gains.astype(BF))
        last_sent = own_second.sent
        total, gains = own_second.total()
        bit *= 2
    second_sum = total
    gains = gains.reshape(-1, MORE, wide[1])[:, :2].transpose(1, 0, 2).reshape(2, width)

    own_first = Halving(then(first_sum, last_sent), mine, 8)
    input_grad = finish(True, (last_sent, own_first.sent), input_grad, "input_grad_edges")
    own_first.got, f_sum.got = lax.optimization_barrier(
        (own_first.got, f_sum.got, last_sent)
    )[:2]
    first_sum = sum_from(own_first.total(), mine, 16, dp)
    f_sum = sum_from(f_sum.total(), mine, 16, dp)
    qkv_sum = jnp.stack(
        [
            jnp.concatenate(
                [a[:, j * n : (j + 1) * n] for a, n in zip((first_sum, second_sum), columns)], axis=1
            )
            for j in range(3)
        ]
    ).transpose(1, 0, 2)

    def unit_columns(j):
        tail = 3 * main + cols + j * rest
        return jnp.concatenate(
            [f_sum[:, j * main : (j + 1) * main], f_sum[:, tail : tail + rest]], axis=1
        )

    return (
        y,
        input_grad,
        qkv_sum,
        f_sum[:, 3 * main : 3 * main + cols].T,
        jnp.stack([unit_columns(0), unit_columns(1)], axis=1),
        unit_columns(2).T,
        gains[0],
        gains[1],
    )


def solution(mesh):
    placed = (
        P(None, "dp", None),
        P(None, "dp"),
        P(None, "dp", None),
        P(),
        P(),
        P(None, None, "tensor"),
        P("tensor", None),
        P(None, None, "tensor"),
        P("tensor", None),
    )
    return jax.shard_map(
        on_device,
        mesh=mesh,
        in_specs=placed,
        out_specs=(
            P(None, ("dp", "tensor"), None),
            P(None, ("dp", "tensor"), None),
            P("dp", None, "tensor"),
            P("tensor", "dp"),
            P("dp", None, "tensor"),
            P("tensor", "dp"),
            P(),
            P(),
        ),
        check_vma=False,
    )
```
